32 devices in a mesh: section: 2 (over core), seq: 4 (over y, x), dp: 4 (over z).
Axes of the slice: x: 2, y: 2, z: 4, core: 2. Of those that a mesh axis runs over, the one named last changes fastest.
Arguments:
- layer_in: bfloat16 [2, 4, 1024, 768], P(None, 'dp', 'seq'), may hold values from -6 to 6
- cotangent: bfloat16 [2, 4, 152, 768], P(None, 'dp', 'seq'), may hold values from -6 to 6
- masked_rows: int32 [2, 4, 152], P(None, 'dp', 'seq'), may hold values from 0 to 1023, as said below
- global_positions: int32 [2, 4, 64], P(None, 'dp'), may hold values from 0 to 1023, as said below
- local_weight: bfloat16 [2, 768, 2304], P('section'), may hold values from -0.3125 to 0.3125
- local_bias: bfloat16 [2, 2, 768], P('section'), may hold values from -3 to 3
- global_weight: bfloat16 [2, 768, 2304], P('section'), may hold values from -0.3125 to 0.3125
- global_bias: bfloat16 [2, 2, 768], P('section'), may hold values from -3 to 3
- out_weight: bfloat16 [2, 768, 768], P('section'), may hold values from -1.75 to 1.75
- out_bias: bfloat16 [2, 768], P('section'), may hold values from -2 to 2
- norm_gain: bfloat16 [2, 2, 768], P('section'), may hold values from 0.5 to 1.5
- norm_shift: bfloat16 [2, 2, 768], P('section'), may hold values from -2 to 2
- up_weight: bfloat16 [2, 768, 3072], P('section'), may hold values from -0.21875 to 0.21875
- up_bias: bfloat16 [2, 3072], P('section'), may hold values from -3 to 3
- down_weight: bfloat16 [2, 3072, 768], P('section'), may hold values from -0.109375 to 0.109375
- down_bias: bfloat16 [2, 768], P('section'), may hold values from -2 to 2
Outputs:
- layer_outputs: bfloat16 [2, 2, 4, 1024, 768], P('section', None, 'dp', 'seq')
- input_grads: bfloat16 [2, 2, 4, 1024, 768], P('section', None, 'dp', 'seq')
- grad_local_weight: float32 [2, 768, 2304], P('section', ('seq', 'dp'))
- grad_local_bias: float32 [2, 2, 768], P('section')
- grad_global_weight: float32 [2, 768, 2304], P('section', ('seq', 'dp'))
- grad_global_bias: float32 [2, 2, 768], P('section')
- grad_out_weight: float32 [2, 768, 768], P('section', ('seq', 'dp'))
- grad_out_bias: float32 [2, 768], P('section', ('seq', 'dp'))
- grad_norm_gain: float32 [2, 2, 768], P('section')
- grad_norm_shift: float32 [2, 2, 768], P('section')
- grad_up_weight: float32 [2, 768, 3072], P('section', ('seq', 'dp'))
- grad_up_bias: float32 [2, 3072], P('section', ('seq', 'dp'))
- grad_down_weight: float32 [2, 3072, 768], P('section', ('seq', 'dp'))
- grad_down_bias: float32 [2, 768], P('section', ('seq', 'dp'))
The draws below stay inside these ranges and needn't reach their ends.
Inputs may be any that keep to these rules, and one draw needn't show every extreme that they name: `global_positions`: in each document the 64 positions increase, the first is 0, the last is 1023, and number k lies in [k * 16, (k + 1) * 16). `masked_rows`: in each document, block k of 38 entries holds distinct positions of [k * 256, (k + 1) * 256); positions 0 and 1023 are always masked.
All inputs are finite; a program needn't handle non-finite values.
Results may differ from the reference program's by a relative error of at most 0.035.
Values may be sent and summed in bfloat16 or wider, within the bound.
No kernel may reach another device: no remote copies, remote signals or barrier semaphores. Data moves between devices by JAX's collectives and lax.ppermute only.
A program may use at most 320 MiB of HBM per device.

```python
import math
import jax
import jax.numpy as jnp
from jax import lax

D = 768
HEADS = 12
HEAD = 64
FF = 3072
HALF = 256
GLOB = 64
MICRO = 2
MASK_DEV = 38
ROWS_DEV = 256
LAYERS = 2
DOCS = 4
LEN = 1024
NMASK = 152


def draw_global_positions(key, part):
    key = jax.random.fold_in(key, 11)
    cell_size = LEN // GLOB
    offsets = jax.random.randint(key, (MICRO, DOCS, GLOB), 0, cell_size).astype(jnp.int32)
    offsets = offsets.at[:, :, 0].set(0)
    offsets = offsets.at[:, :, GLOB - 1].set(cell_size - 1)
    starts = (jnp.arange(GLOB) * cell_size).astype(jnp.int32)
    return (starts[None, None, :] + offsets).astype(jnp.int32)


def draw_masked_rows(key, part):
    key = jax.random.fold_in(key, 23)
    block_count = LEN // ROWS_DEV
    scores = jax.random.randint(key, (MICRO, DOCS, block_count, ROWS_DEV), 0, 32768).astype(jnp.int32)
    scores = scores * ROWS_DEV + jnp.arange(ROWS_DEV).astype(jnp.int32)
    scores = scores.at[:, :, 0, 0].set(-1)
    scores = scores.at[:, :, block_count - 1, ROWS_DEV - 1].set(-1)
    chosen = jnp.argsort(scores, axis=-1)[..., :MASK_DEV].astype(jnp.int32)
    offsets = (jnp.arange(block_count) * ROWS_DEV).astype(jnp.int32)
    return (chosen + offsets[:, None]).reshape(MICRO, DOCS, NMASK).astype(jnp.int32)


def block_scale(stream_key, shape, cuts, least, top_value):
    factor_of, own = 1.0, jax.random.fold_in(stream_key, 6)
    for dim, shards_of in cuts:
        draws = jnp.exp(jax.random.uniform(jax.random.fold_in(own, dim), (shards_of,), jnp.float32, least / len(cuts), top_value / len(cuts)))
        factor_of = factor_of * jnp.repeat(draws, shape[dim] // shards_of).reshape([-1 if axis == dim else 1 for axis in range(len(shape))])
    return factor_of


def normal_values(stream_key, dims, width, limit, cuts=(), held_as=jnp.bfloat16):
    values = jax.random.normal(stream_key, dims, jnp.float32) * width
    if len(cuts) > 0:
        values = block_scale(stream_key, dims, cuts, -0.22, 0.18) * values
    return jnp.clip(values, min=-limit, max=limit).astype(held_as)


def setup_inputs(seed: int = 0) -> dict:
    arg_keys = jax.random.split(jax.random.key(seed), 17)
    return {
        "layer_in": normal_values(arg_keys[0], (MICRO, DOCS, LEN, D), 1.0, 6.0, ((1, 4), (2, 4))),
        "cotangent": normal_values(arg_keys[1], (MICRO, DOCS, NMASK, D), 1.0, 6.0, ((1, 4), (2, 4))),
        "masked_rows": draw_masked_rows(jax.random.fold_in(arg_keys[16], 71), 0),
        "global_positions": draw_global_positions(jax.random.fold_in(arg_keys[16], 71), 0),
        "local_weight": normal_values(arg_keys[4], (LAYERS, D, 3 * D), (D // 2) ** -0.5, 0.3125, ((0, 2),)),
        "local_bias": normal_values(arg_keys[5], (LAYERS, 2, D), 0.5, 3.0, ((0, 2),)),
        "global_weight": normal_values(arg_keys[6], (LAYERS, D, 3 * D), (D // 2) ** -0.5, 0.3125, ((0, 2),)),
        "global_bias": normal_values(arg_keys[7], (LAYERS, 2, D), 0.5, 3.0, ((0, 2),)),
        "out_weight": normal_values(arg_keys[8], (LAYERS, D, D), (D // 64) ** -0.5, 1.75, ((0, 2),)),
        "out_bias": normal_values(arg_keys[9], (LAYERS, D), 0.3, 2.0, ((0, 2),)),
        "norm_gain": jnp.clip(1.0 + 0.1 * jax.random.normal(arg_keys[10], (LAYERS, 2, D), jnp.float32), 0.5, 1.5).astype(jnp.bfloat16),
        "norm_shift": normal_values(arg_keys[11], (LAYERS, 2, D), 0.3, 2.0, ((0, 2),)),
        "up_weight": normal_values(arg_keys[12], (LAYERS, D, FF), D ** -0.5, 0.21875, ((0, 2),)),
        "up_bias": normal_values(arg_keys[13], (LAYERS, FF), 0.5, 3.0, ((0, 2),)),
        "down_weight": normal_values(arg_keys[14], (LAYERS, FF, D), FF ** -0.5, 0.109375, ((0, 2),)),
        "down_bias": normal_values(arg_keys[15], (LAYERS, D), 0.3, 2.0, ((0, 2),)),
    }


highest = lax.Precision.HIGHEST
far_below = -1e+30
norm_eps = 1e-05

@jax.custom_vjp
def low(v):
    return lax.optimization_barrier(v.astype(jnp.bfloat16)).astype(jnp.float32)

@jax.custom_vjp
def low_back(v):
    return v

def low_keep(v):
    return (low(v), None)

def low_pass(kept, grad):
    return (grad,)

def back_keep(v):
    return (v, None)

def back_low(kept, grad):
    return (low(grad),)
low.defvjp(low_keep, low_pass)
low_back.defvjp(back_keep, back_low)

def low_both(values):
    return low_back(low(values))

def band_mask(first_row, row_count, reach_rows, length, positions, dilated):
    rows_at = first_row + jnp.arange(row_count)
    cols_at = first_row - reach_rows + jnp.arange(row_count + 2 * reach_rows)
    offset = cols_at[None, :] - rows_at[:, None]
    inside = (jnp.abs(offset) <= reach_rows) & (cols_at >= 0)[None, :] & (cols_at < length)[None, :]
    plain_key = jnp.logical_not(jnp.any(cols_at[:, None] == positions[None, :], axis=1))
    usable = inside & plain_key[None, :]
    even_gap = offset % 2 == 0
    return usable[None, :, :] & (jnp.logical_not(dilated)[:, None, None] | even_gap[None, :, :])

def layer_norm(values, gain_row, shift_row):
    center = values - lax.optimization_barrier(jnp.mean(values, axis=-1, keepdims=True))
    scaled = lax.rsqrt(lax.optimization_barrier(jnp.mean(center * center, axis=-1, keepdims=True)) + norm_eps)
    return center * scaled * gain_row + shift_row

def attend_band(queries, keys_all, values_all, extra_keys, extra_values, positions, dilated, score_scale):
    block_rows = math.gcd(LEN, 512)
    pad_keys = jnp.pad(keys_all, ((HALF, HALF), (0, 0), (0, 0)))
    pad_values = jnp.pad(values_all, ((HALF, HALF), (0, 0), (0, 0)))

    def one_block(begin):
        block_q = lax.dynamic_slice_in_dim(queries, begin, block_rows, 0)
        block_k = lax.dynamic_slice_in_dim(pad_keys, begin, block_rows + 2 * HALF, 0)
        block_v = lax.dynamic_slice_in_dim(pad_values, begin, block_rows + 2 * HALF, 0)
        allowed = band_mask(begin, block_rows, HALF, LEN, positions, dilated)
        band_score = low_back(jnp.einsum('qhd,khd->hqk', block_q, block_k, precision=highest) * score_scale)
        toward = low_back(jnp.einsum('qhd,ghd->hqg', block_q, extra_keys, precision=highest) * score_scale)
        band_score = jnp.where(allowed, band_score, far_below)
        peak_score = jnp.maximum(lax.optimization_barrier(jnp.max(band_score, axis=-1)), lax.optimization_barrier(jnp.max(toward, axis=-1)))[..., None]
        band_exp = jnp.exp(band_score - peak_score)
        toward_exp = jnp.exp(toward - peak_score)
        totals = lax.optimization_barrier(jnp.sum(band_exp, axis=-1, keepdims=True)) + lax.optimization_barrier(jnp.sum(toward_exp, axis=-1, keepdims=True))
        first_part = jnp.einsum('hqk,khd->qhd', low(band_exp / totals), block_v, precision=highest)
        second_part = jnp.einsum('hqg,ghd->qhd', low(toward_exp / totals), extra_values, precision=highest)
        return first_part + second_part
    begins = (jnp.arange(LEN // block_rows) * block_rows).astype(jnp.int32)
    return lax.map(jax.checkpoint(one_block), begins)

def layer(source, positions, weights, upper):
    local_w, local_b, glob_w, glob_b, out_w, out_b, gains, shifts, up_w, up_b, down_w, down_b = weights
    score_scale = HEAD ** (-0.5)
    if upper:
        dilated = jnp.arange(HEADS) >= HEADS - 2
    else:
        dilated = jnp.zeros((HEADS,), dtype=bool)
    proj = jnp.dot(source, local_w, precision=highest)
    queries = low_both(proj[:, :D] + local_b[0]).reshape(LEN, HEADS, HEAD)
    keys_all = low_both(proj[:, D:2 * D]).reshape(LEN, HEADS, HEAD)
    values_all = low_both(proj[:, 2 * D:] + local_b[1]).reshape(LEN, HEADS, HEAD)
    gproj = jnp.dot(source, glob_w, precision=highest)
    gqueries = low_both(gproj[:, :D] + glob_b[0]).reshape(LEN, HEADS, HEAD)
    gkeys = low_both(gproj[:, D:2 * D]).reshape(LEN, HEADS, HEAD)
    gvalues = low_both(gproj[:, 2 * D:] + glob_b[1]).reshape(LEN, HEADS, HEAD)
    local_ctx = attend_band(queries, keys_all, values_all, keys_all[positions], values_all[positions], positions, dilated, score_scale).reshape(LEN, D)
    spread = low_back(jnp.einsum('ghd,khd->hgk', gqueries[positions], gkeys, precision=highest) * score_scale)
    peak_score = lax.optimization_barrier(jnp.max(spread, axis=-1, keepdims=True))
    spread_exp = jnp.exp(spread - peak_score)
    spread_prob = spread_exp / lax.optimization_barrier(jnp.sum(spread_exp, axis=-1, keepdims=True))
    glob_ctx = jnp.einsum('hgk,khd->ghd', low(spread_prob), gvalues, precision=highest).reshape(GLOB, D)
    context = low_both(local_ctx.at[positions].set(glob_ctx))
    attn_out = low_back(jnp.dot(context, out_w, precision=highest) + out_b)
    mixed = layer_norm(source + attn_out, gains[0], shifts[0])
    pre_act = low_back(jnp.dot(low(mixed), up_w, precision=highest) + up_b)
    activated = low(jax.nn.gelu(pre_act, approximate=False))
    branch = low_back(jnp.dot(activated, down_w, precision=highest) + down_b)
    return layer_norm(mixed + branch, gains[1], shifts[1])

def reference(layer_in, cotangent, masked_rows, global_positions, local_weight, local_bias, global_weight, global_bias, out_weight, out_bias, norm_gain, norm_shift, up_weight, up_bias, down_weight, down_bias):
    params = tuple((item.astype(jnp.float32) for item in (local_weight, local_bias, global_weight, global_bias, out_weight, out_bias, norm_gain, norm_shift, up_weight, up_bias, down_weight, down_bias)))
    doc_count = MICRO * DOCS
    inputs_all = layer_in.astype(jnp.float32).reshape(doc_count, LEN, D)
    cot_all = cotangent.astype(jnp.float32).reshape(doc_count, NMASK, D)
    rows_all = masked_rows.reshape(doc_count, NMASK)
    places_all = global_positions.reshape(doc_count, GLOB)

    def one_doc(carry, item):
        source, cot_rows, row_index, positions = item

        def whole(start_rows, probe, weights):
            lower = layer(start_rows, positions, tuple((member[0] for member in weights)), False)
            middle = low_back(low(lower) + probe)
            upper_out = layer(middle, positions, tuple((member[1] for member in weights)), True)
            return (upper_out, middle)
        probe = jnp.zeros((LEN, D), jnp.float32)
        top_out, back_fn, middle = jax.vjp(whole, source, probe, params, has_aux=True)
        full_cot = jnp.zeros((LEN, D), jnp.float32).at[row_index].set(cot_rows)
        d_source, d_middle, d_params = back_fn(full_cot)
        carry = jax.tree.map(jnp.add, carry, d_params)
        return (carry, (middle, top_out, d_source, d_middle))
    start_carry = jax.tree.map(jnp.zeros_like, params)
    grads_all, (middles, tops, d_sources, d_middles) = lax.scan(one_doc, start_carry, (inputs_all, cot_all, rows_all, places_all))
    out_shape = (MICRO, DOCS, LEN, D)
    layer_outputs = jnp.stack([middles.reshape(out_shape), tops.reshape(out_shape)]).astype(jnp.bfloat16)
    input_grads = jnp.stack([d_sources.reshape(out_shape), d_middles.reshape(out_shape)]).astype(jnp.bfloat16)
    return (layer_outputs, input_grads, grads_all[0], grads_all[1], grads_all[2], grads_all[3], grads_all[4], grads_all[5], grads_all[6], grads_all[7], grads_all[8], grads_all[9], grads_all[10], grads_all[11])
```

```python
from functools import partial
from types import SimpleNamespace

import jax
import jax.numpy as jnp
import numpy as np
from jax import lax
from jax.experimental import pallas as pl
from jax.experimental.pallas import tpu as pltpu
from jax.sharding import PartitionSpec as P

HEAD = 64
HALF = 256

SECTION, SEQ, DP = "section", "seq", "dp"
BOTH = (SECTION, SEQ)


far_below = -1e30
norm_eps = 1e-05


def padded(block, sides, width):
    for axis, dim in sides:
        count = lax.axis_size(axis)
        forward = [(i, i + 1) for i in range(count - 1)]
        backward = [(target, source) for source, target in forward]
        low = lax.ppermute(
            lax.slice_in_dim(block, block.shape[dim] - width, None, axis=dim), axis, forward
        )
        high = lax.ppermute(lax.slice_in_dim(block, 0, width, axis=dim), axis, backward)
        block = jnp.concatenate([low, block, high], axis=dim)
    return block


def joined(value, axis, join):
    pieces = jax.tree.map(lambda part: lax.all_gather(part, axis), value)
    head = jax.tree.map(lambda part: part[0], pieces)
    tail = jax.tree.map(lambda part: part[1:], pieces)
    running, _ = lax.scan(lambda running, piece: (join(running, piece), None), head, tail)
    return running


def shifted(shard, axis, by):
    length = lax.axis_size(axis)
    pairs = [(i, i + by) for i in range(length) if 0 <= i + by < length]
    return lax.ppermute(shard, axis, pairs)


def band_mask(first_row, row_count, reach_rows, length, positions, dilated):
    rows_at = first_row + jnp.arange(row_count)
    cols_at = first_row - reach_rows + jnp.arange(row_count + 2 * reach_rows)
    offset = cols_at[None, :] - rows_at[:, None]
    inside = (jnp.abs(offset) <= reach_rows) & (cols_at >= 0)[None, :] & (cols_at < length)[None, :]
    plain_key = jnp.logical_not(jnp.any(cols_at[:, None] == positions[None, :], axis=1))
    usable = inside & plain_key[None, :]
    even_gap = offset % 2 == 0
    return usable[None, :, :] & (jnp.logical_not(dilated)[:, None, None] | even_gap[None, :, :])


def layer_norm(values, gain_row, shift_row):
    center = values - jnp.mean(values, axis=-1, keepdims=True)
    scaled = lax.rsqrt(jnp.mean(center * center, axis=-1, keepdims=True) + norm_eps)
    unit_rows = center * scaled
    return (unit_rows * gain_row + shift_row, unit_rows, scaled)


def norm_back(unit_rows, scaled, gain_row, upstream):
    d_unit = upstream * gain_row
    inward = scaled * (
        d_unit
        - jnp.mean(d_unit, axis=-1, keepdims=True)
        - unit_rows * jnp.mean(d_unit * unit_rows, axis=-1, keepdims=True)
    )
    return (inward, jnp.sum(upstream * unit_rows, axis=0), jnp.sum(upstream, axis=0))


def join_stats(first_pair, second_pair):
    top_value = jnp.maximum(first_pair[0], second_pair[0])
    merged = first_pair[1] * jnp.exp(first_pair[0] - top_value) + second_pair[1] * jnp.exp(
        second_pair[0] - top_value
    )
    return (top_value, merged)


def forward_layer(source, positions, weights, first_row, length, dilated, active):
    local_w, local_b, glob_w, glob_b, out_w, out_b, gains, shifts, up_w, up_b, down_w, down_b = (
        weights
    )
    row_count = source.shape[0]
    model_width = source.shape[1]
    ff_width = up_w.shape[1]
    head_count = dilated.shape[0]
    head_size = model_width // head_count
    glob_count = positions.shape[0]
    score_scale = head_size ** (-0.5)
    owner_hit = (first_row + jnp.arange(row_count))[:, None] == positions[None, :]
    owner_low = owner_hit.astype(jnp.bfloat16)
    owner_full = owner_hit.astype(jnp.float32)
    is_global = jnp.any(owner_hit, axis=1)
    picked = jnp.einsum("cg,cd->gd", owner_low, source, preferred_element_type=jnp.float32)
    global_rows = lax.psum(picked.astype(jnp.bfloat16), SEQ)
    proj = jnp.dot(source, local_w, preferred_element_type=jnp.float32)
    queries = (proj[:, :model_width] + local_b[0]).astype(jnp.bfloat16)
    keys_low = proj[:, model_width : 2 * model_width].astype(jnp.bfloat16)
    values_low = (proj[:, 2 * model_width :] + local_b[1]).astype(jnp.bfloat16)
    gproj = jnp.dot(source, glob_w[:, model_width:], preferred_element_type=jnp.float32)
    gkeys = gproj[:, :model_width].astype(jnp.bfloat16)
    gvalues = (gproj[:, model_width:] + glob_b[1]).astype(jnp.bfloat16)
    gqueries = (
        jnp.dot(global_rows, glob_w[:, :model_width], preferred_element_type=jnp.float32)
        + glob_b[0]
    ).astype(jnp.bfloat16)
    side_proj = jnp.dot(global_rows, local_w[:, model_width:], preferred_element_type=jnp.float32)
    extra_keys = (
        side_proj[:, :model_width].astype(jnp.bfloat16).reshape(glob_count, head_count, head_size)
    )
    extra_values = (
        (side_proj[:, model_width:] + local_b[1])
        .astype(jnp.bfloat16)
        .reshape(glob_count, head_count, head_size)
    )
    key_value = jnp.concatenate([keys_low, values_low], axis=1)
    widened = padded(key_value, ((SEQ, 0),), HALF)
    reach_rows = (widened.shape[0] - row_count) // 2
    wide_keys = widened[:, :model_width].reshape(-1, head_count, head_size)
    wide_values = widened[:, model_width:].reshape(-1, head_count, head_size)
    allowed = band_mask(first_row, row_count, reach_rows, length, positions, dilated)
    queries_h = queries.reshape(row_count, head_count, head_size)
    band_score = (
        jnp.einsum("qhd,khd->hqk", queries_h, wide_keys, preferred_element_type=jnp.float32)
        * score_scale
    )
    band_score = jnp.where(allowed, band_score, far_below)
    toward = (
        jnp.einsum("qhd,ghd->hqg", queries_h, extra_keys, preferred_element_type=jnp.float32)
        * score_scale
    )
    peak_score = jnp.maximum(jnp.max(band_score, axis=-1), jnp.max(toward, axis=-1))[..., None]
    band_exp = jnp.exp(band_score - peak_score)
    toward_exp = jnp.exp(toward - peak_score)
    totals = jnp.sum(band_exp, axis=-1, keepdims=True) + jnp.sum(toward_exp, axis=-1, keepdims=True)
    band_full = band_exp / totals
    toward_full = toward_exp / totals
    band_prob = band_full.astype(jnp.bfloat16)
    toward_prob = toward_full.astype(jnp.bfloat16)
    local_ctx = jnp.einsum(
        "hqk,khd->qhd", band_prob, wide_values, preferred_element_type=jnp.float32
    ) + jnp.einsum("hqg,ghd->qhd", toward_prob, extra_values, preferred_element_type=jnp.float32)
    gqueries_h = gqueries.reshape(glob_count, head_count, head_size)
    gkeys_h = gkeys.reshape(row_count, head_count, head_size)
    gvalues_h = gvalues.reshape(row_count, head_count, head_size)
    spread = (
        jnp.einsum("ghd,khd->hgk", gqueries_h, gkeys_h, preferred_element_type=jnp.float32)
        * score_scale
    )
    part_peak = jnp.max(spread, axis=-1)
    part_total = jnp.sum(jnp.exp(spread - part_peak[..., None]), axis=-1)
    glob_peak, glob_total = joined((part_peak, part_total), SEQ, join_stats)
    glob_full = jnp.exp(spread - glob_peak[..., None]) / glob_total[..., None]
    glob_prob = glob_full.astype(jnp.bfloat16)
    part_ctx = jnp.einsum("hgk,khd->ghd", glob_prob, gvalues_h, preferred_element_type=jnp.float32)
    glob_ctx = lax.psum(part_ctx.reshape(glob_count, model_width), SEQ)
    placed_ctx = jnp.dot(owner_full, glob_ctx, precision=lax.Precision.HIGHEST)
    context = jnp.where(is_global[:, None], placed_ctx, local_ctx.reshape(row_count, model_width))
    context_low = context.astype(jnp.bfloat16)
    attn_out = jnp.dot(context_low, out_w, preferred_element_type=jnp.float32) + out_b
    mixed, unit_one, scale_one = layer_norm(
        source.astype(jnp.float32) + attn_out, gains[0], shifts[0]
    )

    def feed_forward(hidden_in):
        pre_act = (
            jnp.dot(hidden_in.astype(jnp.bfloat16), up_w, preferred_element_type=jnp.float32) + up_b
        )
        lifted = jax.nn.gelu(pre_act, approximate=False).astype(jnp.bfloat16)
        return (
            pre_act,
            lifted,
            jnp.dot(lifted, down_w, preferred_element_type=jnp.float32) + down_b,
        )

    def skip_block(hidden_in):
        return (
            jnp.zeros((row_count, ff_width), jnp.float32),
            jnp.zeros((row_count, ff_width), jnp.bfloat16),
            jnp.zeros((row_count, model_width), jnp.float32),
        )

    pre_act, activated, branch = lax.cond(active, feed_forward, skip_block, mixed)
    result, unit_two, scale_two = layer_norm(mixed + branch, gains[1], shifts[1])
    return SimpleNamespace(
        source=source,
        owner_low=owner_low,
        owner_full=owner_full,
        is_global=is_global,
        queries_h=queries_h,
        wide_keys=wide_keys,
        wide_values=wide_values,
        extra_keys=extra_keys,
        extra_values=extra_values,
        band_full=band_full,
        toward_full=toward_full,
        band_prob=band_prob,
        toward_prob=toward_prob,
        gqueries_h=gqueries_h,
        gkeys_h=gkeys_h,
        gvalues_h=gvalues_h,
        glob_full=glob_full,
        glob_prob=glob_prob,
        context_low=context_low,
        unit_one=unit_one,
        scale_one=scale_one,
        mixed=mixed,
        pre_act=pre_act,
        activated=activated,
        unit_two=unit_two,
        scale_two=scale_two,
        result=result,
        reach_rows=reach_rows,
        score_scale=score_scale,
    )


def ffn_back(kept_values, weights, upstream, active):
    local_w, local_b, glob_w, glob_b, out_w, out_b, gains, shifts, up_w, up_b, down_w, down_b = (
        weights
    )
    d_second, gain_two, shift_two = norm_back(
        kept_values.unit_two, kept_values.scale_two, gains[1], upstream
    )
    d_branch = d_second.astype(jnp.bfloat16)

    def ffn_work(operands):
        pre_act, d_out = operands
        d_lifted = jnp.einsum("cd,fd->cf", d_out, down_w, preferred_element_type=jnp.float32)
        gelu_vals, gelu_back = jax.vjp(partial(jax.nn.gelu, approximate=False), pre_act)
        d_pre = gelu_back(d_lifted)[0].astype(jnp.bfloat16)
        d_hidden = jnp.einsum("cf,df->cd", d_pre, up_w, preferred_element_type=jnp.float32)
        return (d_hidden, d_pre)

    def ffn_spare(operands):
        return (
            jnp.zeros(upstream.shape, jnp.float32),
            jnp.zeros((upstream.shape[0], up_w.shape[1]), jnp.bfloat16),
        )

    d_hidden, d_pre = lax.cond(active, ffn_work, ffn_spare, (kept_values.pre_act, d_branch))
    return (d_second + d_hidden, d_pre, d_branch, (gain_two, shift_two))


def attention_back(kept_values, weights, d_mixed):
    local_w, local_b, glob_w, glob_b, out_w, out_b, gains, shifts, up_w, up_b, down_w, down_b = (
        weights
    )
    row_count, model_width = kept_values.source.shape
    queries_h = kept_values.queries_h
    head_count, head_size = (queries_h.shape[1], queries_h.shape[2])
    glob_count = kept_values.owner_full.shape[1]
    reach_rows = kept_values.reach_rows
    score_scale = kept_values.score_scale
    d_first, gain_one, shift_one = norm_back(
        kept_values.unit_one, kept_values.scale_one, gains[0], d_mixed
    )
    d_attn = d_first.astype(jnp.bfloat16)
    d_context = jnp.einsum("ce,de->cd", d_attn, out_w, preferred_element_type=jnp.float32).astype(
        jnp.bfloat16
    )
    glob_part = jnp.einsum(
        "cg,cd->gd", kept_values.owner_low, d_context, preferred_element_type=jnp.float32
    )
    d_glob_ctx = lax.psum(glob_part.astype(jnp.bfloat16), SEQ)
    d_local = jnp.where(kept_values.is_global[:, None], jnp.zeros_like(d_context), d_context)
    d_local = d_local.reshape(row_count, head_count, head_size)
    band_full = kept_values.band_full
    toward_full = kept_values.toward_full
    d_band = jnp.einsum(
        "qhd,khd->hqk", d_local, kept_values.wide_values, preferred_element_type=jnp.float32
    )
    d_toward = jnp.einsum(
        "qhd,ghd->hqg", d_local, kept_values.extra_values, preferred_element_type=jnp.float32
    )
    inner_sum = jnp.sum(band_full * d_band, axis=-1) + jnp.sum(toward_full * d_toward, axis=-1)
    grad_band = (band_full * (d_band - inner_sum[..., None])).astype(jnp.bfloat16)
    grad_toward = (toward_full * (d_toward - inner_sum[..., None])).astype(jnp.bfloat16)
    d_queries = (
        jnp.einsum(
            "hqk,khd->qhd", grad_band, kept_values.wide_keys, preferred_element_type=jnp.float32
        )
        + jnp.einsum(
            "hqg,ghd->qhd",
            grad_toward,
            kept_values.extra_keys,
            preferred_element_type=jnp.float32,
        )
    ) * score_scale
    d_wide_keys = (
        jnp.einsum("hqk,qhd->khd", grad_band, queries_h, preferred_element_type=jnp.float32)
        * score_scale
    )
    d_wide_values = jnp.einsum(
        "hqk,qhd->khd", kept_values.band_prob, d_local, preferred_element_type=jnp.float32
    )
    d_extra_keys = (
        jnp.einsum("hqg,qhd->ghd", grad_toward, queries_h, preferred_element_type=jnp.float32)
        * score_scale
    )
    d_extra_values = jnp.einsum(
        "hqg,qhd->ghd", kept_values.toward_prob, d_local, preferred_element_type=jnp.float32
    )
    glob_full = kept_values.glob_full
    d_glob_h = d_glob_ctx.reshape(glob_count, head_count, head_size)
    d_spread = jnp.einsum(
        "ghd,khd->hgk", d_glob_h, kept_values.gvalues_h, preferred_element_type=jnp.float32
    )
    part_inner = jnp.sum(glob_full * d_spread, axis=-1)
    glob_inner, sum_extra_keys, sum_extra_values = (
        lax.psum(part_inner.astype(jnp.bfloat16), SEQ).astype(jnp.float32),
        lax.psum(d_extra_keys.reshape(glob_count, model_width).astype(jnp.bfloat16), SEQ).astype(
            jnp.float32
        ),
        lax.psum(
            d_extra_values.reshape(glob_count, model_width).astype(jnp.bfloat16), SEQ
        ).astype(jnp.float32),
    )
    grad_spread = (glob_full * (d_spread - glob_inner[..., None])).astype(jnp.bfloat16)
    part_query = (
        jnp.einsum(
            "hgk,khd->ghd", grad_spread, kept_values.gkeys_h, preferred_element_type=jnp.float32
        )
        * score_scale
    )
    d_gkeys = (
        jnp.einsum(
            "hgk,ghd->khd",
            grad_spread,
            kept_values.gqueries_h,
            preferred_element_type=jnp.float32,
        )
        * score_scale
    )
    d_gvalues = jnp.einsum(
        "hgk,ghd->khd", kept_values.glob_prob, d_glob_h, preferred_element_type=jnp.float32
    )
    d_gqueries = lax.psum(
        part_query.reshape(glob_count, model_width).astype(jnp.bfloat16), SEQ
    ).astype(jnp.float32)
    d_wide = jnp.concatenate(
        [d_wide_keys.reshape(-1, model_width), d_wide_values.reshape(-1, model_width)], axis=1
    )
    rim_grads = jnp.concatenate([d_wide[:reach_rows], d_wide[reach_rows + row_count :]], axis=0)
    incoming = padded(rim_grads.astype(jnp.bfloat16), ((SEQ, 0),), HALF).astype(rim_grads.dtype)
    own_part = (
        d_wide[reach_rows : reach_rows + row_count]
        + incoming[:reach_rows]
        + incoming[3 * reach_rows :]
    )
    owner_full = kept_values.owner_full
    d_keys_low = (
        own_part[:, :model_width]
        + jnp.dot(owner_full, sum_extra_keys, precision=lax.Precision.HIGHEST)
    ).astype(jnp.bfloat16)
    d_values_low = (
        own_part[:, model_width:]
        + jnp.dot(owner_full, sum_extra_values, precision=lax.Precision.HIGHEST)
    ).astype(jnp.bfloat16)
    d_queries_low = d_queries.reshape(row_count, model_width).astype(jnp.bfloat16)
    d_proj = jnp.concatenate([d_queries_low, d_keys_low, d_values_low], axis=1)
    d_gq_rows = jnp.dot(owner_full, d_gqueries, precision=lax.Precision.HIGHEST).astype(
        jnp.bfloat16
    )
    d_gproj = jnp.concatenate(
        [
            d_gq_rows,
            d_gkeys.reshape(row_count, model_width).astype(jnp.bfloat16),
            d_gvalues.reshape(row_count, model_width).astype(jnp.bfloat16),
        ],
        axis=1,
    )
    d_source = (
        d_first
        + jnp.einsum("ce,de->cd", d_proj, local_w, preferred_element_type=jnp.float32)
        + jnp.einsum("ce,de->cd", d_gproj, glob_w, preferred_element_type=jnp.float32)
    )
    return (d_source, d_proj, d_gproj, d_attn, (gain_one, shift_one))


def ffn_terms(mixed_buf, pre_buf, act_buf, branch_buf, count):
    return (
        jnp.einsum(
            "mcd,mcf->df", mixed_buf[:count], pre_buf[:count], preferred_element_type=jnp.float32
        ),
        jnp.sum(pre_buf[:count].astype(jnp.float32), axis=(0, 1)),
        jnp.einsum(
            "mcf,mcd->fd", act_buf[:count], branch_buf[:count], preferred_element_type=jnp.float32
        ),
        jnp.sum(branch_buf[:count].astype(jnp.float32), axis=(0, 1)),
    )


def on_device(
    layer_in,
    cotangent,
    masked_rows,
    global_positions,
    local_weight,
    local_bias,
    global_weight,
    global_bias,
    out_weight,
    out_bias,
    norm_gain,
    norm_shift,
    up_weight,
    up_bias,
    down_weight,
    down_bias,
):
    weights = (
        local_weight[0],
        local_bias[0],
        global_weight[0],
        global_bias[0],
        out_weight[0],
        out_bias[0],
        norm_gain[0],
        norm_shift[0],
        up_weight[0],
        up_bias[0],
        down_weight[0],
        down_bias[0],
    )
    section_index = lax.axis_index(SECTION)
    seq_index = lax.axis_index(SEQ)
    micro_count = layer_in.shape[0]
    row_count = layer_in.shape[2]
    model_width = layer_in.shape[3]
    ff_width = up_weight.shape[2]
    length = row_count * lax.axis_size(SEQ)
    first_row = seq_index * row_count
    head_count = model_width // HEAD
    dilated = (jnp.arange(head_count) >= head_count - 2) & (section_index == 1)
    kept_inputs = jnp.zeros((micro_count, row_count, model_width), jnp.bfloat16)
    outputs = jnp.zeros_like(kept_inputs)
    arrived = jnp.zeros((row_count, model_width), jnp.bfloat16)
    for step_index in range(micro_count + 1):
        micro_index = step_index - section_index
        in_range = (micro_index >= 0) & (micro_index < micro_count)
        slot_index = jnp.clip(micro_index, 0, micro_count - 1)
        fresh = lax.dynamic_index_in_dim(layer_in, slot_index, 0, keepdims=False)[0]
        source = jnp.where(section_index == 0, fresh, arrived)
        positions = lax.dynamic_index_in_dim(global_positions, slot_index, 0, keepdims=False)[0]
        kept_values = forward_layer(
            source, positions, weights, first_row, length, dilated, in_range
        )
        result = kept_values.result.astype(jnp.bfloat16)
        kept_inputs = jnp.where(
            in_range,
            lax.dynamic_update_index_in_dim(kept_inputs, source, slot_index, 0),
            kept_inputs,
        )
        outputs = jnp.where(
            in_range, lax.dynamic_update_index_in_dim(outputs, result, slot_index, 0), outputs
        )
        if step_index < micro_count:
            arrived = shifted(result, SECTION, 1)
    slots = micro_count + 1
    proj_buf = jnp.zeros((slots, row_count, 3 * model_width), jnp.bfloat16)
    gproj_buf = jnp.zeros_like(proj_buf)
    ctx_buf = jnp.zeros((slots, row_count, model_width), jnp.bfloat16)
    attn_buf = jnp.zeros_like(ctx_buf)
    mixed_buf = jnp.zeros_like(ctx_buf)
    branch_buf = jnp.zeros_like(ctx_buf)
    pre_buf = jnp.zeros((slots, row_count, ff_width), jnp.bfloat16)
    act_buf = jnp.zeros_like(pre_buf)
    gain_total = jnp.zeros((2, model_width), jnp.float32)
    shift_total = jnp.zeros((2, model_width), jnp.float32)
    back_arrived = jnp.zeros((row_count, model_width), jnp.bfloat16)
    in_grads = jnp.zeros_like(kept_inputs)
    for step_index in range(micro_count + 1):
        micro_index = step_index - 1 + section_index
        in_range = (micro_index >= 0) & (micro_index < micro_count)
        slot_index = jnp.clip(micro_index, 0, micro_count - 1)
        store = jnp.where(in_range, micro_index, micro_count)
        source = lax.dynamic_index_in_dim(kept_inputs, slot_index, 0, keepdims=False)
        positions = lax.dynamic_index_in_dim(global_positions, slot_index, 0, keepdims=False)[0]
        picked_rows = lax.dynamic_index_in_dim(masked_rows, slot_index, 0, keepdims=False)[0]
        picked_grads = lax.dynamic_index_in_dim(cotangent, slot_index, 0, keepdims=False)[0]
        row_hit = ((first_row + jnp.arange(row_count))[:, None] == picked_rows[None, :]).astype(
            jnp.bfloat16
        )
        placed = jnp.dot(row_hit, picked_grads, preferred_element_type=jnp.float32)
        upstream = jnp.where(section_index == 1, placed, back_arrived.astype(jnp.float32))
        kept_values = forward_layer(
            source, positions, weights, first_row, length, dilated, in_range
        )
        d_mixed, d_pre, d_branch, norm_two = ffn_back(kept_values, weights, upstream, in_range)
        mixed_buf = lax.dynamic_update_index_in_dim(
            mixed_buf, kept_values.mixed.astype(jnp.bfloat16), store, 0
        )
        pre_buf = lax.dynamic_update_index_in_dim(pre_buf, d_pre, store, 0)
        act_buf = lax.dynamic_update_index_in_dim(act_buf, kept_values.activated, store, 0)
        branch_buf = lax.dynamic_update_index_in_dim(branch_buf, d_branch, store, 0)
        d_source, d_proj, d_gproj, d_attn, norm_one = attention_back(kept_values, weights, d_mixed)
        proj_buf = lax.dynamic_update_index_in_dim(proj_buf, d_proj, store, 0)
        gproj_buf = lax.dynamic_update_index_in_dim(gproj_buf, d_gproj, store, 0)
        ctx_buf = lax.dynamic_update_index_in_dim(ctx_buf, kept_values.context_low, store, 0)
        attn_buf = lax.dynamic_update_index_in_dim(attn_buf, d_attn, store, 0)
        gain_total = gain_total + jnp.where(in_range, jnp.stack([norm_one[0], norm_two[0]]), 0.0)
        shift_total = shift_total + jnp.where(in_range, jnp.stack([norm_one[1], norm_two[1]]), 0.0)
        d_low = d_source.astype(jnp.bfloat16)
        in_grads = jnp.where(
            in_range, lax.dynamic_update_index_in_dim(in_grads, d_low, slot_index, 0), in_grads
        )
        if step_index < micro_count:
            back_arrived = shifted(d_low, SECTION, -1)
    used_proj = proj_buf[:micro_count]
    used_gproj = gproj_buf[:micro_count]
    grad_local = jnp.einsum(
        "mcd,mce->de", kept_inputs, used_proj, preferred_element_type=jnp.float32
    )
    grad_glob = jnp.einsum(
        "mcd,mce->de", kept_inputs, used_gproj, preferred_element_type=jnp.float32
    )
    grad_out = jnp.einsum(
        "mcd,mce->de",
        ctx_buf[:micro_count],
        attn_buf[:micro_count],
        preferred_element_type=jnp.float32,
    )
    grad_out_b = jnp.sum(attn_buf[:micro_count].astype(jnp.float32), axis=(0, 1))
    local_b_grad = jnp.stack(
        [
            jnp.sum(used_proj[:, :, :model_width].astype(jnp.float32), axis=(0, 1)),
            jnp.sum(used_proj[:, :, 2 * model_width :].astype(jnp.float32), axis=(0, 1)),
        ]
    )
    glob_b_grad = jnp.stack(
        [
            jnp.sum(used_gproj[:, :, :model_width].astype(jnp.float32), axis=(0, 1)),
            jnp.sum(used_gproj[:, :, 2 * model_width :].astype(jnp.float32), axis=(0, 1)),
        ]
    )
    small_sums = lax.psum((local_b_grad, glob_b_grad, gain_total, shift_total), (SEQ, DP))
    ffn_parts = ffn_terms(mixed_buf, pre_buf, act_buf, branch_buf, micro_count)
    large_sums = (
        lax.psum_scatter(grad_local, (SEQ, DP), scatter_dimension=0, tiled=True),
        lax.psum_scatter(grad_glob, (SEQ, DP), scatter_dimension=0, tiled=True),
        lax.psum_scatter(grad_out, (SEQ, DP), scatter_dimension=0, tiled=True),
        lax.psum_scatter(grad_out_b, (SEQ, DP), scatter_dimension=0, tiled=True),
        lax.psum_scatter(ffn_parts[0], (SEQ, DP), scatter_dimension=0, tiled=True),
        lax.psum_scatter(ffn_parts[1], (SEQ, DP), scatter_dimension=0, tiled=True),
        lax.psum_scatter(ffn_parts[2], (SEQ, DP), scatter_dimension=0, tiled=True),
        lax.psum_scatter(ffn_parts[3], (SEQ, DP), scatter_dimension=0, tiled=True),
    )
    summed = (
        large_sums[0],
        small_sums[0],
        large_sums[1],
        small_sums[1],
        large_sums[2],
        large_sums[3],
        small_sums[2],
        small_sums[3],
        large_sums[4],
        large_sums[5],
        large_sums[6],
        large_sums[7],
    )
    return (outputs[None, :, None], in_grads[None, :, None]) + tuple(
        (member[None] for member in summed)
    )


bf16 = jnp.bfloat16
f32 = jnp.float32
VMEM_BYTES = 60 * 1024 * 1024
VMEM_GRADS = 40 * 1024 * 1024


def nn(a, b):
    return jnp.dot(a, b, preferred_element_type=f32)


def nt(a, b):
    return lax.dot_general(a, b, (((1,), (1,)), ((), ())), preferred_element_type=f32)


def tn(a, b):
    return lax.dot_general(a, b, (((0,), (0,)), ((), ())), preferred_element_type=f32)


def owner_rows(prow, chunk, rows):
    at = lax.broadcasted_iota(jnp.int32, (rows, prow.shape[1]), 0) + chunk * rows
    return (at == prow[...]).astype(f32)


def owner_cols(pcol, chunk, rows):
    at = lax.broadcasted_iota(jnp.int32, (pcol.shape[0], rows), 1) + chunk * rows
    return (at == pcol[...]).astype(f32)


def is_dilated(layer, group, h):
    return ((3 * group + h >= 10) & (layer == 1)).astype(jnp.int32)


def band_masks(mask_s, dilated, rows):
    row = lax.broadcasted_iota(jnp.int32, (rows, rows), 0)
    col = lax.broadcasted_iota(jnp.int32, (rows, rows), 1)
    odd = ((row + col) % 2).astype(f32)
    level = odd * (dilated.astype(f32) * far_below)
    mask_s[0] = jnp.where(row >= col, level, far_below)
    mask_s[1] = level
    mask_s[2] = jnp.where(row <= col, level, far_below)


def neighbours(block, count):
    return [b for b in (block - 1, block, block + 1) if 0 <= b < count]


def cost(us):
    return pl.CostEstimate(
        flops=int(us * 1e9), transcendentals=0, bytes_accessed=int(us * 3.5e6)
    )


def choose(flag, first, second, target, sem):
    for value, source in ((0, first), (1, second)):

        @pl.when(flag == value)
        def _(source=source):
            pltpu.make_async_copy(source, target, sem).start()

    return pltpu.make_async_copy(first, target, sem)


def prepare_kernel(
    ids, lw, gw, lb, gb, ob, ng, ns, db, ub, own_o, send_o, pack_o, win_s, sems
):
    width = lw.shape[0]
    hw = width // 4
    sources = [(lw, 0), (lw, 1), (lw, 2), (gw, 1), (gw, 2), (gw, 0)]
    copies = []
    for t, group in enumerate((ids[1], ids[0])):
        for i, (ref, part) in enumerate(sources):
            start = pl.multiple_of(part * width + 128 * ((3 * group) // 2), 128)
            copies.append(
                pltpu.make_async_copy(
                    ref.at[:, pl.ds(start, 256)], win_s.at[t, i], sems.at[6 * t + i]
                )
            )
            copies[-1].start()
    pack_o[...] = jnp.zeros(pack_o.shape, bf16)
    at = 0
    for ref in (lb, gb, ob, ng, ns, db):
        pack_o[at : at + ref.shape[0], :] = ref[...]
        at += ref.shape[0]
    for i in range(ub.shape[1] // width):
        pack_o[at + i : at + i + 1, :] = ub[:, i * width : (i + 1) * width]
    for t, target in enumerate((send_o, own_o)):
        for i in range(6):
            copies[6 * t + i].wait()
        for odd in range(2):

            @pl.when(ids[6] == odd)
            def _(t=t, target=target, odd=odd):
                parts = [win_s[t, i][:, 64 * odd : 64 * odd + hw] for i in range(6)]
                target[...] = jnp.concatenate(parts, axis=1)


def prepare(ids, local_w, global_w, rows):
    width = local_w.shape[0]
    vm = pl.BlockSpec(memory_space=pltpu.VMEM)
    hbm = pl.BlockSpec(memory_space=pl.ANY)
    chosen = jax.ShapeDtypeStruct((width, 6 * width // 4), bf16)
    return pl.pallas_call(
        prepare_kernel,
        out_shape=[chosen, chosen, jax.ShapeDtypeStruct((16, width), bf16)],
        in_specs=[pl.BlockSpec(memory_space=pltpu.SMEM), hbm, hbm] + [vm] * 7,
        out_specs=[vm] * 3,
        scratch_shapes=[
            pltpu.VMEM((2, 6, width, 256), bf16),
            pltpu.SemaphoreType.DMA((12,)),
        ],
        compiler_params=pltpu.CompilerParams(vmem_limit_bytes=VMEM_BYTES),
        cost_estimate=cost(3),
        name="prepare",
    )(ids, local_w, global_w, *rows)


def attend_kernel(layer, *refs):
    count = 4
    sources = 7 if layer == 0 else 4
    ids, parts, refs = refs[0], refs[1 : 1 + sources], refs[1 + sources :]
    (
        w_a, w_b, pack_a, pack_b, prow, pcol,
        c0, c1, c2, c3, u_o, own_o, q_o, k_o, v_o, gk_o, gv_o, gq_o, kg_o, vg_o, lse_o,
        w_s, sem, vt_s, mask_s, ctx_s, gctx_s,
    ) = refs
    rows = c0.shape[0]
    heads = q_o.shape[0]
    hw = heads * HEAD
    scale = HEAD ** (-0.5)
    glob = prow.shape[1]
    group, core = ids[0], ids[4]
    w_copy = choose((core != layer).astype(jnp.int32), w_a, w_b, w_s, sem)
    if layer == 0:
        block = parts[0]
        half = rows // 2
        u_o[pl.ds(pl.multiple_of((2 * ids[5] + ids[6]) * rows, rows), rows), :] = block[ids[5]]
        places = (
            2 * ids[5] + 1 - ids[6],
            2 * (1 - ids[5]) + ids[6],
            2 * (1 - ids[5]) + 1 - ids[6],
        )
        for i, place in enumerate(places):
            for part, side in ((parts[1 + i], core), (parts[4 + i], 1 - core)):
                at = pl.multiple_of(place * rows + side * half, half)
                u_o[pl.ds(at, half), :] = part[...]
    else:
        for r in range(count):
            u_o[pl.ds(pl.multiple_of(ids[r] * rows, rows), rows), :] = parts[r][...]
    own_o[...] = u_o[pl.ds(pl.multiple_of(group * rows, rows), rows), :]
    pack = jnp.where(core == layer, pack_a[...].astype(f32), pack_b[...].astype(f32))[:4]
    hb = pack[:, :hw]
    for i in range(1, 4):
        hb = jnp.where(group == i, pack[:, i * hw : (i + 1) * hw], hb)
    kg_all = jnp.zeros((glob, hw), f32)
    vg_all = jnp.zeros((glob, hw), f32)
    ug_all = jnp.zeros((glob, u_o.shape[1]), f32)
    first = lax.broadcasted_iota(jnp.int32, (rows, HEAD), 1) == 0
    w_copy.wait()
    w = w_s
    for chunk in range(count):
        at = slice(chunk * rows, (chunk + 1) * rows)
        x = u_o[at, :]
        p = nn(x, w[:, : 5 * hw])
        queries = (p[:, :hw] + hb[0:1, :]).astype(bf16).astype(f32) * scale
        keys = p[:, hw : 2 * hw]
        values = p[:, 2 * hw : 3 * hw] + hb[1:2, :]
        gkeys = p[:, 3 * hw : 4 * hw]
        gvalues = p[:, 4 * hw : 5 * hw] + hb[3:4, :]
        is_global = jnp.max(owner_rows(prow, chunk, rows), axis=1, keepdims=True)
        tail_k = jnp.where(first, is_global * far_below, 0.0)
        tail_q = jnp.where(first, 1.0, 0.0)
        for h in range(heads):
            cut = slice(HEAD * h, HEAD * h + HEAD)
            q_o[h, at, :] = jnp.concatenate([queries[:, cut], tail_q], axis=1).astype(bf16)
            k_o[h, at, :] = jnp.concatenate([keys[:, cut], tail_k], axis=1).astype(bf16)
            v_o[h, at, :] = values[:, cut].astype(bf16)
            gk_o[h, at, :] = gkeys[:, cut].astype(bf16)
            gv_o[h, at, :] = gvalues[:, cut].astype(bf16)
            vt_s[h, chunk] = values[:, cut].T.astype(bf16)
        hit = owner_cols(pcol, chunk, rows).astype(bf16)
        kg_all += nn(hit, keys.astype(bf16))
        vg_all += nn(hit, values.astype(bf16))
        ug_all += nn(hit, x)
    gq_all = (nn(ug_all.astype(bf16), w[:, 5 * hw :]) + hb[2:3, :]).astype(bf16).astype(f32) * scale
    none = jnp.zeros((glob, HEAD), f32)
    for h in range(heads):
        cut = slice(HEAD * h, HEAD * h + HEAD)
        gq_o[h] = gq_all[:, cut].astype(bf16)
        kg_o[h] = jnp.concatenate([kg_all[:, cut], none], axis=1).astype(bf16)
        vg_o[h] = vg_all[:, cut].astype(bf16)

    def head(h, carry):
        band_masks(mask_s, is_dilated(layer, group, h), rows)
        kg = kg_o[h]
        vgt = vg_o[h].astype(f32).T.astype(bf16)
        for qb in range(count):
            q = q_o[h, qb * rows : (qb + 1) * rows, :]
            near = neighbours(qb, count)
            scores = [
                nt(k_o[h, kb * rows : (kb + 1) * rows, :], q) + mask_s[kb - qb + 1] for kb in near
            ]
            side = nt(kg, q)
            peak = jnp.max(side, axis=0, keepdims=True)
            for s in scores:
                peak = jnp.maximum(peak, jnp.max(s, axis=0, keepdims=True))
            side = jnp.exp(side - peak)
            scores = [jnp.exp(s - peak) for s in scores]
            total = jnp.sum(side, axis=0, keepdims=True)
            for s in scores:
                total += jnp.sum(s, axis=0, keepdims=True)
            inverse = 1.0 / total
            ctx = nn(vgt, (side * inverse).astype(bf16))
            for kb, s in zip(near, scores):
                ctx += nn(vt_s[h, kb], (s * inverse).astype(bf16))
            ctx_s[h, qb * rows : (qb + 1) * rows, :] = ctx.T
            lse_o[h, qb : qb + 1, :] = peak + jnp.log(total)
        spread = nt(gq_o[h], gk_o[h])
        e = jnp.exp(spread - jnp.max(spread, axis=1, keepdims=True))
        prob = (e / jnp.sum(e, axis=1, keepdims=True)).astype(bf16)
        gctx_s[h] = nn(prob, gv_o[h])
        return carry

    lax.fori_loop(0, heads, head, 0)
    gctx = jnp.concatenate([gctx_s[h] for h in range(heads)], axis=1).astype(bf16)
    for r, c_o in enumerate((c0, c1, c2, c3)):
        chunk = ids[r]
        at = pl.ds(pl.multiple_of(chunk * rows, rows), rows)
        hit = owner_rows(prow, chunk, rows)
        placed = nn(hit.astype(bf16), gctx)
        local = jnp.concatenate([ctx_s[h, at, :] for h in range(heads)], axis=1)
        c_o[...] = jnp.where(jnp.max(hit, axis=1, keepdims=True) > 0, placed, local).astype(bf16)


def attend(layer, ids, parts, weights, packs, prow, pcol):
    width = weights[0].shape[0]
    hw = weights[0].shape[1] // 6
    heads = hw // HEAD
    glob = prow.shape[1]
    rows = HALF
    full = 4 * rows
    sds = jax.ShapeDtypeStruct
    outs = [sds((rows, hw), bf16)] * 4 + [
        sds((full, width), bf16),
        sds((rows, width), bf16),
        sds((heads, full, 2 * HEAD), bf16),
        sds((heads, full, 2 * HEAD), bf16),
        sds((heads, full, HEAD), bf16),
        sds((heads, full, HEAD), bf16),
        sds((heads, full, HEAD), bf16),
        sds((heads, glob, HEAD), bf16),
        sds((heads, glob, 2 * HEAD), bf16),
        sds((heads, glob, HEAD), bf16),
        sds((heads, 4, rows), f32),
    ]
    vm = pl.BlockSpec(memory_space=pltpu.VMEM)
    hbm = pl.BlockSpec(memory_space=pl.ANY)
    res = pl.pallas_call(
        partial(attend_kernel, layer),
        out_shape=outs,
        in_specs=[pl.BlockSpec(memory_space=pltpu.SMEM)]
        + [vm] * len(parts)
        + [hbm] * 2
        + [vm] * 4,
        out_specs=[vm] * len(outs),
        scratch_shapes=[
            pltpu.VMEM(weights[0].shape, bf16),
            pltpu.SemaphoreType.DMA,
            pltpu.VMEM((heads, 4, HEAD, rows), bf16),
            pltpu.VMEM((3, rows, rows), f32),
            pltpu.VMEM((heads, full, HEAD), f32),
            pltpu.VMEM((heads, glob, HEAD), f32),
        ],
        compiler_params=pltpu.CompilerParams(vmem_limit_bytes=VMEM_BYTES),
        cost_estimate=cost(14),
        name="attend",
    )(ids, *parts, *weights, *packs, prow, pcol)
    return res[:4], res[4], res[5], res[6:]


def attend_back_kernel(
    layer, ids, d0, d1, d2, d3, q, k, v, gk, gv, gq, kg, vg, lse, prow, pcol, w_a, w_b,
    d_o, bias_o, p0, p1, p2, p3,
    w_s, sem, mask_s, do_s, dog_s, dq_s, dk_s, dv_s, dkg_s, dvg_s, dgk_s, dgv_s, dgq_s,
):
    rows = d0.shape[0]
    heads = q.shape[0]
    count = 4
    scale = HEAD ** (-0.5)
    glob = prow.shape[1]
    w_copy = choose((ids[4] != layer).astype(jnp.int32), w_a, w_b, w_s, sem)
    dg_all = jnp.zeros((glob, heads * HEAD), f32)
    for r, d in enumerate((d0, d1, d2, d3)):
        chunk = ids[r]
        at = pl.ds(pl.multiple_of(chunk * rows, rows), rows)
        dx = d[...]
        dg_all += nn(owner_cols(pcol, chunk, rows).astype(bf16), dx)
        is_global = jnp.max(owner_rows(prow, chunk, rows), axis=1, keepdims=True)
        local = jnp.where(is_global > 0, 0.0, dx.astype(f32))
        for h in range(heads):
            do_s[h, at, :] = local[:, HEAD * h : HEAD * h + HEAD].astype(bf16)
    for h in range(heads):
        dog_s[h] = dg_all[:, HEAD * h : HEAD * h + HEAD].astype(bf16)

    def head(h, carry):
        band_masks(mask_s, is_dilated(layer, ids[0], h), rows)
        kgh = kg[h]
        vgh = vg[h]
        kgt = kgh[:, :HEAD].astype(f32).T.astype(bf16)
        kt = [
            k[h, b * rows : (b + 1) * rows, :][:, :HEAD].astype(f32).T.astype(bf16)
            for b in range(count)
        ]
        dk = [jnp.zeros((rows, 2 * HEAD), f32) for _ in range(count)]
        dv = [jnp.zeros((rows, HEAD), f32) for _ in range(count)]
        dkg = jnp.zeros((glob, 2 * HEAD), f32)
        dvg = jnp.zeros((glob, HEAD), f32)
        for qb in range(count):
            span = slice(qb * rows, (qb + 1) * rows)
            qq = q[h, span, :]
            do = do_s[h, span, :]
            row = lse[h, qb : qb + 1, :]
            near = neighbours(qb, count)
            prob = [
                jnp.exp(nt(k[h, b * rows : (b + 1) * rows, :], qq) + mask_s[b - qb + 1] - row)
                for b in near
            ]
            side = jnp.exp(nt(kgh, qq) - row)
            dprob = [nt(v[h, b * rows : (b + 1) * rows, :], do) for b in near]
            dside = nt(vgh, do)
            inner = jnp.sum(side * dside, axis=0, keepdims=True)
            for p, dp in zip(prob, dprob):
                inner += jnp.sum(p * dp, axis=0, keepdims=True)
            ds = (side * (dside - inner)).astype(bf16)
            dvg += nn(side.astype(bf16), do)
            dkg += nn(ds, qq)
            dq = nn(kgt, ds)
            for b, p, dp in zip(near, prob, dprob):
                ds = (p * (dp - inner)).astype(bf16)
                dv[b] += nn(p.astype(bf16), do)
                dk[b] += nn(ds, qq)
                dq += nn(kt[b], ds)
            dq_s[h, span, :] = dq.T * scale
        for b in range(count):
            dk_s[h, b * rows : (b + 1) * rows, :] = dk[b][:, :HEAD]
            dv_s[h, b * rows : (b + 1) * rows, :] = dv[b]
        dkg_s[h] = dkg[:, :HEAD]
        dvg_s[h] = dvg
        spread = nt(gk[h], gq[h])
        e = jnp.exp(spread - jnp.max(spread, axis=0, keepdims=True))
        p = e / jnp.sum(e, axis=0, keepdims=True)
        dog = dog_s[h]
        dp = nt(gv[h], dog)
        ds = (p * (dp - jnp.sum(p * dp, axis=0, keepdims=True))).astype(bf16)
        dgv_s[h] = nn(p.astype(bf16), dog)
        dgk_s[h] = nn(ds, gq[h])
        dgq_s[h] = tn(ds, gk[h]) * scale
        return carry

    lax.fori_loop(0, heads, head, 0)

    def wide(ref, at=None):
        parts = [ref[h] if at is None else ref[h, at, :] for h in range(heads)]
        return jnp.concatenate(parts, axis=1)

    dkg_all = wide(dkg_s).astype(bf16)
    dvg_all = wide(dvg_s).astype(bf16)
    dgq_all = wide(dgq_s).astype(bf16)
    sums = [jnp.zeros((1, heads * HEAD), f32) for _ in range(4)]
    w_copy.wait()
    for r, p_o in enumerate((p0, p1, p2, p3)):
        chunk = ids[r]
        at = pl.ds(pl.multiple_of(chunk * rows, rows), rows)
        hit = owner_rows(prow, chunk, rows).astype(bf16)
        dq = wide(dq_s, at)
        dk = wide(dk_s, at) + nn(hit, dkg_all)
        dv = wide(dv_s, at) + nn(hit, dvg_all)
        dgk = wide(dgk_s, at)
        dgv = wide(dgv_s, at)
        dgq = nn(hit, dgq_all)
        joint = jnp.concatenate([dq, dk, dv, dgk, dgv, dgq], axis=1).astype(bf16)
        d_o[at, :] = joint
        p_o[...] = nt(joint, w_s[...]).astype(p_o.dtype)
        for i, part in enumerate((dq, dv, dgq, dgv)):
            sums[i] += jnp.sum(part, axis=0, keepdims=True)
    bias_o[...] = jnp.concatenate(sums, axis=0)


def attend_back(layer, ids, pieces, kept, prow, pcol, weights):
    rows, hw = pieces[0].shape
    width = weights[0].shape[0]
    heads = hw // HEAD
    glob = prow.shape[1]
    full = 4 * rows
    vm = pl.BlockSpec(memory_space=pltpu.VMEM)
    hbm = pl.BlockSpec(memory_space=pl.ANY)
    big = (heads, full, HEAD)
    small = (heads, glob, HEAD)
    res = pl.pallas_call(
        partial(attend_back_kernel, layer),
        out_shape=[
            jax.ShapeDtypeStruct((full, 6 * hw), bf16),
            jax.ShapeDtypeStruct((4, hw), f32),
        ]
        + [jax.ShapeDtypeStruct((rows, width), t) for t in (f32, bf16, f32, bf16)],
        in_specs=[pl.BlockSpec(memory_space=pltpu.SMEM)] + [vm] * 15 + [hbm] * 2,
        out_specs=[vm] * 6,
        scratch_shapes=[
            pltpu.VMEM(weights[0].shape, bf16),
            pltpu.SemaphoreType.DMA,
            pltpu.VMEM((3, rows, rows), f32),
            pltpu.VMEM(big, bf16),
            pltpu.VMEM(small, bf16),
            pltpu.VMEM(big, f32),
            pltpu.VMEM(big, f32),
            pltpu.VMEM(big, f32),
            pltpu.VMEM(small, f32),
            pltpu.VMEM(small, f32),
            pltpu.VMEM(big, f32),
            pltpu.VMEM(big, f32),
            pltpu.VMEM(small, f32),
        ],
        compiler_params=pltpu.CompilerParams(vmem_limit_bytes=VMEM_BYTES),
        cost_estimate=cost(18),
        name="attend_back",
    )(ids, *pieces, *kept, prow, pcol, *weights)
    return res[0], res[1], res[2:]


def fetch(first, second, use_second, pairs, sems):
    for flag, source in ((0, first), (1, second)):

        @pl.when(use_second.astype(jnp.int32) == flag)
        def _(source=source):
            for i, (pick, target) in enumerate(pairs):
                pltpu.make_async_copy(pick(source), target, sems.at[i]).start()

    def wait(i):
        pick, target = pairs[i]
        pltpu.make_async_copy(pick(first), target, sems.at[i]).wait()

    return wait


def weight_pairs(steps, cols, wo_s, wu_s, wd_s):
    pairs = [(lambda w: w[0], wo_s)]
    for j in range(steps):
        pairs.append((lambda w, j=j: w[1].at[:, pl.ds(j * cols, cols)], wu_s.at[j]))
        pairs.append((lambda w, j=j: w[2].at[pl.ds(j * cols, cols), :], wd_s.at[j]))
    return pairs


def row_norm(z):
    center = z - jnp.mean(z, axis=1, keepdims=True)
    scaled = lax.rsqrt(jnp.mean(center * center, axis=1, keepdims=True) + norm_eps)
    return center * scaled, scaled


def rows_kernel(
    layer, ids, c0, c1, c2, c3, u, pack_a, pack_b, wo_a, wo_b, wu_a, wu_b, wd_a, wd_b,
    y_o, fwd_o, slope_o, unit1_o, unit2_o, scale1_o, scale2_o,
    wo_s, wu_s, wd_s, sems,
):
    steps, cols = wu_s.shape[0], wu_s.shape[2]
    pairs = weight_pairs(steps, cols, wo_s, wu_s, wd_s)
    wait = fetch((wo_a, wu_a, wd_a), (wo_b, wu_b, wd_b), ids[4] != layer, pairs, sems)
    pack = jnp.where(ids[4] == layer, pack_a[...].astype(f32), pack_b[...].astype(f32))
    hw = c0.shape[1]
    width = 4 * hw
    pieces = [c[...] for c in (c0, c1, c2, c3)]
    for a in range(4):
        part = pieces[0]
        for r in range(1, 4):
            part = jnp.where(ids[r] == a, pieces[r].astype(f32), part.astype(f32))
        fwd_o[:, width + a * hw : width + (a + 1) * hw] = part.astype(bf16)
    wait(0)
    attn = nn(fwd_o[:, width : 2 * width], wo_s[...]) + pack[4:5, :]
    unit1, scale1 = row_norm(u[...].astype(f32) + attn)
    mixed = unit1 * pack[5:6, :] + pack[7:8, :]
    low = mixed.astype(bf16)
    fwd_o[:, :width] = low
    unit1_o[...] = unit1
    scale1_o[...] = jnp.broadcast_to(scale1, scale1_o.shape)
    branch = jnp.zeros(mixed.shape, f32)
    for j in range(steps):
        wait(1 + 2 * j)
        pre = nn(low, wu_s[j]) + pack[10 + j : 11 + j, :]
        gauss = 0.5 * (1.0 + lax.erf(pre * (2.0 ** -0.5)))
        act = (pre * gauss).astype(bf16)
        bell = jnp.exp(-0.5 * pre * pre) * ((2.0 * np.pi) ** -0.5)
        slope_o[:, j * cols : (j + 1) * cols] = (gauss + pre * bell).astype(bf16)
        fwd_o[:, 2 * width + j * cols : 2 * width + (j + 1) * cols] = act
        wait(2 + 2 * j)
        branch += nn(act, wd_s[j])
    unit2, scale2 = row_norm(mixed + (branch + pack[9:10, :]))
    unit2_o[...] = unit2
    scale2_o[...] = jnp.broadcast_to(scale2, scale2_o.shape)
    y_o[...] = (unit2 * pack[6:7, :] + pack[8:9, :]).astype(bf16)


def rows_forward(layer, ids, pieces, u, packs, own, other):
    rows, width = u.shape
    ff = own[1].shape[1]
    steps = ff // width
    vm = pl.BlockSpec(memory_space=pltpu.VMEM)
    hbm = pl.BlockSpec(memory_space=pl.ANY)
    sds = jax.ShapeDtypeStruct
    return pl.pallas_call(
        partial(rows_kernel, layer),
        out_shape=[
            sds((rows, width), bf16),
            sds((rows, 2 * width + ff), bf16),
            sds((rows, ff), bf16),
            sds((rows, width), f32),
            sds((rows, width), f32),
            sds((rows, 128), f32),
            sds((rows, 128), f32),
        ],
        in_specs=[pl.BlockSpec(memory_space=pltpu.SMEM)] + [vm] * 7 + [hbm] * 6,
        out_specs=[vm] * 7,
        scratch_shapes=[
            pltpu.VMEM((width, width), bf16),
            pltpu.VMEM((steps, width, width), bf16),
            pltpu.VMEM((steps, width, width), bf16),
            pltpu.SemaphoreType.DMA((1 + 2 * steps,)),
        ],
        compiler_params=pltpu.CompilerParams(vmem_limit_bytes=VMEM_BYTES),
        cost_estimate=cost(10),
        name="rows_forward",
    )(ids, *pieces, u, *packs, own[0], other[0], own[1], other[1], own[2], other[2])


def norm_inward(unit, scaled, gain, upstream):
    d_unit = upstream * gain
    return scaled * (
        d_unit
        - jnp.mean(d_unit, axis=1, keepdims=True)
        - unit * jnp.mean(d_unit * unit, axis=1, keepdims=True)
    )


def rows_back_kernel(
    layer, ids, up, unit1, unit2, scale1, scale2, slope, pack_a, pack_b, wo_a, wo_b, wu_a, wu_b, wd_a, wd_b,
    first_o, d0, d1, d2, d3, keep_o, send_o, small_o,
    wo_s, wu_s, wd_s, sems,
):
    steps, cols = wu_s.shape[0], wu_s.shape[2]
    pairs = weight_pairs(steps, cols, wo_s, wu_s, wd_s)
    wait = fetch((wo_a, wu_a, wd_a), (wo_b, wu_b, wd_b), ids[4] != layer, pairs, sems)
    pack = jnp.where(ids[4] == layer, pack_a[...].astype(f32), pack_b[...].astype(f32))
    side = ids[4]
    half = first_o.shape[1] // 2
    ffh = keep_o.shape[1] - 2 * half

    def split(value, at):
        for s in range(2):

            @pl.when(side == s)
            def _(s=s):
                keep_o[:, at : at + half] = value[:, s * half : (s + 1) * half]
                send_o[:, at : at + half] = value[:, (1 - s) * half : (2 - s) * half]

    def total(value):
        return jnp.sum(value, axis=0, keepdims=True)

    upstream = up[...].astype(f32)
    unit = unit2[...]
    small_o[0:1, :] = total(upstream * unit)
    small_o[1:2, :] = total(upstream)
    d_second = norm_inward(unit, scale2[:, :1], pack[6:7, :], upstream)
    d_branch = d_second.astype(bf16)
    split(d_branch, ffh)
    small_o[5:6, :] = total(d_branch.astype(f32))
    d_mixed = d_second
    for j in range(steps):
        wait(2 + 2 * j)
        d_act = nt(d_branch, wd_s[j])
        d_pre = (d_act * slope[:, j * cols : (j + 1) * cols].astype(f32)).astype(bf16)
        small_o[6 + j : 7 + j, :] = total(d_pre.astype(f32))
        place = slice((j % (steps // 2)) * cols, (j % (steps // 2) + 1) * cols)

        @pl.when(side == j // (steps // 2))
        def _(d_pre=d_pre, place=place):
            keep_o[:, place] = d_pre

        @pl.when(side != j // (steps // 2))
        def _(d_pre=d_pre, place=place):
            send_o[:, place] = d_pre

        wait(1 + 2 * j)
        d_mixed += nt(d_pre, wu_s[j])
    unit = unit1[...]
    small_o[2:3, :] = total(d_mixed * unit)
    small_o[3:4, :] = total(d_mixed)
    d_first = norm_inward(unit, scale1[:, :1], pack[5:6, :], d_mixed)
    first_o[...] = d_first
    d_attn = d_first.astype(bf16)
    split(d_attn, ffh + half)
    small_o[4:5, :] = total(d_attn.astype(f32))
    small_o[10:, :] = jnp.zeros((small_o.shape[0] - 10, small_o.shape[1]), f32)
    wait(0)
    d_ctx = nt(d_attn, wo_s[...])
    hw = d0.shape[1]
    parts = [d_ctx[:, a * hw : (a + 1) * hw] for a in range(4)]
    for r, d_o in enumerate((d0, d1, d2, d3)):
        part = parts[0]
        for a in range(1, 4):
            part = jnp.where(ids[r] == a, parts[a], part)
        d_o[...] = part.astype(bf16)


def rows_back(layer, ids, upstream, kept, packs, own, other):
    rows, width = upstream.shape
    ff = own[1].shape[1]
    steps = ff // width
    hw = width // 4
    unit1, unit2, scale1, scale2, slope = kept
    vm = pl.BlockSpec(memory_space=pltpu.VMEM)
    hbm = pl.BlockSpec(memory_space=pl.ANY)
    sds = jax.ShapeDtypeStruct
    return pl.pallas_call(
        partial(rows_back_kernel, layer),
        out_shape=[sds((rows, width), f32)]
        + [sds((rows, hw), bf16)] * 4
        + [sds((rows, ff // 2 + width), bf16)] * 2
        + [sds((16, width), f32)],
        in_specs=[pl.BlockSpec(memory_space=pltpu.SMEM)] + [vm] * 8 + [hbm] * 6,
        out_specs=[vm] * 8,
        scratch_shapes=[
            pltpu.VMEM((width, width), bf16),
            pltpu.VMEM((steps, width, width), bf16),
            pltpu.VMEM((steps, width, width), bf16),
            pltpu.SemaphoreType.DMA((1 + 2 * steps,)),
        ],
        compiler_params=pltpu.CompilerParams(vmem_limit_bytes=VMEM_BYTES),
        cost_estimate=cost(11),
        name="rows_back",
    )(
        ids, upstream, unit1, unit2, scale1, scale2, slope, *packs,
        own[0], other[0], own[1], other[1], own[2], other[2],
    )


def grads_kernel(layer, ids, f0, f1, k0, k1, *outs):
    part = f0.shape[1] // 12
    width = 2 * part
    ffh = k0.shape[1] - width

    def rows_of(at, count):
        return jnp.concatenate([f0[:, at : at + count], f1[:, at : at + count]], axis=0)

    def rows_at(at):
        at = pl.multiple_of(at, 128)
        return jnp.concatenate([f0[:, pl.ds(at, part)], f1[:, pl.ds(at, part)]], axis=0)

    pre = jnp.concatenate([k0[:, :ffh], k1[:, :ffh]], axis=0)
    branch = jnp.concatenate([k0[:, ffh : ffh + part], k1[:, ffh : ffh + part]], axis=0)
    attn = jnp.concatenate([k0[:, ffh + part :], k1[:, ffh + part :]], axis=0)
    if layer == 1:
        out = outs[0]
        few, many = width // 16, 8 * part // 16
        blocks = ffh // part
        for j in range(2):
            at = j * part
            up = tn(rows_of(at, part), pre).astype(bf16)
            last = tn(rows_of(width + at, part), attn).astype(bf16)
            for s in range(8):
                cut = slice(s * few, (s + 1) * few)
                for i in range(blocks):
                    out[8 * j + s, i * few : (i + 1) * few, :] = up[cut, i * part : (i + 1) * part]
                out[8 * j + s, blocks * few : (blocks + 1) * few, :] = last[cut]
        for j in range(8):
            at = j * part
            down = tn(rows_of(2 * width + at, part), branch).astype(bf16)
            for s in range(2):
                out[2 * j + s, (blocks + 1) * few :, :] = down[s * many : (s + 1) * many]
        return
    ua_o, ub_o, uk_o, da_o, db_o, dk_o = outs
    ua = ua_o.shape[1]
    small = dk_o.shape[1]
    sub = small // 2
    start = (1 - ids[5]) * part
    up = tn(rows_at(start), pre).astype(bf16)
    ua_o[...] = up[:, :ua]
    ub_o[:, : ffh - ua] = up[:, ua:]
    ub_o[:, ffh - ua :] = tn(rows_at(start + width), attn).astype(bf16)
    start = ids[5] * part
    uk_o[:, :ffh] = tn(rows_at(start), pre).astype(bf16)
    uk_o[:, ffh:] = tn(rows_at(start + width), attn).astype(bf16)
    for j in range(8):
        down = tn(rows_of(2 * width + 2 * small * j, 2 * small), branch).astype(bf16)
        for low in range(2):
            block = down[small * low : small * (low + 1)]
            share = 2 * j + low
            place, mine = (share // 8) * 4 + share % 4, ids[6] == (share // 4) % 2

            @pl.when(mine)
            def _(block=block, place=place):
                dk_o[place] = block

            @pl.when(jnp.logical_not(mine))
            def _(block=block, place=place):
                da_o[place] = block[:sub]
                db_o[place] = block[sub:]


def grads(layer, ids, fwd, fwd_other, keep, got):
    width = HEAD * 12
    ff = 2 * (keep.shape[1] - width)
    part = width // 2
    ua = 1024
    small = ff // 16
    vm = pl.BlockSpec(memory_space=pltpu.VMEM)
    shapes = [
        (part, ua),
        (part, ff // 2 + part - ua),
        (part, ff // 2 + part),
        (8, small // 2, part),
        (8, small // 2, part),
        (8, small, part),
    ]
    if layer == 1:
        shapes = [(16, (ff // 2 // part + 1) * width // 16 + ff // 16, part)]
    return pl.pallas_call(
        partial(grads_kernel, layer),
        out_shape=[jax.ShapeDtypeStruct(shape, bf16) for shape in shapes],
        in_specs=[pl.BlockSpec(memory_space=pltpu.SMEM)] + [vm] * 4,
        out_specs=[vm] * len(shapes),
        compiler_params=pltpu.CompilerParams(vmem_limit_bytes=VMEM_GRADS),
        cost_estimate=cost(5),
        name="grads",
    )(ids, fwd, fwd_other, keep, got)


def proj_grads_kernel(ids, u, d, ra_o, rb_o, rk_o):
    part = rk_o.shape[0]
    ra = ra_o.shape[1]
    rows = tn(u[:, pl.ds(pl.multiple_of((1 - ids[5]) * part, 128), part)], d[...]).astype(bf16)
    ra_o[...] = rows[:, :ra]
    rb_o[...] = rows[:, ra:]
    rk_o[...] = tn(u[:, pl.ds(pl.multiple_of(ids[5] * part, 128), part)], d[...]).astype(bf16)


def proj_grads(ids, u, d):
    part = u.shape[1] // 2
    cols = d.shape[1]
    vm = pl.BlockSpec(memory_space=pltpu.VMEM)
    return pl.pallas_call(
        proj_grads_kernel,
        out_shape=[jax.ShapeDtypeStruct((part, n), bf16) for n in (640, cols - 640, cols)],
        in_specs=[pl.BlockSpec(memory_space=pltpu.SMEM)] + [vm] * 2,
        out_specs=[vm] * 3,
        compiler_params=pltpu.CompilerParams(vmem_limit_bytes=VMEM_GRADS),
        cost_estimate=cost(4),
        name="proj_grads",
    )(ids, u, d)


def core_flip(v):
    return lax.ppermute(v, SECTION, [(0, 1), (1, 0)])


def seq_flip(v, by):
    return lax.ppermute(v, SEQ, [(i, i ^ by) for i in range(4)])


def core_x_flip(v):
    return lax.ppermute(v, BOTH, [(i, i ^ 5) for i in range(8)])


def dp_flip(v, by):
    return lax.ppermute(v, DP, [(i, i ^ by) for i in range(lax.axis_size(DP))])


def pick(which, options):
    result = options[-1]
    for i in range(len(options) - 2, -1, -1):
        result = jnp.where(which == i, options[i], result)
    return result


def to_section(v, layer):
    near = [(y_ * 4 + 2 * y_ + x_, layer * 4 + 2 * y_ + x_) for y_ in (0, 1) for x_ in (0, 1)]
    far = [
        ((1 - y_) * 4 + 2 * y_ + x_, layer * 4 + 2 * (1 - y_) + x_) for y_ in (0, 1) for x_ in (0, 1)
    ]
    return lax.ppermute(v, BOTH, near), lax.ppermute(v, BOTH, far)


def by_micro(first, lower, upper, y):
    mine = jnp.where(first, lower[0], upper[0])
    away = jnp.where(first, lower[1], upper[1])
    return jnp.where(y == 0, jnp.stack([mine, away]), jnp.stack([away, mine]))


def two_chips(
    layer_in, cotangent, masked_rows, global_positions, local_weight, local_bias, global_weight,
    global_bias, out_weight, out_bias, norm_gain, norm_shift, up_weight, up_bias, down_weight,
    down_bias,
):
    c = lax.axis_index(SECTION)
    q = lax.axis_index(SEQ)
    z = lax.axis_index(DP)
    dp = lax.axis_size(DP)
    y, x = q // 2, q % 2
    g = 2 * c + x
    g_other = 2 * (1 - c) + x
    rows, width = layer_in.shape[2:]
    hw = width // 4
    ff = up_weight.shape[2]
    heads = hw // HEAD
    half_rows = rows // 2
    same = c == y
    first = c == 0

    block = layer_in[:, 0]

    def half_of(micro):
        return lax.dynamic_slice(block, (micro, c * half_rows, 0), (1, half_rows, width))[0]

    mine_part, away_part = half_of(y), half_of(1 - y)
    got = [seq_flip(mine_part, 1), seq_flip(away_part, 2), seq_flip(away_part, 3)]

    cot = cotangent[:, 0]
    marks = masked_rows[:, 0]

    def of_micro(v, micro):
        return lax.dynamic_index_in_dim(v, micro, 0, keepdims=False)

    cot_away = seq_flip(of_micro(cot, 1 - y), 2)
    marks_away = seq_flip(of_micro(marks, 1 - y), 2)

    ids = jnp.stack([g, g_other, 2 * c + 1 - x, 2 * (1 - c) + 1 - x, c, y, x, z]).astype(jnp.int32)
    ids, _ = lax.optimization_barrier((ids, (mine_part, away_part)))
    w_own, w_send, pack = prepare(
        ids,
        local_weight[0],
        global_weight[0],
        (local_bias[0], global_bias[0], out_bias, norm_gain[0], norm_shift[0], down_bias, up_bias),
    )
    own = (out_weight[0], up_weight[0], down_weight[0])
    (w_own, w_send, pack), got = lax.optimization_barrier(((w_own, w_send, pack), got))
    weights = (w_own, core_flip(w_send))
    packs = (pack, core_flip(pack))
    positions = of_micro(global_positions[:, 0], y)
    prow = positions[None, :]
    pcol = positions[:, None]
    parts = [block] + got + [core_flip(v) for v in got]
    own_late, _ = lax.optimization_barrier((own, (parts, weights, packs)))
    other = tuple(core_flip(w) for w in own_late)

    def exchange(pieces):
        return [pieces[0], core_flip(pieces[1]), seq_flip(pieces[2], 1), core_x_flip(pieces[3])]

    saved = []
    for layer in range(2):
        ctx, u_all, u_own, kept = attend(layer, ids, parts, weights, packs, prow, pcol)
        pieces = exchange(ctx)
        if layer == 1:
            pieces, out0 = lax.optimization_barrier((pieces, to_section(saved_low, 0)))
        res = rows_forward(layer, ids, pieces, u_own, packs, own, other)
        y_low, fwd, slope, unit1, unit2, scale1, scale2 = res
        if layer == 0:
            across = seq_flip(y_low, 1)
            across, (cot_away, marks_away, fwd_other) = lax.optimization_barrier(
                (across, (cot_away, marks_away, core_flip(fwd)))
            )
            parts = [y_low, core_flip(y_low), across, core_flip(across)]
            saved_low = y_low
        else:
            fwd_other = core_flip(fwd)
        saved.append((u_all, kept, fwd, fwd_other, (unit1, unit2, scale1, scale2, slope)))

    cot_rows = jnp.where(same, of_micro(cot, y), cot_away)
    cot_marks = jnp.where(same, of_micro(marks, y), marks_away)
    row_hit = (g * rows + jnp.arange(rows))[:, None] == cot_marks[None, :]
    upstream = nn(row_hit.astype(bf16), cot_rows).astype(bf16)

    flip_x = partial(seq_flip, by=1)
    flip_y = partial(seq_flip, by=2)
    flip_z1 = partial(dp_flip, by=1)
    flip_z2 = partial(dp_flip, by=2)
    low_z, high_z = z % 2, z // 2

    def after(value, others):
        return lax.optimization_barrier((value, others))

    def cut(value, axis, bit):
        return of_axis(value, axis, 1 - bit).astype(bf16), of_axis(value, axis, bit)

    def of_axis(value, axis, index):
        return lax.dynamic_index_in_dim(value, index, axis, keepdims=False)

    def plus(keep, got):
        return keep.astype(f32) + got.astype(f32)

    def bias_rows(small, bias):
        placed = jnp.concatenate([jnp.where(g == i, bias, 0.0) for i in range(4)], axis=1)
        return jnp.concatenate([small[:10], placed], axis=0)

    def inward(partials):
        low = [core_flip(partials[1]), core_flip(partials[3])]
        return plus(partials[0], low[0]), plus(partials[2], low[1]).astype(bf16)

    ua = 1024
    share_w = width // (4 * dp)
    share_f = ff // (4 * dp)
    sub = share_f // 2
    part = width // 2

    u_all, kept, fwd, fwd_other, row_kept = saved[1]
    res = rows_back(1, ids, upstream, row_kept, packs, own, other)
    res, fwd_other = after(res, fwd_other)
    d_first, pieces, (keep, send, small) = res[0], exchange(res[1:5]), res[5:]
    gr = grads(1, ids, fwd, fwd_other, keep, core_flip(send))
    pieces, gr = after(pieces, gr)
    ffn1 = lax.psum_scatter(gr[0], SEQ, scatter_dimension=0, tiled=True)
    res = attend_back(1, ids, pieces, kept, prow, pcol, weights)
    d_all, bias, partials = res
    small1 = bias_rows(small, bias)
    summed, send = inward(partials)
    across = flip_x(send)
    d_all, send = after(d_all, send)
    gr = proj_grads(ids, u_all, d_all)
    across, gr = after(across, gr)
    r1a, r1b, r1k = gr
    d_upper = (d_first + summed + across.astype(f32)).astype(bf16)

    got_r1a = flip_y(r1a)
    u_all, kept, fwd, fwd_other, row_kept = saved[0]
    res = rows_back(0, ids, d_upper, row_kept, packs, own, other)
    res, got_r1a = after(res, got_r1a)
    d_first, pieces, (keep, send, small) = res[0], exchange(res[1:5]), res[5:]
    got_r1b = flip_y(r1b)
    gr = grads(0, ids, fwd, fwd_other, keep, core_flip(send))
    pieces, (gr, ffn1) = after(pieces, (gr, ffn1))
    ffn1 = lax.psum_scatter(ffn1, DP, scatter_dimension=0, tiled=True)[0]
    u0a, u0b, u0k, d0a, d0b, d0k = gr
    got_u0a, got_d0a, got_u0b, got_d0b = flip_y(u0a), flip_x(d0a), flip_y(u0b), flip_x(d0b)
    res = attend_back(0, ids, pieces, kept, prow, pcol, weights)
    (res, y_low, d_upper), (got_u0a, got_d0a, got_r1b) = after(
        (res, y_low, d_upper), (got_u0a, got_d0a, got_r1b)
    )
    d_all, bias, partials = res
    small0 = bias_rows(small, bias)

    def step(flights):
        sends = lax.optimization_barrier([send for _, send in flights])
        return [flip(send) for (flip, _), send in zip(flights, sends)]

    def end(got, *more):
        return lax.optimization_barrier((got, more))

    swapped = partial(jnp.where, first)
    small_keep, small_send = swapped(small0, small1), swapped(small1, small0)
    r1 = plus(r1k, jnp.concatenate([got_r1a, got_r1b], axis=1))
    r1_send, r1_keep = cut(r1.reshape(2, 2, 2, share_w, -1), 2, low_z)
    small = small_keep + core_flip(small_send)
    got = step([(flip_z1, r1_send), (flip_x, small)])
    r0a, r0b, r0k = proj_grads(ids, u_all, d_all)
    summed, d_send = inward(partials)
    out1 = to_section(y_low, 1)
    got, ends = end(got, got_u0b, got_d0b, (r0a, r0b, r0k), d_send, out1)
    got_u0b, got_d0b, gr, d_send, out1 = ends
    r0a, r0b, r0k = gr

    u0 = plus(u0k, jnp.concatenate([got_u0a, got_u0b], axis=1)).astype(bf16)
    u0_send, u0_keep = cut(u0.reshape(2, 2, 2, share_w, -1), 2, low_z)
    r1_send, r1_keep = cut(plus(r1_keep, got[0]).astype(bf16), 1, high_z)
    small = small + got[1]
    got = step([(flip_z1, u0_send), (flip_y, r0a), (flip_y, r0b), (flip_z2, r1_send), (flip_y, small), (flip_x, d_send)])
    d0 = plus(d0k, jnp.concatenate([got_d0a, got_d0b], axis=1)).astype(bf16)
    d0_send, d0_keep = cut(d0.reshape(2, 2, 2, share_f, part), 0, y)
    got, ends = end(got, d0_send)
    d0_send = ends[0]

    u0_send, u0_keep = cut(plus(u0_keep, got[0]).astype(bf16), 1, high_z)
    r0 = plus(r0k, jnp.concatenate([got[1], got[2]], axis=1)).astype(bf16)
    r0_send, r0_keep = cut(r0.reshape(2, 2, 2, share_w, -1), 2, low_z)
    r1 = plus(r1_keep, got[3]).astype(bf16)
    small = small + got[4]
    d_lower = (d_first + summed + got[5].astype(f32)).astype(bf16)
    got = step([(flip_z2, u0_send), (flip_y, d0_send), (flip_z1, r0_send), (flip_z1, small)])
    in1 = to_section(d_upper, 1)
    got, in1 = end(got, in1)
    near1, far1 = in1[0]

    u0_send, u0_keep = cut(plus(u0_keep, got[0]).astype(bf16), 0, x)
    d0_send, d0_keep = cut(plus(d0_keep, got[1]).astype(bf16), 1, low_z)
    r0_send, r0_keep = cut(plus(r0_keep, got[2]).astype(bf16), 1, high_z)
    small = small + got[3]
    got = step([(flip_z2, r0_send), (flip_x, u0_send), (flip_z1, d0_send), (flip_z2, small)])
    near0, far0 = to_section(d_lower, 0)
    got, ends = end(got, near0, far0, ffn1)
    near0, far0, ffn1 = ends

    few = 5 * share_w
    one1 = jnp.concatenate([ffn1[i * share_w : (i + 1) * share_w] for i in range(5)], axis=1)
    one0, one1 = plus(u0_keep, got[1]), one1.astype(f32)
    d0_send, d0_keep = cut(plus(d0_keep, got[2]).astype(bf16), 0, high_z)
    r0 = plus(r0_keep, got[0]).astype(bf16)
    small = small + got[3]
    r_send, r_keep = cut(jnp.stack([r0, r1]), 1, x)
    one_send, one_keep = swapped(one1, one0), swapped(one0, one1)
    got = step([(flip_z2, d0_send), (flip_x, r_send), (core_flip, one_send)])
    got = end(got)[0]
    two0, two1 = plus(d0_keep, got[0]), ffn1[few:].astype(f32)
    one_got = got[2]
    attn_shares = [jnp.stack([r_keep[i], got[1][i]]) for i in range(2)]

    def swap(pair):
        return swapped(pair[0], pair[1]), core_flip(swapped(pair[1], pair[0]))

    def side_by_side(keep, got):
        return jnp.where(
            first, jnp.concatenate([keep, got], axis=-1), jnp.concatenate([got, keep], axis=-1)
        )

    grad_up = side_by_side(one_keep[:, : ff // 2], one_got[:, : ff // 2])
    grad_out = side_by_side(one_keep[:, ff // 2 :], one_got[:, ff // 2 :])
    grad_down = side_by_side(*swap([two0, two1]))

    att_keep, att_got = swap(attn_shares)
    by_group = []
    for group in range(4):
        gc, gx = group // 2, group % 2
        held = jnp.where(c == gc, att_keep, att_got)
        by_group.append(jnp.where(x == gx, held[0], held[1]).astype(f32))

    def assembled(kinds):
        return jnp.concatenate(
            [by_group[group][:, k * hw : (k + 1) * hw] for k in kinds for group in range(4)], axis=1
        )

    grad_local = assembled((0, 1, 2))
    grad_glob = assembled((5, 3, 4))

    at = q * dp + z
    piece = partial(lax.dynamic_slice_in_dim, axis=0)
    outs = (
        grad_local,
        jnp.stack([small[10], small[11]]),
        grad_glob,
        jnp.stack([small[12], small[13]]),
        grad_out,
        piece(small[4], at * share_w, share_w),
        jnp.stack([small[2], small[0]]),
        jnp.stack([small[3], small[1]]),
        grad_up,
        piece(small[6:10].reshape(ff), at * (ff // (4 * dp)), ff // (4 * dp)),
        grad_down,
        piece(small[5], at * share_w, share_w),
    )
    layer_outputs = by_micro(first, out0, out1, y)
    in_grads = by_micro(first, (near0, far0), (near1, far1), y)
    return (layer_outputs[None, :, None], in_grads[None, :, None]) + tuple(o[None] for o in outs)


def fits_two_chips(mesh, layer_in):
    sizes = dict(mesh.shape)
    micro, _, length, width = layer_in.shape
    dp = sizes[DP]
    return (
        sizes[SECTION] == 2
        and sizes[SEQ] == 4
        and micro == 2
        and dp == 4
        and length == 4 * HALF
        and width == 12 * HEAD
    )


def solution(mesh):
    in_specs = (
        P(None, DP, SEQ, None),
        P(None, DP, SEQ, None),
        P(None, DP, SEQ),
        P(None, DP, None),
        P(SECTION, None, None),
        P(SECTION, None, None),
        P(SECTION, None, None),
        P(SECTION, None, None),
        P(SECTION, None, None),
        P(SECTION, None),
        P(SECTION, None, None),
        P(SECTION, None, None),
        P(SECTION, None, None),
        P(SECTION, None),
        P(SECTION, None, None),
        P(SECTION, None),
    )
    out_specs = (
        P(SECTION, None, DP, SEQ, None),
        P(SECTION, None, DP, SEQ, None),
        P(SECTION, (SEQ, DP), None),
        P(SECTION, None, None),
        P(SECTION, (SEQ, DP), None),
        P(SECTION, None, None),
        P(SECTION, (SEQ, DP), None),
        P(SECTION, (SEQ, DP)),
        P(SECTION, None, None),
        P(SECTION, None, None),
        P(SECTION, (SEQ, DP), None),
        P(SECTION, (SEQ, DP)),
        P(SECTION, (SEQ, DP), None),
        P(SECTION, (SEQ, DP)),
    )

    def run(layer_in, *rest):
        body = two_chips if fits_two_chips(mesh, layer_in) else on_device
        return jax.shard_map(
            body, mesh=mesh, in_specs=in_specs, out_specs=out_specs, check_vma=False
        )(layer_in, *rest)

    return run
```

```python
from functools import partial
from types import SimpleNamespace

import jax
import jax.numpy as jnp
import numpy as np
from jax import lax
from jax.experimental import pallas as pl
from jax.experimental.pallas import tpu as pltpu
from jax.sharding import PartitionSpec as P

HEAD = 64
HALF = 256

SECTION, SEQ, DP = "section", "seq", "dp"
BOTH = (SECTION, SEQ)


far_below = -1e30
norm_eps = 1e-05


def padded(block, sides, width):
    for axis, dim in sides:
        count = lax.axis_size(axis)
        forward = [(i, i + 1) for i in range(count - 1)]
        backward = [(target, source) for source, target in forward]
        low = lax.ppermute(
            lax.slice_in_dim(block, block.shape[dim] - width, None, axis=dim), axis, forward
        )
        high = lax.ppermute(lax.slice_in_dim(block, 0, width, axis=dim), axis, backward)
        block = jnp.concatenate([low, block, high], axis=dim)
    return block


def joined(value, axis, join):
    pieces = jax.tree.map(lambda part: lax.all_gather(part, axis), value)
    head = jax.tree.map(lambda part: part[0], pieces)
    tail = jax.tree.map(lambda part: part[1:], pieces)
    running, _ = lax.scan(lambda running, piece: (join(running, piece), None), head, tail)
    return running


def shifted(shard, axis, by):
    length = lax.axis_size(axis)
    pairs = [(i, i + by) for i in range(length) if 0 <= i + by < length]
    return lax.ppermute(shard, axis, pairs)


def band_mask(first_row, row_count, reach_rows, length, positions, dilated):
    rows_at = first_row + jnp.arange(row_count)
    cols_at = first_row - reach_rows + jnp.arange(row_count + 2 * reach_rows)
    offset = cols_at[None, :] - rows_at[:, None]
    inside = (jnp.abs(offset) <= reach_rows) & (cols_at >= 0)[None, :] & (cols_at < length)[None, :]
    plain_key = jnp.logical_not(jnp.any(cols_at[:, None] == positions[None, :], axis=1))
    usable = inside & plain_key[None, :]
    even_gap = offset % 2 == 0
    return usable[None, :, :] & (jnp.logical_not(dilated)[:, None, None] | even_gap[None, :, :])


def layer_norm(values, gain_row, shift_row):
    center = values - jnp.mean(values, axis=-1, keepdims=True)
    scaled = lax.rsqrt(jnp.mean(center * center, axis=-1, keepdims=True) + norm_eps)
    unit_rows = center * scaled
    return (unit_rows * gain_row + shift_row, unit_rows, scaled)


def norm_back(unit_rows, scaled, gain_row, upstream):
    d_unit = upstream * gain_row
    inward = scaled * (
        d_unit
        - jnp.mean(d_unit, axis=-1, keepdims=True)
        - unit_rows * jnp.mean(d_unit * unit_rows, axis=-1, keepdims=True)
    )
    return (inward, jnp.sum(upstream * unit_rows, axis=0), jnp.sum(upstream, axis=0))


def join_stats(first_pair, second_pair):
    top_value = jnp.maximum(first_pair[0], second_pair[0])
    merged = first_pair[1] * jnp.exp(first_pair[0] - top_value) + second_pair[1] * jnp.exp(
        second_pair[0] - top_value
    )
    return (top_value, merged)


def forward_layer(source, positions, weights, first_row, length, dilated, active):
    local_w, local_b, glob_w, glob_b, out_w, out_b, gains, shifts, up_w, up_b, down_w, down_b = (
        weights
    )
    row_count = source.shape[0]
    model_width = source.shape[1]
    ff_width = up_w.shape[1]
    head_count = dilated.shape[0]
    head_size = model_width // head_count
    glob_count = positions.shape[0]
    score_scale = head_size ** (-0.5)
    owner_hit = (first_row + jnp.arange(row_count))[:, None] == positions[None, :]
    owner_low = owner_hit.astype(jnp.bfloat16)
    owner_full = owner_hit.astype(jnp.float32)
    is_global = jnp.any(owner_hit, axis=1)
    picked = jnp.einsum("cg,cd->gd", owner_low, source, preferred_element_type=jnp.float32)
    global_rows = lax.psum(picked.astype(jnp.bfloat16), SEQ)
    proj = jnp.dot(source, local_w, preferred_element_type=jnp.float32)
    queries = (proj[:, :model_width] + local_b[0]).astype(jnp.bfloat16)
    keys_low = proj[:, model_width : 2 * model_width].astype(jnp.bfloat16)
    values_low = (proj[:, 2 * model_width :] + local_b[1]).astype(jnp.bfloat16)
    gproj = jnp.dot(source, glob_w[:, model_width:], preferred_element_type=jnp.float32)
    gkeys = gproj[:, :model_width].astype(jnp.bfloat16)
    gvalues = (gproj[:, model_width:] + glob_b[1]).astype(jnp.bfloat16)
    gqueries = (
        jnp.dot(global_rows, glob_w[:, :model_width], preferred_element_type=jnp.float32)
        + glob_b[0]
    ).astype(jnp.bfloat16)
    side_proj = jnp.dot(global_rows, local_w[:, model_width:], preferred_element_type=jnp.float32)
    extra_keys = (
        side_proj[:, :model_width].astype(jnp.bfloat16).reshape(glob_count, head_count, head_size)
    )
    extra_values = (
        (side_proj[:, model_width:] + local_b[1])
        .astype(jnp.bfloat16)
        .reshape(glob_count, head_count, head_size)
    )
    key_value = jnp.concatenate([keys_low, values_low], axis=1)
    widened = padded(key_value, ((SEQ, 0),), HALF)
    reach_rows = (widened.shape[0] - row_count) // 2
    wide_keys = widened[:, :model_width].reshape(-1, head_count, head_size)
    wide_values = widened[:, model_width:].reshape(-1, head_count, head_size)
    allowed = band_mask(first_row, row_count, reach_rows, length, positions, dilated)
    queries_h = queries.reshape(row_count, head_count, head_size)
    band_score = (
        jnp.einsum("qhd,khd->hqk", queries_h, wide_keys, preferred_element_type=jnp.float32)
        * score_scale
    )
    band_score = jnp.where(allowed, band_score, far_below)
    toward = (
        jnp.einsum("qhd,ghd->hqg", queries_h, extra_keys, preferred_element_type=jnp.float32)
        * score_scale
    )
    peak_score = jnp.maximum(jnp.max(band_score, axis=-1), jnp.max(toward, axis=-1))[..., None]
    band_exp = jnp.exp(band_score - peak_score)
    toward_exp = jnp.exp(toward - peak_score)
    totals = jnp.sum(band_exp, axis=-1, keepdims=True) + jnp.sum(toward_exp, axis=-1, keepdims=True)
    band_full = band_exp / totals
    toward_full = toward_exp / totals
    band_prob = band_full.astype(jnp.bfloat16)
    toward_prob = toward_full.astype(jnp.bfloat16)
    local_ctx = jnp.einsum(
        "hqk,khd->qhd", band_prob, wide_values, preferred_element_type=jnp.float32
    ) + jnp.einsum("hqg,ghd->qhd", toward_prob, extra_values, preferred_element_type=jnp.float32)
    gqueries_h = gqueries.reshape(glob_count, head_count, head_size)
    gkeys_h = gkeys.reshape(row_count, head_count, head_size)
    gvalues_h = gvalues.reshape(row_count, head_count, head_size)
    spread = (
        jnp.einsum("ghd,khd->hgk", gqueries_h, gkeys_h, preferred_element_type=jnp.float32)
        * score_scale
    )
    part_peak = jnp.max(spread, axis=-1)
    part_total = jnp.sum(jnp.exp(spread - part_peak[..., None]), axis=-1)
    glob_peak, glob_total = joined((part_peak, part_total), SEQ, join_stats)
    glob_full = jnp.exp(spread - glob_peak[..., None]) / glob_total[..., None]
    glob_prob = glob_full.astype(jnp.bfloat16)
    part_ctx = jnp.einsum("hgk,khd->ghd", glob_prob, gvalues_h, preferred_element_type=jnp.float32)
    glob_ctx = lax.psum(part_ctx.reshape(glob_count, model_width), SEQ)
    placed_ctx = jnp.dot(owner_full, glob_ctx, precision=lax.Precision.HIGHEST)
    context = jnp.where(is_global[:, None], placed_ctx, local_ctx.reshape(row_count, model_width))
    context_low = context.astype(jnp.bfloat16)
    attn_out = jnp.dot(context_low, out_w, preferred_element_type=jnp.float32) + out_b
    mixed, unit_one, scale_one = layer_norm(
        source.astype(jnp.float32) + attn_out, gains[0], shifts[0]
    )

    def feed_forward(hidden_in):
        pre_act = (
            jnp.dot(hidden_in.astype(jnp.bfloat16), up_w, preferred_element_type=jnp.float32) + up_b
        )
        lifted = jax.nn.gelu(pre_act, approximate=False).astype(jnp.bfloat16)
        return (
            pre_act,
            lifted,
            jnp.dot(lifted, down_w, preferred_element_type=jnp.float32) + down_b,
        )

    def skip_block(hidden_in):
        return (
            jnp.zeros((row_count, ff_width), jnp.float32),
            jnp.zeros((row_count, ff_width), jnp.bfloat16),
            jnp.zeros((row_count, model_width), jnp.float32),
        )

    pre_act, activated, branch = lax.cond(active, feed_forward, skip_block, mixed)
    result, unit_two, scale_two = layer_norm(mixed + branch, gains[1], shifts[1])
    return SimpleNamespace(
        source=source,
        owner_low=owner_low,
        owner_full=owner_full,
        is_global=is_global,
        queries_h=queries_h,
        wide_keys=wide_keys,
        wide_values=wide_values,
        extra_keys=extra_keys,
        extra_values=extra_values,
        band_full=band_full,
        toward_full=toward_full,
        band_prob=band_prob,
        toward_prob=toward_prob,
        gqueries_h=gqueries_h,
        gkeys_h=gkeys_h,
        gvalues_h=gvalues_h,
        glob_full=glob_full,
        glob_prob=glob_prob,
        context_low=context_low,
        unit_one=unit_one,
        scale_one=scale_one,
        mixed=mixed,
        pre_act=pre_act,
        activated=activated,
        unit_two=unit_two,
        scale_two=scale_two,
        result=result,
        reach_rows=reach_rows,
        score_scale=score_scale,
    )


def ffn_back(kept_values, weights, upstream, active):
    local_w, local_b, glob_w, glob_b, out_w, out_b, gains, shifts, up_w, up_b, down_w, down_b = (
        weights
    )
    d_second, gain_two, shift_two = norm_back(
        kept_values.unit_two, kept_values.scale_two, gains[1], upstream
    )
    d_branch = d_second.astype(jnp.bfloat16)

    def ffn_work(operands):
        pre_act, d_out = operands
        d_lifted = jnp.einsum("cd,fd->cf", d_out, down_w, preferred_element_type=jnp.float32)
        gelu_vals, gelu_back = jax.vjp(partial(jax.nn.gelu, approximate=False), pre_act)
        d_pre = gelu_back(d_lifted)[0].astype(jnp.bfloat16)
        d_hidden = jnp.einsum("cf,df->cd", d_pre, up_w, preferred_element_type=jnp.float32)
        return (d_hidden, d_pre)

    def ffn_spare(operands):
        return (
            jnp.zeros(upstream.shape, jnp.float32),
            jnp.zeros((upstream.shape[0], up_w.shape[1]), jnp.bfloat16),
        )

    d_hidden, d_pre = lax.cond(active, ffn_work, ffn_spare, (kept_values.pre_act, d_branch))
    return (d_second + d_hidden, d_pre, d_branch, (gain_two, shift_two))


def attention_back(kept_values, weights, d_mixed):
    local_w, local_b, glob_w, glob_b, out_w, out_b, gains, shifts, up_w, up_b, down_w, down_b = (
        weights
    )
    row_count, model_width = kept_values.source.shape
    queries_h = kept_values.queries_h
    head_count, head_size = (queries_h.shape[1], queries_h.shape[2])
    glob_count = kept_values.owner_full.shape[1]
    reach_rows = kept_values.reach_rows
    score_scale = kept_values.score_scale
    d_first, gain_one, shift_one = norm_back(
        kept_values.unit_one, kept_values.scale_one, gains[0], d_mixed
    )
    d_attn = d_first.astype(jnp.bfloat16)
    d_context = jnp.einsum("ce,de->cd", d_attn, out_w, preferred_element_type=jnp.float32).astype(
        jnp.bfloat16
    )
    glob_part = jnp.einsum(
        "cg,cd->gd", kept_values.owner_low, d_context, preferred_element_type=jnp.float32
    )
    d_glob_ctx = lax.psum(glob_part.astype(jnp.bfloat16), SEQ)
    d_local = jnp.where(kept_values.is_global[:, None], jnp.zeros_like(d_context), d_context)
    d_local = d_local.reshape(row_count, head_count, head_size)
    band_full = kept_values.band_full
    toward_full = kept_values.toward_full
    d_band = jnp.einsum(
        "qhd,khd->hqk", d_local, kept_values.wide_values, preferred_element_type=jnp.float32
    )
    d_toward = jnp.einsum(
        "qhd,ghd->hqg", d_local, kept_values.extra_values, preferred_element_type=jnp.float32
    )
    inner_sum = jnp.sum(band_full * d_band, axis=-1) + jnp.sum(toward_full * d_toward, axis=-1)
    grad_band = (band_full * (d_band - inner_sum[..., None])).astype(jnp.bfloat16)
    grad_toward = (toward_full * (d_toward - inner_sum[..., None])).astype(jnp.bfloat16)
    d_queries = (
        jnp.einsum(
            "hqk,khd->qhd", grad_band, kept_values.wide_keys, preferred_element_type=jnp.float32
        )
        + jnp.einsum(
            "hqg,ghd->qhd",
            grad_toward,
            kept_values.extra_keys,
            preferred_element_type=jnp.float32,
        )
    ) * score_scale
    d_wide_keys = (
        jnp.einsum("hqk,qhd->khd", grad_band, queries_h, preferred_element_type=jnp.float32)
        * score_scale
    )
    d_wide_values = jnp.einsum(
        "hqk,qhd->khd", kept_values.band_prob, d_local, preferred_element_type=jnp.float32
    )
    d_extra_keys = (
        jnp.einsum("hqg,qhd->ghd", grad_toward, queries_h, preferred_element_type=jnp.float32)
        * score_scale
    )
    d_extra_values = jnp.einsum(
        "hqg,qhd->ghd", kept_values.toward_prob, d_local, preferred_element_type=jnp.float32
    )
    glob_full = kept_values.glob_full
    d_glob_h = d_glob_ctx.reshape(glob_count, head_count, head_size)
    d_spread = jnp.einsum(
        "ghd,khd->hgk", d_glob_h, kept_values.gvalues_h, preferred_element_type=jnp.float32
    )
    part_inner = jnp.sum(glob_full * d_spread, axis=-1)
    glob_inner, sum_extra_keys, sum_extra_values = (
        lax.psum(part_inner.astype(jnp.bfloat16), SEQ).astype(jnp.float32),
        lax.psum(d_extra_keys.reshape(glob_count, model_width).astype(jnp.bfloat16), SEQ).astype(
            jnp.float32
        ),
        lax.psum(
            d_extra_values.reshape(glob_count, model_width).astype(jnp.bfloat16), SEQ
        ).astype(jnp.float32),
    )
    grad_spread = (glob_full * (d_spread - glob_inner[..., None])).astype(jnp.bfloat16)
    part_query = (
        jnp.einsum(
            "hgk,khd->ghd", grad_spread, kept_values.gkeys_h, preferred_element_type=jnp.float32
        )
        * score_scale
    )
    d_gkeys = (
        jnp.einsum(
            "hgk,ghd->khd",
            grad_spread,
            kept_values.gqueries_h,
            preferred_element_type=jnp.float32,
        )
        * score_scale
    )
    d_gvalues = jnp.einsum(
        "hgk,ghd->khd", kept_values.glob_prob, d_glob_h, preferred_element_type=jnp.float32
    )
    d_gqueries = lax.psum(
        part_query.reshape(glob_count, model_width).astype(jnp.bfloat16), SEQ
    ).astype(jnp.float32)
    d_wide = jnp.concatenate(
        [d_wide_keys.reshape(-1, model_width), d_wide_values.reshape(-1, model_width)], axis=1
    )
    rim_grads = jnp.concatenate([d_wide[:reach_rows], d_wide[reach_rows + row_count :]], axis=0)
    incoming = padded(rim_grads.astype(jnp.bfloat16), ((SEQ, 0),), HALF).astype(rim_grads.dtype)
    own_part = (
        d_wide[reach_rows : reach_rows + row_count]
        + incoming[:reach_rows]
        + incoming[3 * reach_rows :]
    )
    owner_full = kept_values.owner_full
    d_keys_low = (
        own_part[:, :model_width]
        + jnp.dot(owner_full, sum_extra_keys, precision=lax.Precision.HIGHEST)
    ).astype(jnp.bfloat16)
    d_values_low = (
        own_part[:, model_width:]
        + jnp.dot(owner_full, sum_extra_values, precision=lax.Precision.HIGHEST)
    ).astype(jnp.bfloat16)
    d_queries_low = d_queries.reshape(row_count, model_width).astype(jnp.bfloat16)
    d_proj = jnp.concatenate([d_queries_low, d_keys_low, d_values_low], axis=1)
    d_gq_rows = jnp.dot(owner_full, d_gqueries, precision=lax.Precision.HIGHEST).astype(
        jnp.bfloat16
    )
    d_gproj = jnp.concatenate(
        [
            d_gq_rows,
            d_gkeys.reshape(row_count, model_width).astype(jnp.bfloat16),
            d_gvalues.reshape(row_count, model_width).astype(jnp.bfloat16),
        ],
        axis=1,
    )
    d_source = (
        d_first
        + jnp.einsum("ce,de->cd", d_proj, local_w, preferred_element_type=jnp.float32)
        + jnp.einsum("ce,de->cd", d_gproj, glob_w, preferred_element_type=jnp.float32)
    )
    return (d_source, d_proj, d_gproj, d_attn, (gain_one, shift_one))


def ffn_terms(mixed_buf, pre_buf, act_buf, branch_buf, count):
    return (
        jnp.einsum(
            "mcd,mcf->df", mixed_buf[:count], pre_buf[:count], preferred_element_type=jnp.float32
        ),
        jnp.sum(pre_buf[:count].astype(jnp.float32), axis=(0, 1)),
        jnp.einsum(
            "mcf,mcd->fd", act_buf[:count], branch_buf[:count], preferred_element_type=jnp.float32
        ),
        jnp.sum(branch_buf[:count].astype(jnp.float32), axis=(0, 1)),
    )


def on_device(
    layer_in,
    cotangent,
    masked_rows,
    global_positions,
    local_weight,
    local_bias,
    global_weight,
    global_bias,
    out_weight,
    out_bias,
    norm_gain,
    norm_shift,
    up_weight,
    up_bias,
    down_weight,
    down_bias,
):
    weights = (
        local_weight[0],
        local_bias[0],
        global_weight[0],
        global_bias[0],
        out_weight[0],
        out_bias[0],
        norm_gain[0],
        norm_shift[0],
        up_weight[0],
        up_bias[0],
        down_weight[0],
        down_bias[0],
    )
    section_index = lax.axis_index(SECTION)
    seq_index = lax.axis_index(SEQ)
    micro_count = layer_in.shape[0]
    row_count = layer_in.shape[2]
    model_width = layer_in.shape[3]
    ff_width = up_weight.shape[2]
    length = row_count * lax.axis_size(SEQ)
    first_row = seq_index * row_count
    head_count = model_width // HEAD
    dilated = (jnp.arange(head_count) >= head_count - 2) & (section_index == 1)
    kept_inputs = jnp.zeros((micro_count, row_count, model_width), jnp.bfloat16)
    outputs = jnp.zeros_like(kept_inputs)
    arrived = jnp.zeros((row_count, model_width), jnp.bfloat16)
    for step_index in range(micro_count + 1):
        micro_index = step_index - section_index
        in_range = (micro_index >= 0) & (micro_index < micro_count)
        slot_index = jnp.clip(micro_index, 0, micro_count - 1)
        fresh = lax.dynamic_index_in_dim(layer_in, slot_index, 0, keepdims=False)[0]
        source = jnp.where(section_index == 0, fresh, arrived)
        positions = lax.dynamic_index_in_dim(global_positions, slot_index, 0, keepdims=False)[0]
        kept_values = forward_layer(
            source, positions, weights, first_row, length, dilated, in_range
        )
        result = kept_values.result.astype(jnp.bfloat16)
        kept_inputs = jnp.where(
            in_range,
            lax.dynamic_update_index_in_dim(kept_inputs, source, slot_index, 0),
            kept_inputs,
        )
        outputs = jnp.where(
            in_range, lax.dynamic_update_index_in_dim(outputs, result, slot_index, 0), outputs
        )
        if step_index < micro_count:
            arrived = shifted(result, SECTION, 1)
    slots = micro_count + 1
    proj_buf = jnp.zeros((slots, row_count, 3 * model_width), jnp.bfloat16)
    gproj_buf = jnp.zeros_like(proj_buf)
    ctx_buf = jnp.zeros((slots, row_count, model_width), jnp.bfloat16)
    attn_buf = jnp.zeros_like(ctx_buf)
    mixed_buf = jnp.zeros_like(ctx_buf)
    branch_buf = jnp.zeros_like(ctx_buf)
    pre_buf = jnp.zeros((slots, row_count, ff_width), jnp.bfloat16)
    act_buf = jnp.zeros_like(pre_buf)
    gain_total = jnp.zeros((2, model_width), jnp.float32)
    shift_total = jnp.zeros((2, model_width), jnp.float32)
    back_arrived = jnp.zeros((row_count, model_width), jnp.bfloat16)
    in_grads = jnp.zeros_like(kept_inputs)
    for step_index in range(micro_count + 1):
        micro_index = step_index - 1 + section_index
        in_range = (micro_index >= 0) & (micro_index < micro_count)
        slot_index = jnp.clip(micro_index, 0, micro_count - 1)
        store = jnp.where(in_range, micro_index, micro_count)
        source = lax.dynamic_index_in_dim(kept_inputs, slot_index, 0, keepdims=False)
        positions = lax.dynamic_index_in_dim(global_positions, slot_index, 0, keepdims=False)[0]
        picked_rows = lax.dynamic_index_in_dim(masked_rows, slot_index, 0, keepdims=False)[0]
        picked_grads = lax.dynamic_index_in_dim(cotangent, slot_index, 0, keepdims=False)[0]
        row_hit = ((first_row + jnp.arange(row_count))[:, None] == picked_rows[None, :]).astype(
            jnp.bfloat16
        )
        placed = jnp.dot(row_hit, picked_grads, preferred_element_type=jnp.float32)
        upstream = jnp.where(section_index == 1, placed, back_arrived.astype(jnp.float32))
        kept_values = forward_layer(
            source, positions, weights, first_row, length, dilated, in_range
        )
        d_mixed, d_pre, d_branch, norm_two = ffn_back(kept_values, weights, upstream, in_range)
        mixed_buf = lax.dynamic_update_index_in_dim(
            mixed_buf, kept_values.mixed.astype(jnp.bfloat16), store, 0
        )
        pre_buf = lax.dynamic_update_index_in_dim(pre_buf, d_pre, store, 0)
        act_buf = lax.dynamic_update_index_in_dim(act_buf, kept_values.activated, store, 0)
        branch_buf = lax.dynamic_update_index_in_dim(branch_buf, d_branch, store, 0)
        d_source, d_proj, d_gproj, d_attn, norm_one = attention_back(kept_values, weights, d_mixed)
        proj_buf = lax.dynamic_update_index_in_dim(proj_buf, d_proj, store, 0)
        gproj_buf = lax.dynamic_update_index_in_dim(gproj_buf, d_gproj, store, 0)
        ctx_buf = lax.dynamic_update_index_in_dim(ctx_buf, kept_values.context_low, store, 0)
        attn_buf = lax.dynamic_update_index_in_dim(attn_buf, d_attn, store, 0)
        gain_total = gain_total + jnp.where(in_range, jnp.stack([norm_one[0], norm_two[0]]), 0.0)
        shift_total = shift_total + jnp.where(in_range, jnp.stack([norm_one[1], norm_two[1]]), 0.0)
        d_low = d_source.astype(jnp.bfloat16)
        in_grads = jnp.where(
            in_range, lax.dynamic_update_index_in_dim(in_grads, d_low, slot_index, 0), in_grads
        )
        if step_index < micro_count:
            back_arrived = shifted(d_low, SECTION, -1)
    used_proj = proj_buf[:micro_count]
    used_gproj = gproj_buf[:micro_count]
    grad_local = jnp.einsum(
        "mcd,mce->de", kept_inputs, used_proj, preferred_element_type=jnp.float32
    )
    grad_glob = jnp.einsum(
        "mcd,mce->de", kept_inputs, used_gproj, preferred_element_type=jnp.float32
    )
    grad_out = jnp.einsum(
        "mcd,mce->de",
        ctx_buf[:micro_count],
        attn_buf[:micro_count],
        preferred_element_type=jnp.float32,
    )
    grad_out_b = jnp.sum(attn_buf[:micro_count].astype(jnp.float32), axis=(0, 1))
    local_b_grad = jnp.stack(
        [
            jnp.sum(used_proj[:, :, :model_width].astype(jnp.float32), axis=(0, 1)),
            jnp.sum(used_proj[:, :, 2 * model_width :].astype(jnp.float32), axis=(0, 1)),
        ]
    )
    glob_b_grad = jnp.stack(
        [
            jnp.sum(used_gproj[:, :, :model_width].astype(jnp.float32), axis=(0, 1)),
            jnp.sum(used_gproj[:, :, 2 * model_width :].astype(jnp.float32), axis=(0, 1)),
        ]
    )
    small_sums = lax.psum((local_b_grad, glob_b_grad, gain_total, shift_total), (SEQ, DP))
    ffn_parts = ffn_terms(mixed_buf, pre_buf, act_buf, branch_buf, micro_count)
    large_sums = (
        lax.psum_scatter(grad_local, (SEQ, DP), scatter_dimension=0, tiled=True),
        lax.psum_scatter(grad_glob, (SEQ, DP), scatter_dimension=0, tiled=True),
        lax.psum_scatter(grad_out, (SEQ, DP), scatter_dimension=0, tiled=True),
        lax.psum_scatter(grad_out_b, (SEQ, DP), scatter_dimension=0, tiled=True),
        lax.psum_scatter(ffn_parts[0], (SEQ, DP), scatter_dimension=0, tiled=True),
        lax.psum_scatter(ffn_parts[1], (SEQ, DP), scatter_dimension=0, tiled=True),
        lax.psum_scatter(ffn_parts[2], (SEQ, DP), scatter_dimension=0, tiled=True),
        lax.psum_scatter(ffn_parts[3], (SEQ, DP), scatter_dimension=0, tiled=True),
    )
    summed = (
        large_sums[0],
        small_sums[0],
        large_sums[1],
        small_sums[1],
        large_sums[2],
        large_sums[3],
        small_sums[2],
        small_sums[3],
        large_sums[4],
        large_sums[5],
        large_sums[6],
        large_sums[7],
    )
    return (outputs[None, :, None], in_grads[None, :, None]) + tuple(
        (member[None] for member in summed)
    )


bf16 = jnp.bfloat16
f32 = jnp.float32
VMEM_BYTES = 50 * 1024 * 1024


def nn(a, b):
    return jnp.dot(a, b, preferred_element_type=f32)


def nt(a, b):
    return lax.dot_general(a, b, (((1,), (1,)), ((), ())), preferred_element_type=f32)


def tn(a, b):
    return lax.dot_general(a, b, (((0,), (0,)), ((), ())), preferred_element_type=f32)


def owner_rows(prow, chunk, rows):
    at = lax.broadcasted_iota(jnp.int32, (rows, prow.shape[1]), 0) + chunk * rows
    return (at == prow[...]).astype(f32)


def owner_cols(pcol, chunk, rows):
    at = lax.broadcasted_iota(jnp.int32, (pcol.shape[0], rows), 1) + chunk * rows
    return (at == pcol[...]).astype(f32)


def is_dilated(layer, group, h):
    return ((3 * group + h >= 10) & (layer == 1)).astype(jnp.int32)


def band_masks(mask_s, dilated, rows):
    row = lax.broadcasted_iota(jnp.int32, (rows, rows), 0)
    col = lax.broadcasted_iota(jnp.int32, (rows, rows), 1)
    odd = ((row + col) % 2).astype(f32)
    level = odd * (dilated.astype(f32) * far_below)
    mask_s[0] = jnp.where(row >= col, level, far_below)
    mask_s[1] = level
    mask_s[2] = jnp.where(row <= col, level, far_below)


def neighbours(block, count):
    return [b for b in (block - 1, block, block + 1) if 0 <= b < count]


def cost(us):
    return pl.CostEstimate(
        flops=int(us * 1e9), transcendentals=0, bytes_accessed=int(us * 3.5e6)
    )


def start_all(copies):
    for copy in copies:
        copy.start()
    return copies


def wait_all(copies):
    for copy in copies:
        copy.wait()


def moves(pairs, sems, at=0):
    return [pltpu.make_async_copy(a, b, sems.at[at + i]) for i, (a, b) in enumerate(pairs)]


def choose(flag, first, second, target, sem):
    for value, source in ((0, first), (1, second)):

        @pl.when(flag == value)
        def _(source=source):
            pltpu.make_async_copy(source, target, sem).start()

    return pltpu.make_async_copy(first, target, sem)


def prepare_kernel(
    ids, lw, gw, lb, gb, ob, ng, ns, db, ub, own_o, send_o, pack_o, win_s, sems
):
    width = lw.shape[0]
    hw = width // 4
    sources = [(lw, 0), (lw, 1), (lw, 2), (gw, 1), (gw, 2), (gw, 0)]
    copies = []
    for t, group in enumerate((ids[1], ids[0])):
        for i, (ref, part) in enumerate(sources):
            start = pl.multiple_of(part * width + 128 * ((3 * group) // 2), 128)
            copies.append(
                pltpu.make_async_copy(
                    ref.at[:, pl.ds(start, 256)], win_s.at[t, i], sems.at[6 * t + i]
                )
            )
            copies[-1].start()
    pack_o[...] = jnp.zeros(pack_o.shape, bf16)
    at = 0
    for ref in (lb, gb, ob, ng, ns, db):
        pack_o[at : at + ref.shape[0], :] = ref[...]
        at += ref.shape[0]
    for i in range(ub.shape[1] // width):
        pack_o[at + i : at + i + 1, :] = ub[:, i * width : (i + 1) * width]
    for t, target in enumerate((send_o, own_o)):
        for i in range(6):
            copies[6 * t + i].wait()
        for odd in range(2):

            @pl.when(ids[6] == odd)
            def _(t=t, target=target, odd=odd):
                parts = [win_s[t, i][:, 64 * odd : 64 * odd + hw] for i in range(6)]
                target[...] = jnp.concatenate(parts, axis=1)


def prepare(ids, local_w, global_w, rows):
    width = local_w.shape[0]
    vm = pl.BlockSpec(memory_space=pltpu.VMEM)
    hbm = pl.BlockSpec(memory_space=pl.ANY)
    chosen = jax.ShapeDtypeStruct((width, 6 * width // 4), bf16)
    return pl.pallas_call(
        prepare_kernel,
        out_shape=[chosen, chosen, jax.ShapeDtypeStruct((16, width), bf16)],
        in_specs=[pl.BlockSpec(memory_space=pltpu.SMEM), hbm, hbm] + [vm] * 7,
        out_specs=[vm] * 3,
        scratch_shapes=[
            pltpu.VMEM((2, 6, width, 256), bf16),
            pltpu.SemaphoreType.DMA((12,)),
        ],
        compiler_params=pltpu.CompilerParams(vmem_limit_bytes=VMEM_BYTES),
        cost_estimate=cost(3),
        name="prepare",
    )(ids, local_w, global_w, *rows)


def attend_kernel(layer, *refs):
    count = 4
    sources = 7 if layer == 0 else 4
    ids, parts, refs = refs[0], refs[1 : 1 + sources], refs[1 + sources :]
    (
        w_a, w_b, pack_a, pack_b, prow, pcol,
        c0, c1, c2, c3, u_o, own_o, q_o, k_o, v_o, gk_o, gv_o, gq_o, kg_o, vg_o, lse_o,
        w_s, sem, vt_s, mask_s, ctx_s, gctx_s,
    ) = refs
    rows = c0.shape[0]
    heads = q_o.shape[0]
    hw = heads * HEAD
    scale = HEAD ** (-0.5)
    glob = prow.shape[1]
    group, core = ids[0], ids[4]
    w_copy = choose((core != layer).astype(jnp.int32), w_a, w_b, w_s, sem)
    if layer == 0:
        block = parts[0]
        half = rows // 2
        u_o[pl.ds(pl.multiple_of((2 * ids[5] + ids[6]) * rows, rows), rows), :] = block[ids[5]]
        places = (
            2 * ids[5] + 1 - ids[6],
            2 * (1 - ids[5]) + ids[6],
            2 * (1 - ids[5]) + 1 - ids[6],
        )
        for i, place in enumerate(places):
            for part, side in ((parts[1 + i], core), (parts[4 + i], 1 - core)):
                at = pl.multiple_of(place * rows + side * half, half)
                u_o[pl.ds(at, half), :] = part[...]
    else:
        for r in range(count):
            u_o[pl.ds(pl.multiple_of(ids[r] * rows, rows), rows), :] = parts[r][...]
    own_o[...] = u_o[pl.ds(pl.multiple_of(group * rows, rows), rows), :]
    pack = jnp.where(core == layer, pack_a[...].astype(f32), pack_b[...].astype(f32))[:4]
    hb = pack[:, :hw]
    for i in range(1, 4):
        hb = jnp.where(group == i, pack[:, i * hw : (i + 1) * hw], hb)
    kg_all = jnp.zeros((glob, hw), f32)
    vg_all = jnp.zeros((glob, hw), f32)
    ug_all = jnp.zeros((glob, u_o.shape[1]), f32)
    first = lax.broadcasted_iota(jnp.int32, (rows, HEAD), 1) == 0
    w_copy.wait()
    w = w_s
    for chunk in range(count):
        at = slice(chunk * rows, (chunk + 1) * rows)
        x = u_o[at, :]
        p = nn(x, w[:, : 5 * hw])
        queries = (p[:, :hw] + hb[0:1, :]).astype(bf16).astype(f32) * scale
        keys = p[:, hw : 2 * hw]
        values = p[:, 2 * hw : 3 * hw] + hb[1:2, :]
        gkeys = p[:, 3 * hw : 4 * hw]
        gvalues = p[:, 4 * hw : 5 * hw] + hb[3:4, :]
        is_global = jnp.max(owner_rows(prow, chunk, rows), axis=1, keepdims=True)
        tail_k = jnp.where(first, is_global * far_below, 0.0)
        tail_q = jnp.where(first, 1.0, 0.0)
        for h in range(heads):
            cut = slice(HEAD * h, HEAD * h + HEAD)
            q_o[h, at, :] = jnp.concatenate([queries[:, cut], tail_q], axis=1).astype(bf16)
            k_o[h, at, :] = jnp.concatenate([keys[:, cut], tail_k], axis=1).astype(bf16)
            v_o[h, at, :] = values[:, cut].astype(bf16)
            gk_o[h, at, :] = gkeys[:, cut].astype(bf16)
            gv_o[h, at, :] = gvalues[:, cut].astype(bf16)
            vt_s[h, chunk] = values[:, cut].T.astype(bf16)
        hit = owner_cols(pcol, chunk, rows).astype(bf16)
        kg_all += nn(hit, keys.astype(bf16))
        vg_all += nn(hit, values.astype(bf16))
        ug_all += nn(hit, x)
    gq_all = (nn(ug_all.astype(bf16), w[:, 5 * hw :]) + hb[2:3, :]).astype(bf16).astype(f32) * scale
    none = jnp.zeros((glob, HEAD), f32)
    for h in range(heads):
        cut = slice(HEAD * h, HEAD * h + HEAD)
        gq_o[h] = gq_all[:, cut].astype(bf16)
        kg_o[h] = jnp.concatenate([kg_all[:, cut], none], axis=1).astype(bf16)
        vg_o[h] = vg_all[:, cut].astype(bf16)

    def head(h, carry):
        band_masks(mask_s, is_dilated(layer, group, h), rows)
        kg = kg_o[h]
        vgt = vg_o[h].astype(f32).T.astype(bf16)
        for qb in range(count):
            q = q_o[h, qb * rows : (qb + 1) * rows, :]
            near = neighbours(qb, count)
            scores = [
                nt(k_o[h, kb * rows : (kb + 1) * rows, :], q) + mask_s[kb - qb + 1] for kb in near
            ]
            side = nt(kg, q)
            peak = jnp.max(side, axis=0, keepdims=True)
            for s in scores:
                peak = jnp.maximum(peak, jnp.max(s, axis=0, keepdims=True))
            side = jnp.exp(side - peak)
            scores = [jnp.exp(s - peak) for s in scores]
            total = jnp.sum(side, axis=0, keepdims=True)
            for s in scores:
                total += jnp.sum(s, axis=0, keepdims=True)
            inverse = 1.0 / total
            ctx = nn(vgt, (side * inverse).astype(bf16))
            for kb, s in zip(near, scores):
                ctx += nn(vt_s[h, kb], (s * inverse).astype(bf16))
            ctx_s[h, qb * rows : (qb + 1) * rows, :] = ctx.T
            lse_o[h, qb : qb + 1, :] = peak + jnp.log(total)
        spread = nt(gq_o[h], gk_o[h])
        e = jnp.exp(spread - jnp.max(spread, axis=1, keepdims=True))
        prob = (e / jnp.sum(e, axis=1, keepdims=True)).astype(bf16)
        gctx_s[h] = nn(prob, gv_o[h])
        return carry

    lax.fori_loop(0, heads, head, 0)
    gctx = jnp.concatenate([gctx_s[h] for h in range(heads)], axis=1).astype(bf16)
    for r, c_o in enumerate((c0, c1, c2, c3)):
        chunk = ids[r]
        at = pl.ds(pl.multiple_of(chunk * rows, rows), rows)
        hit = owner_rows(prow, chunk, rows)
        placed = nn(hit.astype(bf16), gctx)
        local = jnp.concatenate([ctx_s[h, at, :] for h in range(heads)], axis=1)
        c_o[...] = jnp.where(jnp.max(hit, axis=1, keepdims=True) > 0, placed, local).astype(bf16)


def attend(layer, ids, parts, weights, packs, prow, pcol):
    width = weights[0].shape[0]
    hw = weights[0].shape[1] // 6
    heads = hw // HEAD
    glob = prow.shape[1]
    rows = HALF
    full = 4 * rows
    sds = jax.ShapeDtypeStruct
    outs = [sds((rows, hw), bf16)] * 4 + [
        sds((full, width), bf16),
        sds((rows, width), bf16),
        sds((heads, full, 2 * HEAD), bf16),
        sds((heads, full, 2 * HEAD), bf16),
        sds((heads, full, HEAD), bf16),
        sds((heads, full, HEAD), bf16),
        sds((heads, full, HEAD), bf16),
        sds((heads, glob, HEAD), bf16),
        sds((heads, glob, 2 * HEAD), bf16),
        sds((heads, glob, HEAD), bf16),
        sds((heads, 4, rows), f32),
    ]
    vm = pl.BlockSpec(memory_space=pltpu.VMEM)
    hbm = pl.BlockSpec(memory_space=pl.ANY)
    res = pl.pallas_call(
        partial(attend_kernel, layer),
        out_shape=outs,
        in_specs=[pl.BlockSpec(memory_space=pltpu.SMEM)]
        + [vm] * len(parts)
        + [hbm] * 2
        + [vm] * 4,
        out_specs=[vm] * len(outs),
        scratch_shapes=[
            pltpu.VMEM(weights[0].shape, bf16),
            pltpu.SemaphoreType.DMA,
            pltpu.VMEM((heads, 4, HEAD, rows), bf16),
            pltpu.VMEM((3, rows, rows), f32),
            pltpu.VMEM((heads, full, HEAD), f32),
            pltpu.VMEM((heads, glob, HEAD), f32),
        ],
        compiler_params=pltpu.CompilerParams(vmem_limit_bytes=VMEM_BYTES),
        cost_estimate=cost(14),
        name="attend",
    )(ids, *parts, *weights, *packs, prow, pcol)
    return res[:4], res[4], res[5], res[6:]


def attend_back_kernel(
    layer, ids, d0, d1, d2, d3, q, k, v, gk, gv, gq, kg, vg, lse, prow, pcol, w_a, w_b,
    d_o, bias_o, p0, p1, p2, p3,
    w_s, sem, mask_s, do_s, dog_s, dq_s, dk_s, dv_s, dkg_s, dvg_s, dgk_s, dgv_s, dgq_s,
):
    rows = d0.shape[0]
    heads = q.shape[0]
    count = 4
    scale = HEAD ** (-0.5)
    glob = prow.shape[1]
    w_copy = choose((ids[4] != layer).astype(jnp.int32), w_a, w_b, w_s, sem)
    dg_all = jnp.zeros((glob, heads * HEAD), f32)
    for r, d in enumerate((d0, d1, d2, d3)):
        chunk = ids[r]
        at = pl.ds(pl.multiple_of(chunk * rows, rows), rows)
        dx = d[...]
        dg_all += nn(owner_cols(pcol, chunk, rows).astype(bf16), dx)
        is_global = jnp.max(owner_rows(prow, chunk, rows), axis=1, keepdims=True)
        local = jnp.where(is_global > 0, 0.0, dx.astype(f32))
        for h in range(heads):
            do_s[h, at, :] = local[:, HEAD * h : HEAD * h + HEAD].astype(bf16)
    for h in range(heads):
        dog_s[h] = dg_all[:, HEAD * h : HEAD * h + HEAD].astype(bf16)

    def head(h, carry):
        band_masks(mask_s, is_dilated(layer, ids[0], h), rows)
        kgh = kg[h]
        vgh = vg[h]
        kgt = kgh[:, :HEAD].astype(f32).T.astype(bf16)
        kt = [
            k[h, b * rows : (b + 1) * rows, :][:, :HEAD].astype(f32).T.astype(bf16)
            for b in range(count)
        ]
        dk = [jnp.zeros((rows, 2 * HEAD), f32) for _ in range(count)]
        dv = [jnp.zeros((rows, HEAD), f32) for _ in range(count)]
        dkg = jnp.zeros((glob, 2 * HEAD), f32)
        dvg = jnp.zeros((glob, HEAD), f32)
        for qb in range(count):
            span = slice(qb * rows, (qb + 1) * rows)
            qq = q[h, span, :]
            do = do_s[h, span, :]
            row = lse[h, qb : qb + 1, :]
            near = neighbours(qb, count)
            prob = [
                jnp.exp(nt(k[h, b * rows : (b + 1) * rows, :], qq) + mask_s[b - qb + 1] - row)
                for b in near
            ]
            side = jnp.exp(nt(kgh, qq) - row)
            dprob = [nt(v[h, b * rows : (b + 1) * rows, :], do) for b in near]
            dside = nt(vgh, do)
            inner = jnp.sum(side * dside, axis=0, keepdims=True)
            for p, dp in zip(prob, dprob):
                inner += jnp.sum(p * dp, axis=0, keepdims=True)
            ds = (side * (dside - inner)).astype(bf16)
            dvg += nn(side.astype(bf16), do)
            dkg += nn(ds, qq)
            dq = nn(kgt, ds)
            for b, p, dp in zip(near, prob, dprob):
                ds = (p * (dp - inner)).astype(bf16)
                dv[b] += nn(p.astype(bf16), do)
                dk[b] += nn(ds, qq)
                dq += nn(kt[b], ds)
            dq_s[h, span, :] = dq.T * scale
        for b in range(count):
            dk_s[h, b * rows : (b + 1) * rows, :] = dk[b][:, :HEAD]
            dv_s[h, b * rows : (b + 1) * rows, :] = dv[b]
        dkg_s[h] = dkg[:, :HEAD]
        dvg_s[h] = dvg
        spread = nt(gk[h], gq[h])
        e = jnp.exp(spread - jnp.max(spread, axis=0, keepdims=True))
        p = e / jnp.sum(e, axis=0, keepdims=True)
        dog = dog_s[h]
        dp = nt(gv[h], dog)
        ds = (p * (dp - jnp.sum(p * dp, axis=0, keepdims=True))).astype(bf16)
        dgv_s[h] = nn(p.astype(bf16), dog)
        dgk_s[h] = nn(ds, gq[h])
        dgq_s[h] = tn(ds, gk[h]) * scale
        return carry

    lax.fori_loop(0, heads, head, 0)

    def wide(ref, at=None):
        parts = [ref[h] if at is None else ref[h, at, :] for h in range(heads)]
        return jnp.concatenate(parts, axis=1)

    dkg_all = wide(dkg_s).astype(bf16)
    dvg_all = wide(dvg_s).astype(bf16)
    dgq_all = wide(dgq_s).astype(bf16)
    sums = [jnp.zeros((1, heads * HEAD), f32) for _ in range(4)]
    w_copy.wait()
    for r, p_o in enumerate((p0, p1, p2, p3)):
        chunk = ids[r]
        at = pl.ds(pl.multiple_of(chunk * rows, rows), rows)
        hit = owner_rows(prow, chunk, rows).astype(bf16)
        dq = wide(dq_s, at)
        dk = wide(dk_s, at) + nn(hit, dkg_all)
        dv = wide(dv_s, at) + nn(hit, dvg_all)
        dgk = wide(dgk_s, at)
        dgv = wide(dgv_s, at)
        dgq = nn(hit, dgq_all)
        joint = jnp.concatenate([dq, dk, dv, dgk, dgv, dgq], axis=1).astype(bf16)
        d_o[at, :] = joint
        p_o[...] = nt(joint, w_s[...]).astype(p_o.dtype)
        for i, part in enumerate((dq, dv, dgq, dgv)):
            sums[i] += jnp.sum(part, axis=0, keepdims=True)
    bias_o[...] = jnp.concatenate(sums, axis=0)


def attend_back(layer, ids, pieces, kept, prow, pcol, weights):
    rows, hw = pieces[0].shape
    width = weights[0].shape[0]
    heads = hw // HEAD
    glob = prow.shape[1]
    full = 4 * rows
    vm = pl.BlockSpec(memory_space=pltpu.VMEM)
    hbm = pl.BlockSpec(memory_space=pl.ANY)
    big = (heads, full, HEAD)
    small = (heads, glob, HEAD)
    res = pl.pallas_call(
        partial(attend_back_kernel, layer),
        out_shape=[
            jax.ShapeDtypeStruct((full, 6 * hw), bf16),
            jax.ShapeDtypeStruct((4, hw), f32),
        ]
        + [jax.ShapeDtypeStruct((rows, width), t) for t in (f32, bf16, f32, bf16)],
        in_specs=[pl.BlockSpec(memory_space=pltpu.SMEM)] + [vm] * 15 + [hbm] * 2,
        out_specs=[vm] * 6,
        scratch_shapes=[
            pltpu.VMEM(weights[0].shape, bf16),
            pltpu.SemaphoreType.DMA,
            pltpu.VMEM((3, rows, rows), f32),
            pltpu.VMEM(big, bf16),
            pltpu.VMEM(small, bf16),
            pltpu.VMEM(big, f32),
            pltpu.VMEM(big, f32),
            pltpu.VMEM(big, f32),
            pltpu.VMEM(small, f32),
            pltpu.VMEM(small, f32),
            pltpu.VMEM(big, f32),
            pltpu.VMEM(big, f32),
            pltpu.VMEM(small, f32),
        ],
        compiler_params=pltpu.CompilerParams(vmem_limit_bytes=VMEM_BYTES),
        cost_estimate=cost(18),
        name="attend_back",
    )(ids, *pieces, *kept, prow, pcol, *weights)
    return res[0], res[1], res[2:]


def fetch(first, second, use_second, pairs, sems):
    for flag, source in ((0, first), (1, second)):

        @pl.when(use_second.astype(jnp.int32) == flag)
        def _(source=source):
            for i, (pick, target) in enumerate(pairs):
                pltpu.make_async_copy(pick(source), target, sems.at[i]).start()

    def wait(i):
        pick, target = pairs[i]
        pltpu.make_async_copy(pick(first), target, sems.at[i]).wait()

    return wait


def weight_pairs(steps, cols, wo_s, wu_s, wd_s):
    pairs = [(lambda w: w[0], wo_s)]
    for j in range(steps):
        pairs.append((lambda w, j=j: w[1].at[:, pl.ds(j * cols, cols)], wu_s.at[j]))
        pairs.append((lambda w, j=j: w[2].at[pl.ds(j * cols, cols), :], wd_s.at[j]))
    return pairs


def row_norm(z):
    center = z - jnp.mean(z, axis=1, keepdims=True)
    scaled = lax.rsqrt(jnp.mean(center * center, axis=1, keepdims=True) + norm_eps)
    return center * scaled, scaled


def rows_kernel(
    layer, ids, c0, c1, c2, c3, u, pack_a, pack_b, wo_a, wo_b, wu_a, wu_b, wd_a, wd_b,
    y_o, fwd_o, slope_o, unit1_o, unit2_o, scale1_o, scale2_o,
    wo_s, wu_s, wd_s, sems,
):
    steps, cols = wu_s.shape[0], wu_s.shape[2]
    pairs = weight_pairs(steps, cols, wo_s, wu_s, wd_s)
    wait = fetch((wo_a, wu_a, wd_a), (wo_b, wu_b, wd_b), ids[4] != layer, pairs, sems)
    pack = jnp.where(ids[4] == layer, pack_a[...].astype(f32), pack_b[...].astype(f32))
    hw = c0.shape[1]
    width = 4 * hw
    pieces = [c[...] for c in (c0, c1, c2, c3)]
    for a in range(4):
        part = pieces[0]
        for r in range(1, 4):
            part = jnp.where(ids[r] == a, pieces[r].astype(f32), part.astype(f32))
        fwd_o[:, width + a * hw : width + (a + 1) * hw] = part.astype(bf16)
    wait(0)
    attn = nn(fwd_o[:, width : 2 * width], wo_s[...]) + pack[4:5, :]
    unit1, scale1 = row_norm(u[...].astype(f32) + attn)
    mixed = unit1 * pack[5:6, :] + pack[7:8, :]
    low = mixed.astype(bf16)
    fwd_o[:, :width] = low
    unit1_o[...] = unit1
    scale1_o[...] = jnp.broadcast_to(scale1, scale1_o.shape)
    branch = jnp.zeros(mixed.shape, f32)
    for j in range(steps):
        wait(1 + 2 * j)
        pre = nn(low, wu_s[j]) + pack[10 + j : 11 + j, :]
        gauss = 0.5 * (1.0 + lax.erf(pre * (2.0 ** -0.5)))
        act = (pre * gauss).astype(bf16)
        bell = jnp.exp(-0.5 * pre * pre) * ((2.0 * np.pi) ** -0.5)
        slope_o[:, j * cols : (j + 1) * cols] = (gauss + pre * bell).astype(bf16)
        fwd_o[:, 2 * width + j * cols : 2 * width + (j + 1) * cols] = act
        wait(2 + 2 * j)
        branch += nn(act, wd_s[j])
    unit2, scale2 = row_norm(mixed + (branch + pack[9:10, :]))
    unit2_o[...] = unit2
    scale2_o[...] = jnp.broadcast_to(scale2, scale2_o.shape)
    y_o[...] = (unit2 * pack[6:7, :] + pack[8:9, :]).astype(bf16)


def rows_forward(layer, ids, pieces, u, packs, own, other):
    rows, width = u.shape
    ff = own[1].shape[1]
    steps = ff // width
    vm = pl.BlockSpec(memory_space=pltpu.VMEM)
    hbm = pl.BlockSpec(memory_space=pl.ANY)
    sds = jax.ShapeDtypeStruct
    return pl.pallas_call(
        partial(rows_kernel, layer),
        out_shape=[
            sds((rows, width), bf16),
            sds((rows, 2 * width + ff), bf16),
            sds((rows, ff), bf16),
            sds((rows, width), f32),
            sds((rows, width), f32),
            sds((rows, 128), f32),
            sds((rows, 128), f32),
        ],
        in_specs=[pl.BlockSpec(memory_space=pltpu.SMEM)] + [vm] * 7 + [hbm] * 6,
        out_specs=[vm] * 7,
        scratch_shapes=[
            pltpu.VMEM((width, width), bf16),
            pltpu.VMEM((steps, width, width), bf16),
            pltpu.VMEM((steps, width, width), bf16),
            pltpu.SemaphoreType.DMA((1 + 2 * steps,)),
        ],
        compiler_params=pltpu.CompilerParams(vmem_limit_bytes=VMEM_BYTES),
        cost_estimate=cost(10),
        name="rows_forward",
    )(ids, *pieces, u, *packs, own[0], other[0], own[1], other[1], own[2], other[2])


def norm_inward(unit, scaled, gain, upstream):
    d_unit = upstream * gain
    return scaled * (
        d_unit
        - jnp.mean(d_unit, axis=1, keepdims=True)
        - unit * jnp.mean(d_unit * unit, axis=1, keepdims=True)
    )


def rows_back_kernel(
    layer, ids, up, unit1, unit2, scale1, scale2, slope, pack_a, pack_b, wo_a, wo_b, wu_a, wu_b, wd_a, wd_b,
    first_o, d0, d1, d2, d3, keep_o, send_o, small_o,
    wo_s, wu_s, wd_s, sems,
):
    steps, cols = wu_s.shape[0], wu_s.shape[2]
    pairs = weight_pairs(steps, cols, wo_s, wu_s, wd_s)
    wait = fetch((wo_a, wu_a, wd_a), (wo_b, wu_b, wd_b), ids[4] != layer, pairs, sems)
    pack = jnp.where(ids[4] == layer, pack_a[...].astype(f32), pack_b[...].astype(f32))
    side = ids[4]
    half = first_o.shape[1] // 2
    ffh = keep_o.shape[1] - 2 * half

    def split(value, at):
        for s in range(2):

            @pl.when(side == s)
            def _(s=s):
                keep_o[:, at : at + half] = value[:, s * half : (s + 1) * half]
                send_o[:, at : at + half] = value[:, (1 - s) * half : (2 - s) * half]

    def total(value):
        return jnp.sum(value, axis=0, keepdims=True)

    upstream = up[...].astype(f32)
    unit = unit2[...]
    small_o[0:1, :] = total(upstream * unit)
    small_o[1:2, :] = total(upstream)
    d_second = norm_inward(unit, scale2[:, :1], pack[6:7, :], upstream)
    d_branch = d_second.astype(bf16)
    split(d_branch, ffh)
    small_o[5:6, :] = total(d_branch.astype(f32))
    d_mixed = d_second
    for j in range(steps):
        wait(2 + 2 * j)
        d_act = nt(d_branch, wd_s[j])
        d_pre = (d_act * slope[:, j * cols : (j + 1) * cols].astype(f32)).astype(bf16)
        small_o[6 + j : 7 + j, :] = total(d_pre.astype(f32))
        place = slice((j % (steps // 2)) * cols, (j % (steps // 2) + 1) * cols)

        @pl.when(side == j // (steps // 2))
        def _(d_pre=d_pre, place=place):
            keep_o[:, place] = d_pre

        @pl.when(side != j // (steps // 2))
        def _(d_pre=d_pre, place=place):
            send_o[:, place] = d_pre

        wait(1 + 2 * j)
        d_mixed += nt(d_pre, wu_s[j])
    unit = unit1[...]
    small_o[2:3, :] = total(d_mixed * unit)
    small_o[3:4, :] = total(d_mixed)
    d_first = norm_inward(unit, scale1[:, :1], pack[5:6, :], d_mixed)
    first_o[...] = d_first
    d_attn = d_first.astype(bf16)
    split(d_attn, ffh + half)
    small_o[4:5, :] = total(d_attn.astype(f32))
    small_o[10:, :] = jnp.zeros((small_o.shape[0] - 10, small_o.shape[1]), f32)
    wait(0)
    d_ctx = nt(d_attn, wo_s[...])
    hw = d0.shape[1]
    parts = [d_ctx[:, a * hw : (a + 1) * hw] for a in range(4)]
    for r, d_o in enumerate((d0, d1, d2, d3)):
        part = parts[0]
        for a in range(1, 4):
            part = jnp.where(ids[r] == a, parts[a], part)
        d_o[...] = part.astype(bf16)


def rows_back(layer, ids, upstream, kept, packs, own, other):
    rows, width = upstream.shape
    ff = own[1].shape[1]
    steps = ff // width
    hw = width // 4
    unit1, unit2, scale1, scale2, slope = kept
    vm = pl.BlockSpec(memory_space=pltpu.VMEM)
    hbm = pl.BlockSpec(memory_space=pl.ANY)
    sds = jax.ShapeDtypeStruct
    return pl.pallas_call(
        partial(rows_back_kernel, layer),
        out_shape=[sds((rows, width), f32)]
        + [sds((rows, hw), bf16)] * 4
        + [sds((rows, ff // 2 + width), bf16)] * 2
        + [sds((16, width), f32)],
        in_specs=[pl.BlockSpec(memory_space=pltpu.SMEM)] + [vm] * 8 + [hbm] * 6,
        out_specs=[vm] * 8,
        scratch_shapes=[
            pltpu.VMEM((width, width), bf16),
            pltpu.VMEM((steps, width, width), bf16),
            pltpu.VMEM((steps, width, width), bf16),
            pltpu.SemaphoreType.DMA((1 + 2 * steps,)),
        ],
        compiler_params=pltpu.CompilerParams(vmem_limit_bytes=VMEM_BYTES),
        cost_estimate=cost(11),
        name="rows_back",
    )(
        ids, upstream, unit1, unit2, scale1, scale2, slope, *packs,
        own[0], other[0], own[1], other[1], own[2], other[2],
    )


def rows_ahead(ids, pieces, u, pack, wait, weights, fwd_s, slope_s):
    wo_s, wu_s, wd_s = weights
    steps, cols = wu_s.shape[0], wu_s.shape[2]
    hw = pieces[0].shape[1]
    width = 4 * hw
    values = [c[...].astype(f32) for c in pieces]
    for a in range(4):
        part = values[0]
        for r in range(1, 4):
            part = jnp.where(ids[r] == a, values[r], part)
        fwd_s[:, width + a * hw : width + (a + 1) * hw] = part.astype(bf16)
    wait(0)
    attn = nn(fwd_s[:, width : 2 * width], wo_s[...]) + pack[4:5, :]
    unit1, scale1 = row_norm(u[...].astype(f32) + attn)
    mixed = unit1 * pack[5:6, :] + pack[7:8, :]
    low = mixed.astype(bf16)
    fwd_s[:, :width] = low
    branch = jnp.zeros(mixed.shape, f32)
    for j in range(steps):
        wait(1 + 2 * j)
        pre = nn(low, wu_s[j]) + pack[10 + j : 11 + j, :]
        gauss = 0.5 * (1.0 + lax.erf(pre * (2.0 ** -0.5)))
        act = (pre * gauss).astype(bf16)
        bell = jnp.exp(-0.5 * pre * pre) * ((2.0 * np.pi) ** -0.5)
        slope_s[:, j * cols : (j + 1) * cols] = (gauss + pre * bell).astype(bf16)
        fwd_s[:, 2 * width + j * cols : 2 * width + (j + 1) * cols] = act
        wait(2 + 2 * j)
        branch += nn(act, wd_s[j])
    unit2, scale2 = row_norm(mixed + (branch + pack[9:10, :]))
    return unit2 * pack[6:7, :] + pack[8:9, :], (unit1, scale1), (unit2, scale2)


def rows_behind(ids, upstream, norm1, norm2, pack, wait, weights, slope_s, outs):
    first_o, pieces, keep_s, send_s, small_o = outs
    wo_s, wu_s, wd_s = weights
    steps, cols = wu_s.shape[0], wu_s.shape[2]
    side = ids[4]
    half = first_o.shape[1] // 2
    ffh = keep_s.shape[1] - 2 * half

    def split(value, at):
        for s in range(2):

            @pl.when(side == s)
            def _(s=s):
                keep_s[:, at : at + half] = value[:, s * half : (s + 1) * half]
                send_s[:, at : at + half] = value[:, (1 - s) * half : (2 - s) * half]

    def total(value):
        return jnp.sum(value, axis=0, keepdims=True)

    unit, scaled = norm2
    small_o[0:1, :] = total(upstream * unit)
    small_o[1:2, :] = total(upstream)
    d_second = norm_inward(unit, scaled, pack[6:7, :], upstream)
    d_branch = d_second.astype(bf16)
    split(d_branch, ffh)
    small_o[5:6, :] = total(d_branch.astype(f32))
    d_mixed = d_second
    for j in range(steps):
        wait(2 + 2 * j)
        d_act = nt(d_branch, wd_s[j])
        d_pre = (d_act * slope_s[:, j * cols : (j + 1) * cols].astype(f32)).astype(bf16)
        small_o[6 + j : 7 + j, :] = total(d_pre.astype(f32))
        place = slice((j % (steps // 2)) * cols, (j % (steps // 2) + 1) * cols)

        @pl.when(side == j // (steps // 2))
        def _(d_pre=d_pre, place=place):
            keep_s[:, place] = d_pre

        @pl.when(side != j // (steps // 2))
        def _(d_pre=d_pre, place=place):
            send_s[:, place] = d_pre

        wait(1 + 2 * j)
        d_mixed += nt(d_pre, wu_s[j])
    unit, scaled = norm1
    small_o[2:3, :] = total(d_mixed * unit)
    small_o[3:4, :] = total(d_mixed)
    d_first = norm_inward(unit, scaled, pack[5:6, :], d_mixed)
    first_o[...] = d_first
    d_attn = d_first.astype(bf16)
    split(d_attn, ffh + half)
    small_o[4:5, :] = total(d_attn.astype(f32))
    small_o[10:, :] = jnp.zeros((small_o.shape[0] - 10, small_o.shape[1]), f32)
    wait(0)
    d_ctx = nt(d_attn, wo_s[...])
    hw = pieces[0].shape[1]
    parts = [d_ctx[:, a * hw : (a + 1) * hw] for a in range(4)]
    for r, d_o in enumerate(pieces):
        part = parts[0]
        for a in range(1, 4):
            part = jnp.where(ids[r] == a, parts[a], part)
        d_o[...] = part.astype(bf16)


def own_pack(layer, ids, pack_a, pack_b):
    return jnp.where(ids[4] == layer, pack_a[...].astype(f32), pack_b[...].astype(f32))


def rows_both_kernel(
    ids, c0, c1, c2, c3, u, up, pack_a, pack_b, wo_a, wo_b, wu_a, wu_b, wd_a, wd_b,
    y_o, first_o, d0, d1, d2, d3, small_o, keep_o, send_o, fwd_h,
    fwd_s, slope_s, out_sem, wo_s, wu_s, wd_s, sems,
):
    steps, cols = wu_s.shape[0], wu_s.shape[2]
    pairs = weight_pairs(steps, cols, wo_s, wu_s, wd_s)
    wait = fetch((wo_a, wu_a, wd_a), (wo_b, wu_b, wd_b), ids[4] != 1, pairs, sems)
    pack = own_pack(1, ids, pack_a, pack_b)
    weights = (wo_s, wu_s, wd_s)
    y, norm1, norm2 = rows_ahead(ids, (c0, c1, c2, c3), u, pack, wait, weights, fwd_s, slope_s)
    out = pltpu.make_async_copy(fwd_s, fwd_h, out_sem)
    out.start()
    y_o[...] = y.astype(bf16)
    rows_behind(
        ids, up[...].astype(f32), norm1, norm2, pack, lambda i: None, weights, slope_s,
        (first_o, (d0, d1, d2, d3), keep_o, send_o, small_o),
    )
    out.wait()


def rows_both(ids, pieces, u, upstream, packs, own, other):
    rows, width = u.shape
    ff = own[1].shape[1]
    steps = ff // width
    vm = pl.BlockSpec(memory_space=pltpu.VMEM)
    hbm = pl.BlockSpec(memory_space=pl.ANY)
    sds = jax.ShapeDtypeStruct
    res = pl.pallas_call(
        rows_both_kernel,
        out_shape=[sds((rows, width), bf16), sds((rows, width), f32)]
        + [sds((rows, width // 4), bf16)] * 4
        + [sds((16, width), f32)]
        + [sds((rows, ff // 2 + width), bf16)] * 2
        + [sds((rows, 2 * width + ff), bf16)],
        in_specs=[pl.BlockSpec(memory_space=pltpu.SMEM)] + [vm] * 8 + [hbm] * 6,
        out_specs=[vm] * 9 + [hbm],
        scratch_shapes=[
            pltpu.VMEM((rows, 2 * width + ff), bf16),
            pltpu.VMEM((rows, ff), bf16),
            pltpu.SemaphoreType.DMA,
            pltpu.VMEM((width, width), bf16),
            pltpu.VMEM((steps, width, width), bf16),
            pltpu.VMEM((steps, width, width), bf16),
            pltpu.SemaphoreType.DMA((1 + 2 * steps,)),
        ],
        compiler_params=pltpu.CompilerParams(vmem_limit_bytes=VMEM_BYTES),
        cost_estimate=cost(15),
        name="rows_both",
    )(
        ids, *pieces, u, upstream, *packs, own[0], other[0], own[1], other[1], own[2], other[2],
    )
    return res[0], res[9], res[1:9]


def grads_kernel(layer, ids, f0, f1, k0, k1, *refs):
    count = 1 if layer == 1 else 6
    targets, outs, (f, b, in_sems, out_sems) = refs[:count], refs[count : 2 * count], refs[2 * count :]
    rows = f0.shape[0]
    part = f0.shape[1] // 12
    width = 2 * part
    ffh = k0.shape[1] - width
    ins = []
    for at, n in [(None, None), (0, 2 * width)] + [(width * (2 + i), width) for i in range(4)]:
        for side, (fx, kx) in enumerate(((f0, k0), (f1, k1))):
            to = pl.ds(side * rows, rows)
            pair = (kx, b.at[to, :]) if at is None else (fx.at[:, pl.ds(at, n)], f.at[to, pl.ds(at, n)])
            ins += start_all(moves([pair], in_sems, len(ins)))
    wait_all(ins[:4])
    pre, branch, attn = b[:, :ffh], b[:, ffh : ffh + part], b[:, ffh + part :]
    if layer == 1:
        out, out_h = outs[0], targets[0]
        few, many = width // 16, 8 * part // 16
        blocks = ffh // part
        for j in range(2):
            at = j * part
            up = tn(f[:, at : at + part], pre).astype(bf16)
            last = tn(f[:, width + at : width + at + part], attn).astype(bf16)
            for s in range(8):
                cut = slice(s * few, (s + 1) * few)
                for i in range(blocks):
                    out[8 * j + s, i * few : (i + 1) * few, :] = up[cut, i * part : (i + 1) * part]
                out[8 * j + s, blocks * few : (blocks + 1) * few, :] = last[cut]
        sent = []
        for j in range(8):
            if j % 2 == 0:
                wait_all(ins[4 + j : 6 + j])
            at = 2 * width + j * part
            down = tn(f[:, at : at + part], branch).astype(bf16)
            for s in range(2):
                out[2 * j + s, (blocks + 1) * few :, :] = down[s * many : (s + 1) * many]
            pair = pl.ds(2 * j, 2)
            sent += start_all(moves([(out.at[pair], out_h.at[pair])], out_sems, j))
        wait_all(sent)
        return
    ua_o, ub_o, uk_o, da_o, db_o, dk_o = outs
    ua = ua_o.shape[1]
    small = dk_o.shape[1]
    sub = small // 2

    def rows_at(at):
        return f[:, pl.ds(pl.multiple_of(at, 128), part)]

    start = (1 - ids[5]) * part
    up = tn(rows_at(start), pre).astype(bf16)
    ua_o[...] = up[:, :ua]
    ub_o[:, : ffh - ua] = up[:, ua:]
    ub_o[:, ffh - ua :] = tn(rows_at(start + width), attn).astype(bf16)
    sent = start_all(moves(list(zip(outs[:2], targets[:2])), out_sems))
    start = ids[5] * part
    uk_o[:, :ffh] = tn(rows_at(start), pre).astype(bf16)
    uk_o[:, ffh:] = tn(rows_at(start + width), attn).astype(bf16)
    sent += start_all(moves([(uk_o, targets[2])], out_sems, 2))
    for j in range(8):
        if j % 2 == 0:
            wait_all(ins[4 + j : 6 + j])
        at = 2 * width + 2 * small * j
        down = tn(f[:, at : at + 2 * small], branch).astype(bf16)
        for low in range(2):
            block = down[small * low : small * (low + 1)]
            share = 2 * j + low
            place, mine = (share // 8) * 4 + share % 4, ids[6] == (share // 4) % 2

            @pl.when(mine)
            def _(block=block, place=place):
                dk_o[place] = block

            @pl.when(jnp.logical_not(mine))
            def _(block=block, place=place):
                da_o[place] = block[:sub]
                db_o[place] = block[sub:]

    wait_all(sent + start_all(moves(list(zip(outs[3:], targets[3:])), out_sems, 3)))


def grads(layer, ids, fwd, fwd_other, keep, got):
    width = HEAD * 12
    ff = 2 * (keep.shape[1] - width)
    part = width // 2
    ua = 1024
    small = ff // 16
    hbm = pl.BlockSpec(memory_space=pltpu.HBM)
    shapes = [
        (part, ua),
        (part, ff // 2 + part - ua),
        (part, ff // 2 + part),
        (8, small // 2, part),
        (8, small // 2, part),
        (8, small, part),
    ]
    if layer == 1:
        shapes = [(16, (ff // 2 // part + 1) * width // 16 + ff // 16, part)]
    return pl.pallas_call(
        partial(grads_kernel, layer),
        out_shape=[jax.ShapeDtypeStruct(shape, bf16) for shape in shapes],
        in_specs=[pl.BlockSpec(memory_space=pltpu.SMEM)] + [hbm] * 4,
        out_specs=[hbm] * len(shapes),
        scratch_shapes=[pltpu.VMEM(shape, bf16) for shape in shapes]
        + [
            pltpu.VMEM((2 * fwd.shape[0], fwd.shape[1]), bf16),
            pltpu.VMEM((2 * keep.shape[0], keep.shape[1]), bf16),
            pltpu.SemaphoreType.DMA((12,)),
            pltpu.SemaphoreType.DMA((8,)),
        ],
        compiler_params=pltpu.CompilerParams(vmem_limit_bytes=VMEM_BYTES),
        cost_estimate=cost(5),
        name="grads",
    )(ids, fwd, fwd_other, keep, got)


def proj_grads_kernel(ids, u_h, d_h, ra_h, rb_h, rk_h, u, d, ra_o, rb_o, rk_o, sems):
    wait_all(start_all(moves([(u_h, u), (d_h, d)], sems)))
    part = rk_o.shape[0]
    ra = ra_o.shape[1]
    rows = tn(u[:, pl.ds(pl.multiple_of((1 - ids[5]) * part, 128), part)], d[...]).astype(bf16)
    ra_o[...] = rows[:, :ra]
    rb_o[...] = rows[:, ra:]
    out = start_all(moves([(ra_o, ra_h), (rb_o, rb_h)], sems, 2))
    rk_o[...] = tn(u[:, pl.ds(pl.multiple_of(ids[5] * part, 128), part)], d[...]).astype(bf16)
    wait_all(out + start_all(moves([(rk_o, rk_h)], sems, 4)))


def proj_grads(ids, u, d):
    part = u.shape[1] // 2
    cols = d.shape[1]
    hbm = pl.BlockSpec(memory_space=pltpu.HBM)
    shapes = [(part, n) for n in (640, cols - 640, cols)]
    return pl.pallas_call(
        proj_grads_kernel,
        out_shape=[jax.ShapeDtypeStruct(shape, bf16) for shape in shapes],
        in_specs=[pl.BlockSpec(memory_space=pltpu.SMEM)] + [hbm] * 2,
        out_specs=[hbm] * 3,
        scratch_shapes=[pltpu.VMEM(shape, bf16) for shape in [u.shape, d.shape] + shapes]
        + [pltpu.SemaphoreType.DMA((5,))],
        compiler_params=pltpu.CompilerParams(vmem_limit_bytes=VMEM_BYTES),
        cost_estimate=cost(4),
        name="proj_grads",
    )(ids, u, d)


def assemble_kernel(sizes, ids, fk, fg, ak, ag, up_o, out_o, down_o, local_o, glob_o):
    share_w, share_f, ff, width = sizes
    part, hw = width // 2, width // 4
    core, x = ids[4], ids[6]
    for side in range(2):

        @pl.when(core == side)
        def _(side=side):
            halves = (fk, fg) if side == 0 else (fg, fk)
            for c, ref in enumerate(halves):
                for i in range(4):
                    to = c * (ff // 2) + i * part
                    up_o[:, to : to + part] = ref[i * share_w : (i + 1) * share_w, :]
                out_o[:, c * part : (c + 1) * part] = ref[4 * share_w : 5 * share_w, :]
                down_o[:, c * part : (c + 1) * part] = ref[5 * share_w :, :]

    held = []
    for group in range(4):
        pair = [jnp.where(core == group // 2, ak[i].astype(f32), ag[i].astype(f32)) for i in range(2)]
        held.append(jnp.where(x == group % 2, pair[0], pair[1]))
    for target, kinds in ((local_o, (0, 1, 2)), (glob_o, (5, 3, 4))):
        target[...] = jnp.concatenate(
            [held[g][:, k * hw : (k + 1) * hw] for k in kinds for g in range(4)], axis=1
        )


def assemble(ids, ffn_keep, ffn_got, att_keep, att_got, sizes):
    share_w, share_f, ff, width = sizes
    vm = pl.BlockSpec(memory_space=pltpu.VMEM)
    shapes = [(share_w, ff), (share_w, width), (share_f, width)] + [(share_w, 3 * width)] * 2
    return pl.pallas_call(
        partial(assemble_kernel, sizes),
        out_shape=[jax.ShapeDtypeStruct(shape, f32) for shape in shapes],
        in_specs=[pl.BlockSpec(memory_space=pltpu.SMEM)] + [vm] * 4,
        out_specs=[vm] * 5,
        compiler_params=pltpu.CompilerParams(vmem_limit_bytes=VMEM_BYTES),
        name="assemble",
    )(ids, ffn_keep, ffn_got, att_keep, att_got)


def core_flip(v):
    return lax.ppermute(v, SECTION, [(0, 1), (1, 0)])


def seq_flip(v, by):
    return lax.ppermute(v, SEQ, [(i, i ^ by) for i in range(4)])


def core_x_flip(v):
    return lax.ppermute(v, BOTH, [(i, i ^ 5) for i in range(8)])


def dp_flip(v, by):
    return lax.ppermute(v, DP, [(i, i ^ by) for i in range(lax.axis_size(DP))])


def pick(which, options):
    result = options[-1]
    for i in range(len(options) - 2, -1, -1):
        result = jnp.where(which == i, options[i], result)
    return result


def to_section(v, layer):
    near = [(y_ * 4 + 2 * y_ + x_, layer * 4 + 2 * y_ + x_) for y_ in (0, 1) for x_ in (0, 1)]
    far = [
        ((1 - y_) * 4 + 2 * y_ + x_, layer * 4 + 2 * (1 - y_) + x_) for y_ in (0, 1) for x_ in (0, 1)
    ]
    return lax.ppermute(v, BOTH, near), lax.ppermute(v, BOTH, far)


def by_micro(first, lower, upper, y):
    mine = jnp.where(first, lower[0], upper[0])
    away = jnp.where(first, lower[1], upper[1])
    return jnp.where(y == 0, jnp.stack([mine, away]), jnp.stack([away, mine]))


def two_chips(
    layer_in, cotangent, masked_rows, global_positions, local_weight, local_bias, global_weight,
    global_bias, out_weight, out_bias, norm_gain, norm_shift, up_weight, up_bias, down_weight,
    down_bias,
):
    c = lax.axis_index(SECTION)
    q = lax.axis_index(SEQ)
    z = lax.axis_index(DP)
    dp = lax.axis_size(DP)
    y, x = q // 2, q % 2
    g = 2 * c + x
    g_other = 2 * (1 - c) + x
    rows, width = layer_in.shape[2:]
    hw = width // 4
    ff = up_weight.shape[2]
    heads = hw // HEAD
    half_rows = rows // 2
    same = c == y
    first = c == 0

    block = layer_in[:, 0]

    def half_of(micro):
        return lax.dynamic_slice(block, (micro, c * half_rows, 0), (1, half_rows, width))[0]

    mine_part, away_part = half_of(y), half_of(1 - y)
    got = [seq_flip(mine_part, 1), seq_flip(away_part, 2), seq_flip(away_part, 3)]

    cot = cotangent[:, 0]
    marks = masked_rows[:, 0]

    def of_micro(v, micro):
        return lax.dynamic_index_in_dim(v, micro, 0, keepdims=False)

    cot_away = seq_flip(of_micro(cot, 1 - y), 2)
    marks_away = seq_flip(of_micro(marks, 1 - y), 2)

    ids = jnp.stack([g, g_other, 2 * c + 1 - x, 2 * (1 - c) + 1 - x, c, y, x, z]).astype(jnp.int32)
    ids, _ = lax.optimization_barrier((ids, (mine_part, away_part)))
    w_own, w_send, pack = prepare(
        ids,
        local_weight[0],
        global_weight[0],
        (local_bias[0], global_bias[0], out_bias, norm_gain[0], norm_shift[0], down_bias, up_bias),
    )
    own = (out_weight[0], up_weight[0], down_weight[0])
    other_up = core_flip(own[1])
    (w_own, w_send, pack), (got, other_up) = lax.optimization_barrier(
        ((w_own, w_send, pack), (got, other_up))
    )
    weights = (w_own, core_flip(w_send))
    packs = (pack, core_flip(pack))
    positions = of_micro(global_positions[:, 0], y)
    prow = positions[None, :]
    pcol = positions[:, None]
    parts = [block] + got + [core_flip(v) for v in got]
    own_late, _ = lax.optimization_barrier(((own[0], own[2]), (parts, weights, packs)))
    other_out, other_down = [core_flip(w) for w in own_late]
    other = (other_out, other_up, other_down)

    def exchange(pieces):
        return [pieces[0], core_flip(pieces[1]), seq_flip(pieces[2], 1), core_x_flip(pieces[3])]

    saved = []
    for layer in range(2):
        ctx, u_all, u_own, kept = attend(layer, ids, parts, weights, packs, prow, pcol)
        if layer == 0:
            ctx, other = lax.optimization_barrier((ctx, other))
        pieces = exchange(ctx)
        if layer == 0:
            res = rows_forward(layer, ids, pieces, u_own, packs, own, other)
            y_low, fwd, slope, *row_kept = res
            row_kept.append(slope)
            across = seq_flip(y_low, 1)
            across, (cot_away, marks_away, fwd_other) = lax.optimization_barrier(
                (across, (cot_away, marks_away, core_flip(fwd)))
            )
            parts = [y_low, core_flip(y_low), across, core_flip(across)]
            saved_low = y_low
            saved.append((u_all, kept, fwd, fwd_other, row_kept))
        else:
            pieces, out0 = lax.optimization_barrier((pieces, to_section(saved_low, 0)))
            cot_rows = jnp.where(same, of_micro(cot, y), cot_away)
            cot_marks = jnp.where(same, of_micro(marks, y), marks_away)
            row_hit = (g * rows + jnp.arange(rows))[:, None] == cot_marks[None, :]
            upstream = nn(row_hit.astype(bf16), cot_rows).astype(bf16)
            y_low, fwd, back = rows_both(ids, pieces, u_own, upstream, packs, own, other)

    flip_x = partial(seq_flip, by=1)
    flip_y = partial(seq_flip, by=2)
    flip_z1 = partial(dp_flip, by=1)
    flip_z2 = partial(dp_flip, by=2)
    low_z, high_z = z % 2, z // 2

    def after(value, others):
        return lax.optimization_barrier((value, others))

    def cut(value, axis, bit):
        return of_axis(value, axis, 1 - bit).astype(bf16), of_axis(value, axis, bit)

    def of_axis(value, axis, index):
        return lax.dynamic_index_in_dim(value, index, axis, keepdims=False)

    def plus(keep, got):
        return keep.astype(f32) + got.astype(f32)

    def bias_rows(small, bias):
        placed = jnp.concatenate([jnp.where(g == i, bias, 0.0) for i in range(4)], axis=1)
        return jnp.concatenate([small[:10], placed], axis=0)

    def inward(partials):
        low = [core_flip(partials[1]), core_flip(partials[3])]
        return plus(partials[0], low[0]), plus(partials[2], low[1]).astype(bf16)

    ua = 1024
    share_w = width // (4 * dp)
    share_f = ff // (4 * dp)
    sub = share_f // 2
    part = width // 2

    d_first, pieces, (small, keep, send) = back[0], exchange(back[1:5]), back[5:]
    gr = grads(1, ids, fwd, core_flip(fwd), keep, core_flip(send))
    pieces, gr = after(pieces, gr)
    ffn1 = lax.psum_scatter(gr[0], SEQ, scatter_dimension=0, tiled=True)
    res = attend_back(1, ids, pieces, kept, prow, pcol, weights)
    d_all, bias, partials = res
    small1 = bias_rows(small, bias)
    summed, send = inward(partials)
    across = flip_x(send)
    d_all, send = after(d_all, send)
    gr = proj_grads(ids, u_all, d_all)
    across, gr = after(across, gr)
    r1a, r1b, r1k = gr
    d_upper = (d_first + summed + across.astype(f32)).astype(bf16)

    got_r1a = flip_y(r1a)
    u_all, kept, fwd, fwd_other, row_kept = saved[0]
    res = rows_back(0, ids, d_upper, row_kept, packs, own, other)
    res, got_r1a = after(res, got_r1a)
    d_first, pieces, (keep, send, small) = res[0], exchange(res[1:5]), res[5:]
    got_r1b = flip_y(r1b)
    gr = grads(0, ids, fwd, fwd_other, keep, core_flip(send))
    pieces, gr = after(pieces, gr)
    u0a, u0b, u0k, d0a, d0b, d0k = gr
    got_u0a, got_d0a, got_u0b, got_d0b = flip_y(u0a), flip_x(d0a), flip_y(u0b), flip_x(d0b)
    res = attend_back(0, ids, pieces, kept, prow, pcol, weights)
    (res, y_low, d_upper), (got_u0a, got_d0a, got_r1b, ffn1) = after(
        (res, y_low, d_upper), (got_u0a, got_d0a, got_r1b, ffn1)
    )
    ffn1 = lax.psum_scatter(ffn1, DP, scatter_dimension=0, tiled=True)[0]
    d_all, bias, partials = res
    small0 = bias_rows(small, bias)

    def step(flights):
        sends = lax.optimization_barrier([send for _, send in flights])
        return [flip(send) for (flip, _), send in zip(flights, sends)]

    def end(got, *more):
        return lax.optimization_barrier((got, more))

    swapped = partial(jnp.where, first)
    small_keep, small_send = swapped(small0, small1), swapped(small1, small0)
    small = small_keep + core_flip(small_send)
    r1 = plus(r1k, jnp.concatenate([got_r1a, got_r1b], axis=1)).astype(bf16)
    r1_send, r1_keep = cut(r1.reshape(2, 2, 2, share_w, -1), 2, low_z)
    summed, d_send = inward(partials)
    got = step([(flip_x, d_send), (flip_z1, r1_send), (flip_x, small)])
    gr = proj_grads(ids, u_all, d_all)
    got, ends = end(got, got_u0b, got_d0b, gr)
    got_u0b, got_d0b, (r0a, r0b, r0k) = ends

    d_lower = (d_first + summed + got[0].astype(f32)).astype(bf16)
    u0 = plus(u0k, jnp.concatenate([got_u0a, got_u0b], axis=1)).astype(bf16)
    u0_send, u0_keep = cut(u0.reshape(2, 2, 2, share_w, -1), 2, low_z)
    r1_send, r1_keep = cut(plus(r1_keep, got[1]).astype(bf16), 1, high_z)
    small = small + got[2]
    got = step([(flip_y, r0a), (flip_z1, u0_send), (flip_y, r0b), (flip_z2, r1_send)])
    d0 = plus(d0k, jnp.concatenate([got_d0a, got_d0b], axis=1)).astype(bf16)
    d0_send, d0_keep = cut(d0.reshape(2, 2, 2, share_f, part), 0, y)
    got, ends = end(got, d0_send)
    d0_send = ends[0]

    u0_send, u0_keep = cut(plus(u0_keep, got[1]).astype(bf16), 1, high_z)
    r0 = plus(r0k, jnp.concatenate([got[0], got[2]], axis=1)).astype(bf16)
    r0_send, r0_keep = cut(r0.reshape(2, 2, 2, share_w, -1), 2, low_z)
    r1_send, r1_keep = cut(plus(r1_keep, got[3]).astype(bf16), 0, x)
    got = step([(flip_z2, u0_send), (flip_y, d0_send), (flip_z1, r0_send), (flip_z1, small)])
    in0 = to_section(d_lower, 0)
    got, ends = end(got, in0, ffn1)
    (near0, far0), ffn1 = ends

    u0_send, u0_keep = cut(plus(u0_keep, got[0]).astype(bf16), 0, x)
    d0_send, d0_keep = cut(plus(d0_keep, got[1]).astype(bf16), 1, low_z)
    r0_send, r0_keep = cut(plus(r0_keep, got[2]).astype(bf16), 1, high_z)
    small = small + got[3]
    got = step([(flip_z2, r0_send), (flip_z1, d0_send), (flip_x, u0_send), (flip_y, small), (flip_x, r1_send)])
    upper = to_section(jnp.stack([y_low, d_upper]), 1)
    got, ends = end(got, upper)
    out1, (near1, far1) = [(ends[0][0][i], ends[0][1][i]) for i in range(2)]
    r1_got = got[4]

    few = 5 * share_w
    one0 = plus(u0_keep, got[2])
    d0_send, d0_keep = cut(plus(d0_keep, got[1]).astype(bf16), 0, high_z)
    r0_send, r0_keep = cut(plus(r0_keep, got[0]).astype(bf16), 0, x)
    small = small + got[3]
    got = step([(flip_z2, d0_send), (flip_x, r0_send), (flip_z2, small)])
    got = end(got)[0]
    two0 = plus(d0_keep, got[0])
    small = small + got[2]

    lower = jnp.concatenate(
        [one0[:, i * part : (i + 1) * part] for i in range(5)] + [two0], axis=0
    )
    upper = ffn1.astype(f32)
    ffn_keep, ffn_send = swapped(lower, upper), swapped(upper, lower)
    att0, att1 = jnp.stack([r0_keep, got[1]]), jnp.stack([r1_keep, r1_got])
    att_keep, att_send = swapped(att0, att1), swapped(att1, att0)
    ffn_got, att_got = core_flip(ffn_send), core_flip(att_send)
    grad_up, grad_out, grad_down, grad_local, grad_glob = assemble(
        ids, ffn_keep, ffn_got, att_keep, att_got, (share_w, share_f, ff, width)
    )

    at = q * dp + z
    piece = partial(lax.dynamic_slice_in_dim, axis=0)
    outs = (
        grad_local,
        jnp.stack([small[10], small[11]]),
        grad_glob,
        jnp.stack([small[12], small[13]]),
        grad_out,
        piece(small[4], at * share_w, share_w),
        jnp.stack([small[2], small[0]]),
        jnp.stack([small[3], small[1]]),
        grad_up,
        piece(small[6:10].reshape(ff), at * (ff // (4 * dp)), ff // (4 * dp)),
        grad_down,
        piece(small[5], at * share_w, share_w),
    )
    layer_outputs = by_micro(first, out0, out1, y)
    in_grads = by_micro(first, (near0, far0), (near1, far1), y)
    return (layer_outputs[None, :, None], in_grads[None, :, None]) + tuple(o[None] for o in outs)


def fits_two_chips(mesh, layer_in):
    sizes = dict(mesh.shape)
    micro, _, length, width = layer_in.shape
    dp = sizes[DP]
    return (
        sizes[SECTION] == 2
        and sizes[SEQ] == 4
        and micro == 2
        and dp == 4
        and length == 4 * HALF
        and width == 12 * HEAD
    )


def solution(mesh):
    in_specs = (
        P(None, DP, SEQ, None),
        P(None, DP, SEQ, None),
        P(None, DP, SEQ),
        P(None, DP, None),
        P(SECTION, None, None),
        P(SECTION, None, None),
        P(SECTION, None, None),
        P(SECTION, None, None),
        P(SECTION, None, None),
        P(SECTION, None),
        P(SECTION, None, None),
        P(SECTION, None, None),
        P(SECTION, None, None),
        P(SECTION, None),
        P(SECTION, None, None),
        P(SECTION, None),
    )
    out_specs = (
        P(SECTION, None, DP, SEQ, None),
        P(SECTION, None, DP, SEQ, None),
        P(SECTION, (SEQ, DP), None),
        P(SECTION, None, None),
        P(SECTION, (SEQ, DP), None),
        P(SECTION, None, None),
        P(SECTION, (SEQ, DP), None),
        P(SECTION, (SEQ, DP)),
        P(SECTION, None, None),
        P(SECTION, None, None),
        P(SECTION, (SEQ, DP), None),
        P(SECTION, (SEQ, DP)),
        P(SECTION, (SEQ, DP), None),
        P(SECTION, (SEQ, DP)),
    )

    def run(layer_in, *rest):
        body = two_chips if fits_two_chips(mesh, layer_in) else on_device
        return jax.shard_map(
            body, mesh=mesh, in_specs=in_specs, out_specs=out_specs, check_vma=False
        )(layer_in, *rest)

    return run
```

```python
from functools import partial
from types import SimpleNamespace

import jax
import jax.numpy as jnp
import numpy as np
from jax import lax
from jax.experimental import pallas as pl
from jax.experimental.pallas import tpu as pltpu
from jax.sharding import PartitionSpec as P

HEAD = 64
HALF = 256

SECTION, SEQ, DP = "section", "seq", "dp"
BOTH = (SECTION, SEQ)


far_below = -1e30
norm_eps = 1e-05


def padded(block, sides, width):
    for axis, dim in sides:
        count = lax.axis_size(axis)
        forward = [(i, i + 1) for i in range(count - 1)]
        backward = [(target, source) for source, target in forward]
        low = lax.ppermute(
            lax.slice_in_dim(block, block.shape[dim] - width, None, axis=dim), axis, forward
        )
        high = lax.ppermute(lax.slice_in_dim(block, 0, width, axis=dim), axis, backward)
        block = jnp.concatenate([low, block, high], axis=dim)
    return block


def joined(value, axis, join):
    pieces = jax.tree.map(lambda part: lax.all_gather(part, axis), value)
    head = jax.tree.map(lambda part: part[0], pieces)
    tail = jax.tree.map(lambda part: part[1:], pieces)
    running, _ = lax.scan(lambda running, piece: (join(running, piece), None), head, tail)
    return running


def shifted(shard, axis, by):
    length = lax.axis_size(axis)
    pairs = [(i, i + by) for i in range(length) if 0 <= i + by < length]
    return lax.ppermute(shard, axis, pairs)


def band_mask(first_row, row_count, reach_rows, length, positions, dilated):
    rows_at = first_row + jnp.arange(row_count)
    cols_at = first_row - reach_rows + jnp.arange(row_count + 2 * reach_rows)
    offset = cols_at[None, :] - rows_at[:, None]
    inside = (jnp.abs(offset) <= reach_rows) & (cols_at >= 0)[None, :] & (cols_at < length)[None, :]
    plain_key = jnp.logical_not(jnp.any(cols_at[:, None] == positions[None, :], axis=1))
    usable = inside & plain_key[None, :]
    even_gap = offset % 2 == 0
    return usable[None, :, :] & (jnp.logical_not(dilated)[:, None, None] | even_gap[None, :, :])


def layer_norm(values, gain_row, shift_row):
    center = values - jnp.mean(values, axis=-1, keepdims=True)
    scaled = lax.rsqrt(jnp.mean(center * center, axis=-1, keepdims=True) + norm_eps)
    unit_rows = center * scaled
    return (unit_rows * gain_row + shift_row, unit_rows, scaled)


def norm_back(unit_rows, scaled, gain_row, upstream):
    d_unit = upstream * gain_row
    inward = scaled * (
        d_unit
        - jnp.mean(d_unit, axis=-1, keepdims=True)
        - unit_rows * jnp.mean(d_unit * unit_rows, axis=-1, keepdims=True)
    )
    return (inward, jnp.sum(upstream * unit_rows, axis=0), jnp.sum(upstream, axis=0))


def join_stats(first_pair, second_pair):
    top_value = jnp.maximum(first_pair[0], second_pair[0])
    merged = first_pair[1] * jnp.exp(first_pair[0] - top_value) + second_pair[1] * jnp.exp(
        second_pair[0] - top_value
    )
    return (top_value, merged)


def forward_layer(source, positions, weights, first_row, length, dilated, active):
    local_w, local_b, glob_w, glob_b, out_w, out_b, gains, shifts, up_w, up_b, down_w, down_b = (
        weights
    )
    row_count = source.shape[0]
    model_width = source.shape[1]
    ff_width = up_w.shape[1]
    head_count = dilated.shape[0]
    head_size = model_width // head_count
    glob_count = positions.shape[0]
    score_scale = head_size ** (-0.5)
    owner_hit = (first_row + jnp.arange(row_count))[:, None] == positions[None, :]
    owner_low = owner_hit.astype(jnp.bfloat16)
    owner_full = owner_hit.astype(jnp.float32)
    is_global = jnp.any(owner_hit, axis=1)
    picked = jnp.einsum("cg,cd->gd", owner_low, source, preferred_element_type=jnp.float32)
    global_rows = lax.psum(picked.astype(jnp.bfloat16), SEQ)
    proj = jnp.dot(source, local_w, preferred_element_type=jnp.float32)
    queries = (proj[:, :model_width] + local_b[0]).astype(jnp.bfloat16)
    keys_low = proj[:, model_width : 2 * model_width].astype(jnp.bfloat16)
    values_low = (proj[:, 2 * model_width :] + local_b[1]).astype(jnp.bfloat16)
    gproj = jnp.dot(source, glob_w[:, model_width:], preferred_element_type=jnp.float32)
    gkeys = gproj[:, :model_width].astype(jnp.bfloat16)
    gvalues = (gproj[:, model_width:] + glob_b[1]).astype(jnp.bfloat16)
    gqueries = (
        jnp.dot(global_rows, glob_w[:, :model_width], preferred_element_type=jnp.float32)
        + glob_b[0]
    ).astype(jnp.bfloat16)
    side_proj = jnp.dot(global_rows, local_w[:, model_width:], preferred_element_type=jnp.float32)
    extra_keys = (
        side_proj[:, :model_width].astype(jnp.bfloat16).reshape(glob_count, head_count, head_size)
    )
    extra_values = (
        (side_proj[:, model_width:] + local_b[1])
        .astype(jnp.bfloat16)
        .reshape(glob_count, head_count, head_size)
    )
    key_value = jnp.concatenate([keys_low, values_low], axis=1)
    widened = padded(key_value, ((SEQ, 0),), HALF)
    reach_rows = (widened.shape[0] - row_count) // 2
    wide_keys = widened[:, :model_width].reshape(-1, head_count, head_size)
    wide_values = widened[:, model_width:].reshape(-1, head_count, head_size)
    allowed = band_mask(first_row, row_count, reach_rows, length, positions, dilated)
    queries_h = queries.reshape(row_count, head_count, head_size)
    band_score = (
        jnp.einsum("qhd,khd->hqk", queries_h, wide_keys, preferred_element_type=jnp.float32)
        * score_scale
    )
    band_score = jnp.where(allowed, band_score, far_below)
    toward = (
        jnp.einsum("qhd,ghd->hqg", queries_h, extra_keys, preferred_element_type=jnp.float32)
        * score_scale
    )
    peak_score = jnp.maximum(jnp.max(band_score, axis=-1), jnp.max(toward, axis=-1))[..., None]
    band_exp = jnp.exp(band_score - peak_score)
    toward_exp = jnp.exp(toward - peak_score)
    totals = jnp.sum(band_exp, axis=-1, keepdims=True) + jnp.sum(toward_exp, axis=-1, keepdims=True)
    band_full = band_exp / totals
    toward_full = toward_exp / totals
    band_prob = band_full.astype(jnp.bfloat16)
    toward_prob = toward_full.astype(jnp.bfloat16)
    local_ctx = jnp.einsum(
        "hqk,khd->qhd", band_prob, wide_values, preferred_element_type=jnp.float32
    ) + jnp.einsum("hqg,ghd->qhd", toward_prob, extra_values, preferred_element_type=jnp.float32)
    gqueries_h = gqueries.reshape(glob_count, head_count, head_size)
    gkeys_h = gkeys.reshape(row_count, head_count, head_size)
    gvalues_h = gvalues.reshape(row_count, head_count, head_size)
    spread = (
        jnp.einsum("ghd,khd->hgk", gqueries_h, gkeys_h, preferred_element_type=jnp.float32)
        * score_scale
    )
    part_peak = jnp.max(spread, axis=-1)
    part_total = jnp.sum(jnp.exp(spread - part_peak[..., None]), axis=-1)
    glob_peak, glob_total = joined((part_peak, part_total), SEQ, join_stats)
    glob_full = jnp.exp(spread - glob_peak[..., None]) / glob_total[..., None]
    glob_prob = glob_full.astype(jnp.bfloat16)
    part_ctx = jnp.einsum("hgk,khd->ghd", glob_prob, gvalues_h, preferred_element_type=jnp.float32)
    glob_ctx = lax.psum(part_ctx.reshape(glob_count, model_width), SEQ)
    placed_ctx = jnp.dot(owner_full, glob_ctx, precision=lax.Precision.HIGHEST)
    context = jnp.where(is_global[:, None], placed_ctx, local_ctx.reshape(row_count, model_width))
    context_low = context.astype(jnp.bfloat16)
    attn_out = jnp.dot(context_low, out_w, preferred_element_type=jnp.float32) + out_b
    mixed, unit_one, scale_one = layer_norm(
        source.astype(jnp.float32) + attn_out, gains[0], shifts[0]
    )

    def feed_forward(hidden_in):
        pre_act = (
            jnp.dot(hidden_in.astype(jnp.bfloat16), up_w, preferred_element_type=jnp.float32) + up_b
        )
        lifted = jax.nn.gelu(pre_act, approximate=False).astype(jnp.bfloat16)
        return (
            pre_act,
            lifted,
            jnp.dot(lifted, down_w, preferred_element_type=jnp.float32) + down_b,
        )

    def skip_block(hidden_in):
        return (
            jnp.zeros((row_count, ff_width), jnp.float32),
            jnp.zeros((row_count, ff_width), jnp.bfloat16),
            jnp.zeros((row_count, model_width), jnp.float32),
        )

    pre_act, activated, branch = lax.cond(active, feed_forward, skip_block, mixed)
    result, unit_two, scale_two = layer_norm(mixed + branch, gains[1], shifts[1])
    return SimpleNamespace(
        source=source,
        owner_low=owner_low,
        owner_full=owner_full,
        is_global=is_global,
        queries_h=queries_h,
        wide_keys=wide_keys,
        wide_values=wide_values,
        extra_keys=extra_keys,
        extra_values=extra_values,
        band_full=band_full,
        toward_full=toward_full,
        band_prob=band_prob,
        toward_prob=toward_prob,
        gqueries_h=gqueries_h,
        gkeys_h=gkeys_h,
        gvalues_h=gvalues_h,
        glob_full=glob_full,
        glob_prob=glob_prob,
        context_low=context_low,
        unit_one=unit_one,
        scale_one=scale_one,
        mixed=mixed,
        pre_act=pre_act,
        activated=activated,
        unit_two=unit_two,
        scale_two=scale_two,
        result=result,
        reach_rows=reach_rows,
        score_scale=score_scale,
    )


def ffn_back(kept_values, weights, upstream, active):
    local_w, local_b, glob_w, glob_b, out_w, out_b, gains, shifts, up_w, up_b, down_w, down_b = (
        weights
    )
    d_second, gain_two, shift_two = norm_back(
        kept_values.unit_two, kept_values.scale_two, gains[1], upstream
    )
    d_branch = d_second.astype(jnp.bfloat16)

    def ffn_work(operands):
        pre_act, d_out = operands
        d_lifted = jnp.einsum("cd,fd->cf", d_out, down_w, preferred_element_type=jnp.float32)
        gelu_vals, gelu_back = jax.vjp(partial(jax.nn.gelu, approximate=False), pre_act)
        d_pre = gelu_back(d_lifted)[0].astype(jnp.bfloat16)
        d_hidden = jnp.einsum("cf,df->cd", d_pre, up_w, preferred_element_type=jnp.float32)
        return (d_hidden, d_pre)

    def ffn_spare(operands):
        return (
            jnp.zeros(upstream.shape, jnp.float32),
            jnp.zeros((upstream.shape[0], up_w.shape[1]), jnp.bfloat16),
        )

    d_hidden, d_pre = lax.cond(active, ffn_work, ffn_spare, (kept_values.pre_act, d_branch))
    return (d_second + d_hidden, d_pre, d_branch, (gain_two, shift_two))


def attention_back(kept_values, weights, d_mixed):
    local_w, local_b, glob_w, glob_b, out_w, out_b, gains, shifts, up_w, up_b, down_w, down_b = (
        weights
    )
    row_count, model_width = kept_values.source.shape
    queries_h = kept_values.queries_h
    head_count, head_size = (queries_h.shape[1], queries_h.shape[2])
    glob_count = kept_values.owner_full.shape[1]
    reach_rows = kept_values.reach_rows
    score_scale = kept_values.score_scale
    d_first, gain_one, shift_one = norm_back(
        kept_values.unit_one, kept_values.scale_one, gains[0], d_mixed
    )
    d_attn = d_first.astype(jnp.bfloat16)
    d_context = jnp.einsum("ce,de->cd", d_attn, out_w, preferred_element_type=jnp.float32).astype(
        jnp.bfloat16
    )
    glob_part = jnp.einsum(
        "cg,cd->gd", kept_values.owner_low, d_context, preferred_element_type=jnp.float32
    )
    d_glob_ctx = lax.psum(glob_part.astype(jnp.bfloat16), SEQ)
    d_local = jnp.where(kept_values.is_global[:, None], jnp.zeros_like(d_context), d_context)
    d_local = d_local.reshape(row_count, head_count, head_size)
    band_full = kept_values.band_full
    toward_full = kept_values.toward_full
    d_band = jnp.einsum(
        "qhd,khd->hqk", d_local, kept_values.wide_values, preferred_element_type=jnp.float32
    )
    d_toward = jnp.einsum(
        "qhd,ghd->hqg", d_local, kept_values.extra_values, preferred_element_type=jnp.float32
    )
    inner_sum = jnp.sum(band_full * d_band, axis=-1) + jnp.sum(toward_full * d_toward, axis=-1)
    grad_band = (band_full * (d_band - inner_sum[..., None])).astype(jnp.bfloat16)
    grad_toward = (toward_full * (d_toward - inner_sum[..., None])).astype(jnp.bfloat16)
    d_queries = (
        jnp.einsum(
            "hqk,khd->qhd", grad_band, kept_values.wide_keys, preferred_element_type=jnp.float32
        )
        + jnp.einsum(
            "hqg,ghd->qhd",
            grad_toward,
            kept_values.extra_keys,
            preferred_element_type=jnp.float32,
        )
    ) * score_scale
    d_wide_keys = (
        jnp.einsum("hqk,qhd->khd", grad_band, queries_h, preferred_element_type=jnp.float32)
        * score_scale
    )
    d_wide_values = jnp.einsum(
        "hqk,qhd->khd", kept_values.band_prob, d_local, preferred_element_type=jnp.float32
    )
    d_extra_keys = (
        jnp.einsum("hqg,qhd->ghd", grad_toward, queries_h, preferred_element_type=jnp.float32)
        * score_scale
    )
    d_extra_values = jnp.einsum(
        "hqg,qhd->ghd", kept_values.toward_prob, d_local, preferred_element_type=jnp.float32
    )
    glob_full = kept_values.glob_full
    d_glob_h = d_glob_ctx.reshape(glob_count, head_count, head_size)
    d_spread = jnp.einsum(
        "ghd,khd->hgk", d_glob_h, kept_values.gvalues_h, preferred_element_type=jnp.float32
    )
    part_inner = jnp.sum(glob_full * d_spread, axis=-1)
    glob_inner, sum_extra_keys, sum_extra_values = (
        lax.psum(part_inner.astype(jnp.bfloat16), SEQ).astype(jnp.float32),
        lax.psum(d_extra_keys.reshape(glob_count, model_width).astype(jnp.bfloat16), SEQ).astype(
            jnp.float32
        ),
        lax.psum(
            d_extra_values.reshape(glob_count, model_width).astype(jnp.bfloat16), SEQ
        ).astype(jnp.float32),
    )
    grad_spread = (glob_full * (d_spread - glob_inner[..., None])).astype(jnp.bfloat16)
    part_query = (
        jnp.einsum(
            "hgk,khd->ghd", grad_spread, kept_values.gkeys_h, preferred_element_type=jnp.float32
        )
        * score_scale
    )
    d_gkeys = (
        jnp.einsum(
            "hgk,ghd->khd",
            grad_spread,
            kept_values.gqueries_h,
            preferred_element_type=jnp.float32,
        )
        * score_scale
    )
    d_gvalues = jnp.einsum(
        "hgk,ghd->khd", kept_values.glob_prob, d_glob_h, preferred_element_type=jnp.float32
    )
    d_gqueries = lax.psum(
        part_query.reshape(glob_count, model_width).astype(jnp.bfloat16), SEQ
    ).astype(jnp.float32)
    d_wide = jnp.concatenate(
        [d_wide_keys.reshape(-1, model_width), d_wide_values.reshape(-1, model_width)], axis=1
    )
    rim_grads = jnp.concatenate([d_wide[:reach_rows], d_wide[reach_rows + row_count :]], axis=0)
    incoming = padded(rim_grads.astype(jnp.bfloat16), ((SEQ, 0),), HALF).astype(rim_grads.dtype)
    own_part = (
        d_wide[reach_rows : reach_rows + row_count]
        + incoming[:reach_rows]
        + incoming[3 * reach_rows :]
    )
    owner_full = kept_values.owner_full
    d_keys_low = (
        own_part[:, :model_width]
        + jnp.dot(owner_full, sum_extra_keys, precision=lax.Precision.HIGHEST)
    ).astype(jnp.bfloat16)
    d_values_low = (
        own_part[:, model_width:]
        + jnp.dot(owner_full, sum_extra_values, precision=lax.Precision.HIGHEST)
    ).astype(jnp.bfloat16)
    d_queries_low = d_queries.reshape(row_count, model_width).astype(jnp.bfloat16)
    d_proj = jnp.concatenate([d_queries_low, d_keys_low, d_values_low], axis=1)
    d_gq_rows = jnp.dot(owner_full, d_gqueries, precision=lax.Precision.HIGHEST).astype(
        jnp.bfloat16
    )
    d_gproj = jnp.concatenate(
        [
            d_gq_rows,
            d_gkeys.reshape(row_count, model_width).astype(jnp.bfloat16),
            d_gvalues.reshape(row_count, model_width).astype(jnp.bfloat16),
        ],
        axis=1,
    )
    d_source = (
        d_first
        + jnp.einsum("ce,de->cd", d_proj, local_w, preferred_element_type=jnp.float32)
        + jnp.einsum("ce,de->cd", d_gproj, glob_w, preferred_element_type=jnp.float32)
    )
    return (d_source, d_proj, d_gproj, d_attn, (gain_one, shift_one))


def ffn_terms(mixed_buf, pre_buf, act_buf, branch_buf, count):
    return (
        jnp.einsum(
            "mcd,mcf->df", mixed_buf[:count], pre_buf[:count], preferred_element_type=jnp.float32
        ),
        jnp.sum(pre_buf[:count].astype(jnp.float32), axis=(0, 1)),
        jnp.einsum(
            "mcf,mcd->fd", act_buf[:count], branch_buf[:count], preferred_element_type=jnp.float32
        ),
        jnp.sum(branch_buf[:count].astype(jnp.float32), axis=(0, 1)),
    )


def on_device(
    layer_in,
    cotangent,
    masked_rows,
    global_positions,
    local_weight,
    local_bias,
    global_weight,
    global_bias,
    out_weight,
    out_bias,
    norm_gain,
    norm_shift,
    up_weight,
    up_bias,
    down_weight,
    down_bias,
):
    weights = (
        local_weight[0],
        local_bias[0],
        global_weight[0],
        global_bias[0],
        out_weight[0],
        out_bias[0],
        norm_gain[0],
        norm_shift[0],
        up_weight[0],
        up_bias[0],
        down_weight[0],
        down_bias[0],
    )
    section_index = lax.axis_index(SECTION)
    seq_index = lax.axis_index(SEQ)
    micro_count = layer_in.shape[0]
    row_count = layer_in.shape[2]
    model_width = layer_in.shape[3]
    ff_width = up_weight.shape[2]
    length = row_count * lax.axis_size(SEQ)
    first_row = seq_index * row_count
    head_count = model_width // HEAD
    dilated = (jnp.arange(head_count) >= head_count - 2) & (section_index == 1)
    kept_inputs = jnp.zeros((micro_count, row_count, model_width), jnp.bfloat16)
    outputs = jnp.zeros_like(kept_inputs)
    arrived = jnp.zeros((row_count, model_width), jnp.bfloat16)
    for step_index in range(micro_count + 1):
        micro_index = step_index - section_index
        in_range = (micro_index >= 0) & (micro_index < micro_count)
        slot_index = jnp.clip(micro_index, 0, micro_count - 1)
        fresh = lax.dynamic_index_in_dim(layer_in, slot_index, 0, keepdims=False)[0]
        source = jnp.where(section_index == 0, fresh, arrived)
        positions = lax.dynamic_index_in_dim(global_positions, slot_index, 0, keepdims=False)[0]
        kept_values = forward_layer(
            source, positions, weights, first_row, length, dilated, in_range
        )
        result = kept_values.result.astype(jnp.bfloat16)
        kept_inputs = jnp.where(
            in_range,
            lax.dynamic_update_index_in_dim(kept_inputs, source, slot_index, 0),
            kept_inputs,
        )
        outputs = jnp.where(
            in_range, lax.dynamic_update_index_in_dim(outputs, result, slot_index, 0), outputs
        )
        if step_index < micro_count:
            arrived = shifted(result, SECTION, 1)
    slots = micro_count + 1
    proj_buf = jnp.zeros((slots, row_count, 3 * model_width), jnp.bfloat16)
    gproj_buf = jnp.zeros_like(proj_buf)
    ctx_buf = jnp.zeros((slots, row_count, model_width), jnp.bfloat16)
    attn_buf = jnp.zeros_like(ctx_buf)
    mixed_buf = jnp.zeros_like(ctx_buf)
    branch_buf = jnp.zeros_like(ctx_buf)
    pre_buf = jnp.zeros((slots, row_count, ff_width), jnp.bfloat16)
    act_buf = jnp.zeros_like(pre_buf)
    gain_total = jnp.zeros((2, model_width), jnp.float32)
    shift_total = jnp.zeros((2, model_width), jnp.float32)
    back_arrived = jnp.zeros((row_count, model_width), jnp.bfloat16)
    in_grads = jnp.zeros_like(kept_inputs)
    for step_index in range(micro_count + 1):
        micro_index = step_index - 1 + section_index
        in_range = (micro_index >= 0) & (micro_index < micro_count)
        slot_index = jnp.clip(micro_index, 0, micro_count - 1)
        store = jnp.where(in_range, micro_index, micro_count)
        source = lax.dynamic_index_in_dim(kept_inputs, slot_index, 0, keepdims=False)
        positions = lax.dynamic_index_in_dim(global_positions, slot_index, 0, keepdims=False)[0]
        picked_rows = lax.dynamic_index_in_dim(masked_rows, slot_index, 0, keepdims=False)[0]
        picked_grads = lax.dynamic_index_in_dim(cotangent, slot_index, 0, keepdims=False)[0]
        row_hit = ((first_row + jnp.arange(row_count))[:, None] == picked_rows[None, :]).astype(
            jnp.bfloat16
        )
        placed = jnp.dot(row_hit, picked_grads, preferred_element_type=jnp.float32)
        upstream = jnp.where(section_index == 1, placed, back_arrived.astype(jnp.float32))
        kept_values = forward_layer(
            source, positions, weights, first_row, length, dilated, in_range
        )
        d_mixed, d_pre, d_branch, norm_two = ffn_back(kept_values, weights, upstream, in_range)
        mixed_buf = lax.dynamic_update_index_in_dim(
            mixed_buf, kept_values.mixed.astype(jnp.bfloat16), store, 0
        )
        pre_buf = lax.dynamic_update_index_in_dim(pre_buf, d_pre, store, 0)
        act_buf = lax.dynamic_update_index_in_dim(act_buf, kept_values.activated, store, 0)
        branch_buf = lax.dynamic_update_index_in_dim(branch_buf, d_branch, store, 0)
        d_source, d_proj, d_gproj, d_attn, norm_one = attention_back(kept_values, weights, d_mixed)
        proj_buf = lax.dynamic_update_index_in_dim(proj_buf, d_proj, store, 0)
        gproj_buf = lax.dynamic_update_index_in_dim(gproj_buf, d_gproj, store, 0)
        ctx_buf = lax.dynamic_update_index_in_dim(ctx_buf, kept_values.context_low, store, 0)
        attn_buf = lax.dynamic_update_index_in_dim(attn_buf, d_attn, store, 0)
        gain_total = gain_total + jnp.where(in_range, jnp.stack([norm_one[0], norm_two[0]]), 0.0)
        shift_total = shift_total + jnp.where(in_range, jnp.stack([norm_one[1], norm_two[1]]), 0.0)
        d_low = d_source.astype(jnp.bfloat16)
        in_grads = jnp.where(
            in_range, lax.dynamic_update_index_in_dim(in_grads, d_low, slot_index, 0), in_grads
        )
        if step_index < micro_count:
            back_arrived = shifted(d_low, SECTION, -1)
    used_proj = proj_buf[:micro_count]
    used_gproj = gproj_buf[:micro_count]
    grad_local = jnp.einsum(
        "mcd,mce->de", kept_inputs, used_proj, preferred_element_type=jnp.float32
    )
    grad_glob = jnp.einsum(
        "mcd,mce->de", kept_inputs, used_gproj, preferred_element_type=jnp.float32
    )
    grad_out = jnp.einsum(
        "mcd,mce->de",
        ctx_buf[:micro_count],
        attn_buf[:micro_count],
        preferred_element_type=jnp.float32,
    )
    grad_out_b = jnp.sum(attn_buf[:micro_count].astype(jnp.float32), axis=(0, 1))
    local_b_grad = jnp.stack(
        [
            jnp.sum(used_proj[:, :, :model_width].astype(jnp.float32), axis=(0, 1)),
            jnp.sum(used_proj[:, :, 2 * model_width :].astype(jnp.float32), axis=(0, 1)),
        ]
    )
    glob_b_grad = jnp.stack(
        [
            jnp.sum(used_gproj[:, :, :model_width].astype(jnp.float32), axis=(0, 1)),
            jnp.sum(used_gproj[:, :, 2 * model_width :].astype(jnp.float32), axis=(0, 1)),
        ]
    )
    small_sums = lax.psum((local_b_grad, glob_b_grad, gain_total, shift_total), (SEQ, DP))
    ffn_parts = ffn_terms(mixed_buf, pre_buf, act_buf, branch_buf, micro_count)
    large_sums = (
        lax.psum_scatter(grad_local, (SEQ, DP), scatter_dimension=0, tiled=True),
        lax.psum_scatter(grad_glob, (SEQ, DP), scatter_dimension=0, tiled=True),
        lax.psum_scatter(grad_out, (SEQ, DP), scatter_dimension=0, tiled=True),
        lax.psum_scatter(grad_out_b, (SEQ, DP), scatter_dimension=0, tiled=True),
        lax.psum_scatter(ffn_parts[0], (SEQ, DP), scatter_dimension=0, tiled=True),
        lax.psum_scatter(ffn_parts[1], (SEQ, DP), scatter_dimension=0, tiled=True),
        lax.psum_scatter(ffn_parts[2], (SEQ, DP), scatter_dimension=0, tiled=True),
        lax.psum_scatter(ffn_parts[3], (SEQ, DP), scatter_dimension=0, tiled=True),
    )
    summed = (
        large_sums[0],
        small_sums[0],
        large_sums[1],
        small_sums[1],
        large_sums[2],
        large_sums[3],
        small_sums[2],
        small_sums[3],
        large_sums[4],
        large_sums[5],
        large_sums[6],
        large_sums[7],
    )
    return (outputs[None, :, None], in_grads[None, :, None]) + tuple(
        (member[None] for member in summed)
    )


bf16 = jnp.bfloat16
f32 = jnp.float32
VMEM_BYTES = 50 * 1024 * 1024


def nn(a, b):
    return jnp.dot(a, b, preferred_element_type=f32)


def nt(a, b):
    return lax.dot_general(a, b, (((1,), (1,)), ((), ())), preferred_element_type=f32)


def tn(a, b):
    return lax.dot_general(a, b, (((0,), (0,)), ((), ())), preferred_element_type=f32)


def owner_rows(prow, chunk, rows):
    at = lax.broadcasted_iota(jnp.int32, (rows, prow.shape[1]), 0) + chunk * rows
    return (at == prow[...]).astype(f32)


def owner_cols(pcol, chunk, rows):
    at = lax.broadcasted_iota(jnp.int32, (pcol.shape[0], rows), 1) + chunk * rows
    return (at == pcol[...]).astype(f32)


def is_dilated(layer, group, h):
    return ((3 * group + h >= 10) & (layer == 1)).astype(jnp.int32)


def band_masks(mask_s, dilated, rows):
    row = lax.broadcasted_iota(jnp.int32, (rows, rows), 0)
    col = lax.broadcasted_iota(jnp.int32, (rows, rows), 1)
    odd = ((row + col) % 2).astype(f32)
    level = odd * (dilated.astype(f32) * far_below)
    mask_s[0] = jnp.where(row >= col, level, far_below)
    mask_s[1] = level
    mask_s[2] = jnp.where(row <= col, level, far_below)


def neighbours(block, count):
    return [b for b in (block - 1, block, block + 1) if 0 <= b < count]


def cost(us):
    return pl.CostEstimate(
        flops=int(us * 1e9), transcendentals=0, bytes_accessed=int(us * 3.5e6)
    )


def start_all(copies):
    for copy in copies:
        copy.start()
    return copies


def wait_all(copies):
    for copy in copies:
        copy.wait()


def moves(pairs, sems, at=0):
    return [pltpu.make_async_copy(a, b, sems.at[at + i]) for i, (a, b) in enumerate(pairs)]


def choose(flag, first, second, target, sem):
    for value, source in ((0, first), (1, second)):

        @pl.when(flag == value)
        def _(source=source):
            pltpu.make_async_copy(source, target, sem).start()

    return pltpu.make_async_copy(first, target, sem)


def prepare_kernel(
    ids, lw, gw, lb, gb, ob, ng, ns, db, ub, own_o, send_o, pack_o, win_s, sems
):
    width = lw.shape[0]
    hw = width // 4
    sources = [(lw, 0), (lw, 1), (lw, 2), (gw, 1), (gw, 2), (gw, 0)]
    copies = []
    for t, group in enumerate((ids[1], ids[0])):
        for i, (ref, part) in enumerate(sources):
            start = pl.multiple_of(part * width + 128 * ((3 * group) // 2), 128)
            copies.append(
                pltpu.make_async_copy(
                    ref.at[:, pl.ds(start, 256)], win_s.at[t, i], sems.at[6 * t + i]
                )
            )
            copies[-1].start()
    pack_o[...] = jnp.zeros(pack_o.shape, f32)
    at = 0
    for ref in (lb, gb, ob, ng, ns, db):
        pack_o[at : at + ref.shape[0], :] = ref[...].astype(f32)
        at += ref.shape[0]
    for i in range(ub.shape[1] // width):
        pack_o[at + i : at + i + 1, :] = ub[:, i * width : (i + 1) * width].astype(f32)
    for t, target in enumerate((send_o, own_o)):
        for i in range(6):
            copies[6 * t + i].wait()
        for odd in range(2):

            @pl.when(ids[6] == odd)
            def _(t=t, target=target, odd=odd):
                parts = [win_s[t, i][:, 64 * odd : 64 * odd + hw] for i in range(6)]
                target[...] = jnp.concatenate(parts, axis=1)


def prepare(ids, local_w, global_w, rows):
    width = local_w.shape[0]
    vm = pl.BlockSpec(memory_space=pltpu.VMEM)
    hbm = pl.BlockSpec(memory_space=pl.ANY)
    chosen = jax.ShapeDtypeStruct((width, 6 * width // 4), bf16)
    return pl.pallas_call(
        prepare_kernel,
        out_shape=[chosen, chosen, jax.ShapeDtypeStruct((16, width), f32)],
        in_specs=[pl.BlockSpec(memory_space=pltpu.SMEM), hbm, hbm] + [vm] * 7,
        out_specs=[vm] * 3,
        scratch_shapes=[
            pltpu.VMEM((2, 6, width, 256), bf16),
            pltpu.SemaphoreType.DMA((12,)),
        ],
        compiler_params=pltpu.CompilerParams(vmem_limit_bytes=VMEM_BYTES),
        cost_estimate=cost(3),
        name="prepare",
    )(ids, local_w, global_w, *rows)


def attend_kernel(layer, *refs):
    count = 4
    sources = 7 if layer == 0 else 4
    ids, parts, refs = refs[0], refs[1 : 1 + sources], refs[1 + sources :]
    (
        w_a, w_b, pack_a, pack_b, prow, pcol,
        c0, c1, c2, c3, u_o, own_o, q_o, k_o, v_o, gk_o, gv_o, gq_o, kg_o, vg_o, lse_o,
        w_s, sem, vt_s, mask_s, ctx_s, gctx_s,
    ) = refs
    rows = c0.shape[0]
    heads = q_o.shape[0]
    hw = heads * HEAD
    scale = HEAD ** (-0.5)
    glob = prow.shape[1]
    group, core = ids[0], ids[4]
    w_copy = choose((core != layer).astype(jnp.int32), w_a, w_b, w_s, sem)
    if layer == 0:
        block = parts[0]
        half = rows // 2
        u_o[pl.ds(pl.multiple_of((2 * ids[5] + ids[6]) * rows, rows), rows), :] = block[ids[5]]
        places = (
            2 * ids[5] + 1 - ids[6],
            2 * (1 - ids[5]) + ids[6],
            2 * (1 - ids[5]) + 1 - ids[6],
        )
        for i, place in enumerate(places):
            for part, side in ((parts[1 + i], core), (parts[4 + i], 1 - core)):
                at = pl.multiple_of(place * rows + side * half, half)
                u_o[pl.ds(at, half), :] = part[...]
    else:
        for r in range(count):
            u_o[pl.ds(pl.multiple_of(ids[r] * rows, rows), rows), :] = parts[r][...]
    own_o[...] = u_o[pl.ds(pl.multiple_of(group * rows, rows), rows), :]
    pack = jnp.where(core == layer, pack_a[...], pack_b[...])[:4]
    hb = pack[:, :hw]
    for i in range(1, 4):
        hb = jnp.where(group == i, pack[:, i * hw : (i + 1) * hw], hb)
    kg_all = jnp.zeros((glob, hw), f32)
    vg_all = jnp.zeros((glob, hw), f32)
    ug_all = jnp.zeros((glob, u_o.shape[1]), f32)
    first = lax.broadcasted_iota(jnp.int32, (rows, HEAD), 1) == 0
    w_copy.wait()
    w = w_s
    for chunk in range(count):
        at = slice(chunk * rows, (chunk + 1) * rows)
        x = u_o[at, :]
        p = nn(x, w[:, : 5 * hw])
        queries = (p[:, :hw] + hb[0:1, :]).astype(bf16).astype(f32) * scale
        keys = p[:, hw : 2 * hw]
        values = p[:, 2 * hw : 3 * hw] + hb[1:2, :]
        gkeys = p[:, 3 * hw : 4 * hw]
        gvalues = p[:, 4 * hw : 5 * hw] + hb[3:4, :]
        is_global = jnp.max(owner_rows(prow, chunk, rows), axis=1, keepdims=True)
        tail_k = jnp.where(first, is_global * far_below, 0.0)
        tail_q = jnp.where(first, 1.0, 0.0)
        for h in range(heads):
            cut = slice(HEAD * h, HEAD * h + HEAD)
            q_o[h, at, :] = jnp.concatenate([queries[:, cut], tail_q], axis=1).astype(bf16)
            k_o[h, at, :] = jnp.concatenate([keys[:, cut], tail_k], axis=1).astype(bf16)
            v_o[h, at, :] = values[:, cut].astype(bf16)
            gk_o[h, at, :] = gkeys[:, cut].astype(bf16)
            gv_o[h, at, :] = gvalues[:, cut].astype(bf16)
            vt_s[h, chunk] = values[:, cut].T.astype(bf16)
        hit = owner_cols(pcol, chunk, rows).astype(bf16)
        kg_all += nn(hit, keys.astype(bf16))
        vg_all += nn(hit, values.astype(bf16))
        ug_all += nn(hit, x)
    gq_all = (nn(ug_all.astype(bf16), w[:, 5 * hw :]) + hb[2:3, :]).astype(bf16).astype(f32) * scale
    none = jnp.zeros((glob, HEAD), f32)
    for h in range(heads):
        cut = slice(HEAD * h, HEAD * h + HEAD)
        gq_o[h] = gq_all[:, cut].astype(bf16)
        kg_o[h] = jnp.concatenate([kg_all[:, cut], none], axis=1).astype(bf16)
        vg_o[h] = vg_all[:, cut].astype(bf16)

    def head(h, carry):
        band_masks(mask_s, is_dilated(layer, group, h), rows)
        kg = kg_o[h]
        vgt = vg_o[h].astype(f32).T.astype(bf16)
        for qb in range(count):
            q = q_o[h, qb * rows : (qb + 1) * rows, :]
            near = neighbours(qb, count)
            scores = [
                nt(k_o[h, kb * rows : (kb + 1) * rows, :], q) + mask_s[kb - qb + 1] for kb in near
            ]
            side = nt(kg, q)
            peak = jnp.max(side, axis=0, keepdims=True)
            for s in scores:
                peak = jnp.maximum(peak, jnp.max(s, axis=0, keepdims=True))
            side = jnp.exp(side - peak)
            scores = [jnp.exp(s - peak) for s in scores]
            total = jnp.sum(side, axis=0, keepdims=True)
            for s in scores:
                total += jnp.sum(s, axis=0, keepdims=True)
            inverse = 1.0 / total
            ctx = nn(vgt, (side * inverse).astype(bf16))
            for kb, s in zip(near, scores):
                ctx += nn(vt_s[h, kb], (s * inverse).astype(bf16))
            ctx_s[h, qb * rows : (qb + 1) * rows, :] = ctx.T
            lse_o[h, qb : qb + 1, :] = peak + jnp.log(total)
        spread = nt(gq_o[h], gk_o[h])
        e = jnp.exp(spread - jnp.max(spread, axis=1, keepdims=True))
        prob = (e / jnp.sum(e, axis=1, keepdims=True)).astype(bf16)
        gctx_s[h] = nn(prob, gv_o[h])
        return carry

    lax.fori_loop(0, heads, head, 0)
    gctx = jnp.concatenate([gctx_s[h] for h in range(heads)], axis=1).astype(bf16)
    for r, c_o in enumerate((c0, c1, c2, c3)):
        chunk = ids[r]
        at = pl.ds(pl.multiple_of(chunk * rows, rows), rows)
        hit = owner_rows(prow, chunk, rows)
        placed = nn(hit.astype(bf16), gctx)
        local = jnp.concatenate([ctx_s[h, at, :] for h in range(heads)], axis=1)
        c_o[...] = jnp.where(jnp.max(hit, axis=1, keepdims=True) > 0, placed, local).astype(bf16)


def attend(layer, ids, parts, weights, packs, prow, pcol):
    width = weights[0].shape[0]
    hw = weights[0].shape[1] // 6
    heads = hw // HEAD
    glob = prow.shape[1]
    rows = HALF
    full = 4 * rows
    sds = jax.ShapeDtypeStruct
    outs = [sds((rows, hw), bf16)] * 4 + [
        sds((full, width), bf16),
        sds((rows, width), bf16),
        sds((heads, full, 2 * HEAD), bf16),
        sds((heads, full, 2 * HEAD), bf16),
        sds((heads, full, HEAD), bf16),
        sds((heads, full, HEAD), bf16),
        sds((heads, full, HEAD), bf16),
        sds((heads, glob, HEAD), bf16),
        sds((heads, glob, 2 * HEAD), bf16),
        sds((heads, glob, HEAD), bf16),
        sds((heads, 4, rows), f32),
    ]
    vm = pl.BlockSpec(memory_space=pltpu.VMEM)
    hbm = pl.BlockSpec(memory_space=pl.ANY)
    res = pl.pallas_call(
        partial(attend_kernel, layer),
        out_shape=outs,
        in_specs=[pl.BlockSpec(memory_space=pltpu.SMEM)]
        + [vm] * len(parts)
        + [hbm] * 2
        + [vm] * 4,
        out_specs=[vm] * len(outs),
        scratch_shapes=[
            pltpu.VMEM(weights[0].shape, bf16),
            pltpu.SemaphoreType.DMA,
            pltpu.VMEM((heads, 4, HEAD, rows), bf16),
            pltpu.VMEM((3, rows, rows), f32),
            pltpu.VMEM((heads, full, HEAD), f32),
            pltpu.VMEM((heads, glob, HEAD), f32),
        ],
        compiler_params=pltpu.CompilerParams(vmem_limit_bytes=VMEM_BYTES),
        cost_estimate=cost(14),
        name="attend",
    )(ids, *parts, *weights, *packs, prow, pcol)
    return res[:4], res[4], res[5], res[6:]


def attend_back_kernel(
    layer, ids, d0, d1, d2, d3, q, k, v, gk, gv, gq, kg, vg, lse, prow, pcol, w_a, w_b,
    d_o, bias_o, p0, p1, p2, p3,
    w_s, sem, mask_s, do_s, dog_s, dq_s, dk_s, dv_s, dkg_s, dvg_s, dgk_s, dgv_s, dgq_s,
):
    rows = d0.shape[0]
    heads = q.shape[0]
    count = 4
    scale = HEAD ** (-0.5)
    glob = prow.shape[1]
    w_copy = choose((ids[4] != layer).astype(jnp.int32), w_a, w_b, w_s, sem)
    dg_all = jnp.zeros((glob, heads * HEAD), f32)
    for r, d in enumerate((d0, d1, d2, d3)):
        chunk = ids[r]
        at = pl.ds(pl.multiple_of(chunk * rows, rows), rows)
        dx = d[...]
        dg_all += nn(owner_cols(pcol, chunk, rows).astype(bf16), dx)
        is_global = jnp.max(owner_rows(prow, chunk, rows), axis=1, keepdims=True)
        local = jnp.where(is_global > 0, 0.0, dx.astype(f32))
        for h in range(heads):
            do_s[h, at, :] = local[:, HEAD * h : HEAD * h + HEAD].astype(bf16)
    for h in range(heads):
        dog_s[h] = dg_all[:, HEAD * h : HEAD * h + HEAD].astype(bf16)

    def head(h, carry):
        band_masks(mask_s, is_dilated(layer, ids[0], h), rows)
        kgh = kg[h]
        vgh = vg[h]
        kgt = kgh[:, :HEAD].astype(f32).T.astype(bf16)
        kt = [
            k[h, b * rows : (b + 1) * rows, :][:, :HEAD].astype(f32).T.astype(bf16)
            for b in range(count)
        ]
        dk = [jnp.zeros((rows, 2 * HEAD), f32) for _ in range(count)]
        dv = [jnp.zeros((rows, HEAD), f32) for _ in range(count)]
        dkg = jnp.zeros((glob, 2 * HEAD), f32)
        dvg = jnp.zeros((glob, HEAD), f32)
        for qb in range(count):
            span = slice(qb * rows, (qb + 1) * rows)
            qq = q[h, span, :]
            do = do_s[h, span, :]
            row = lse[h, qb : qb + 1, :]
            near = neighbours(qb, count)
            prob = [
                jnp.exp(nt(k[h, b * rows : (b + 1) * rows, :], qq) + mask_s[b - qb + 1] - row)
                for b in near
            ]
            side = jnp.exp(nt(kgh, qq) - row)
            dprob = [nt(v[h, b * rows : (b + 1) * rows, :], do) for b in near]
            dside = nt(vgh, do)
            inner = jnp.sum(side * dside, axis=0, keepdims=True)
            for p, dp in zip(prob, dprob):
                inner += jnp.sum(p * dp, axis=0, keepdims=True)
            ds = (side * (dside - inner)).astype(bf16)
            dvg += nn(side.astype(bf16), do)
            dkg += nn(ds, qq)
            dq = nn(kgt, ds)
            for b, p, dp in zip(near, prob, dprob):
                ds = (p * (dp - inner)).astype(bf16)
                dv[b] += nn(p.astype(bf16), do)
                dk[b] += nn(ds, qq)
                dq += nn(kt[b], ds)
            dq_s[h, span, :] = dq.T * scale
        for b in range(count):
            dk_s[h, b * rows : (b + 1) * rows, :] = dk[b][:, :HEAD]
            dv_s[h, b * rows : (b + 1) * rows, :] = dv[b]
        dkg_s[h] = dkg[:, :HEAD]
        dvg_s[h] = dvg
        spread = nt(gk[h], gq[h])
        e = jnp.exp(spread - jnp.max(spread, axis=0, keepdims=True))
        p = e / jnp.sum(e, axis=0, keepdims=True)
        dog = dog_s[h]
        dp = nt(gv[h], dog)
        ds = (p * (dp - jnp.sum(p * dp, axis=0, keepdims=True))).astype(bf16)
        dgv_s[h] = nn(p.astype(bf16), dog)
        dgk_s[h] = nn(ds, gq[h])
        dgq_s[h] = tn(ds, gk[h]) * scale
        return carry

    lax.fori_loop(0, heads, head, 0)

    def wide(ref, at=None):
        parts = [ref[h] if at is None else ref[h, at, :] for h in range(heads)]
        return jnp.concatenate(parts, axis=1)

    dkg_all = wide(dkg_s).astype(bf16)
    dvg_all = wide(dvg_s).astype(bf16)
    dgq_all = wide(dgq_s).astype(bf16)
    sums = [jnp.zeros((1, heads * HEAD), f32) for _ in range(4)]
    w_copy.wait()
    for r, p_o in enumerate((p0, p1, p2, p3)):
        chunk = ids[r]
        at = pl.ds(pl.multiple_of(chunk * rows, rows), rows)
        hit = owner_rows(prow, chunk, rows).astype(bf16)
        dq = wide(dq_s, at)
        dk = wide(dk_s, at) + nn(hit, dkg_all)
        dv = wide(dv_s, at) + nn(hit, dvg_all)
        dgk = wide(dgk_s, at)
        dgv = wide(dgv_s, at)
        dgq = nn(hit, dgq_all)
        joint = jnp.concatenate([dq, dk, dv, dgk, dgv, dgq], axis=1).astype(bf16)
        d_o[at, :] = joint
        p_o[...] = nt(joint, w_s[...]).astype(p_o.dtype)
        for i, part in enumerate((dq, dv, dgq, dgv)):
            sums[i] += jnp.sum(part, axis=0, keepdims=True)
    bias_o[...] = jnp.concatenate(sums, axis=0)


def attend_back(layer, ids, pieces, kept, prow, pcol, weights):
    rows, hw = pieces[0].shape
    width = weights[0].shape[0]
    heads = hw // HEAD
    glob = prow.shape[1]
    full = 4 * rows
    vm = pl.BlockSpec(memory_space=pltpu.VMEM)
    hbm = pl.BlockSpec(memory_space=pl.ANY)
    big = (heads, full, HEAD)
    small = (heads, glob, HEAD)
    res = pl.pallas_call(
        partial(attend_back_kernel, layer),
        out_shape=[
            jax.ShapeDtypeStruct((full, 6 * hw), bf16),
            jax.ShapeDtypeStruct((4, hw), f32),
        ]
        + [jax.ShapeDtypeStruct((rows, width), t) for t in (f32, bf16, f32, bf16)],
        in_specs=[pl.BlockSpec(memory_space=pltpu.SMEM)] + [vm] * 15 + [hbm] * 2,
        out_specs=[vm] * 6,
        scratch_shapes=[
            pltpu.VMEM(weights[0].shape, bf16),
            pltpu.SemaphoreType.DMA,
            pltpu.VMEM((3, rows, rows), f32),
            pltpu.VMEM(big, bf16),
            pltpu.VMEM(small, bf16),
            pltpu.VMEM(big, f32),
            pltpu.VMEM(big, f32),
            pltpu.VMEM(big, f32),
            pltpu.VMEM(small, f32),
            pltpu.VMEM(small, f32),
            pltpu.VMEM(big, f32),
            pltpu.VMEM(big, f32),
            pltpu.VMEM(small, f32),
        ],
        compiler_params=pltpu.CompilerParams(vmem_limit_bytes=VMEM_BYTES),
        cost_estimate=cost(18),
        name="attend_back",
    )(ids, *pieces, *kept, prow, pcol, *weights)
    return res[0], res[1], res[2:]


def fetch(first, second, use_second, pairs, sems):
    for flag, source in ((0, first), (1, second)):

        @pl.when(use_second.astype(jnp.int32) == flag)
        def _(source=source):
            for i, (pick, target) in enumerate(pairs):
                pltpu.make_async_copy(pick(source), target, sems.at[i]).start()

    def wait(i):
        pick, target = pairs[i]
        pltpu.make_async_copy(pick(first), target, sems.at[i]).wait()

    return wait


def weight_pairs(steps, cols, wo_s, wu_s, wd_s):
    pairs = [(lambda w: w[0], wo_s)]
    for j in range(steps):
        pairs.append((lambda w, j=j: w[1].at[:, pl.ds(j * cols, cols)], wu_s.at[j]))
        pairs.append((lambda w, j=j: w[2].at[pl.ds(j * cols, cols), :], wd_s.at[j]))
    return pairs


def row_norm(z):
    center = z - jnp.mean(z, axis=1, keepdims=True)
    scaled = lax.rsqrt(jnp.mean(center * center, axis=1, keepdims=True) + norm_eps)
    return center * scaled, scaled


def rows_kernel(
    layer, ids, c0, c1, c2, c3, u, pack_a, pack_b, wo_a, wo_b, wu_a, wu_b, wd_a, wd_b,
    y_o, fwd_o, slope_o, unit1_o, unit2_o, scale1_o, scale2_o,
    wo_s, wu_s, wd_s, sems,
):
    steps, cols = wu_s.shape[0], wu_s.shape[2]
    pairs = weight_pairs(steps, cols, wo_s, wu_s, wd_s)
    wait = fetch((wo_a, wu_a, wd_a), (wo_b, wu_b, wd_b), ids[4] != layer, pairs, sems)
    pack = jnp.where(ids[4] == layer, pack_a[...], pack_b[...])
    hw = c0.shape[1]
    width = 4 * hw
    pieces = [c[...] for c in (c0, c1, c2, c3)]
    for a in range(4):
        part = pieces[0]
        for r in range(1, 4):
            part = jnp.where(ids[r] == a, pieces[r].astype(f32), part.astype(f32))
        fwd_o[:, width + a * hw : width + (a + 1) * hw] = part.astype(bf16)
    wait(0)
    attn = nn(fwd_o[:, width : 2 * width], wo_s[...]) + pack[4:5, :]
    unit1, scale1 = row_norm(u[...].astype(f32) + attn)
    mixed = unit1 * pack[5:6, :] + pack[7:8, :]
    low = mixed.astype(bf16)
    fwd_o[:, :width] = low
    unit1_o[...] = unit1
    scale1_o[...] = jnp.broadcast_to(scale1, scale1_o.shape)
    branch = jnp.zeros(mixed.shape, f32)
    for j in range(steps):
        wait(1 + 2 * j)
        pre = nn(low, wu_s[j]) + pack[10 + j : 11 + j, :]
        gauss = 0.5 * (1.0 + lax.erf(pre * (2.0 ** -0.5)))
        act = (pre * gauss).astype(bf16)
        bell = jnp.exp(-0.5 * pre * pre) * ((2.0 * np.pi) ** -0.5)
        slope_o[:, j * cols : (j + 1) * cols] = (gauss + pre * bell).astype(bf16)
        fwd_o[:, 2 * width + j * cols : 2 * width + (j + 1) * cols] = act
        wait(2 + 2 * j)
        branch += nn(act, wd_s[j])
    unit2, scale2 = row_norm(mixed + (branch + pack[9:10, :]))
    unit2_o[...] = unit2
    scale2_o[...] = jnp.broadcast_to(scale2, scale2_o.shape)
    y_o[...] = (unit2 * pack[6:7, :] + pack[8:9, :]).astype(bf16)


def rows_forward(layer, ids, pieces, u, packs, own, other):
    rows, width = u.shape
    ff = own[1].shape[1]
    steps = ff // width
    vm = pl.BlockSpec(memory_space=pltpu.VMEM)
    hbm = pl.BlockSpec(memory_space=pl.ANY)
    sds = jax.ShapeDtypeStruct
    return pl.pallas_call(
        partial(rows_kernel, layer),
        out_shape=[
            sds((rows, width), bf16),
            sds((rows, 2 * width + ff), bf16),
            sds((rows, ff), bf16),
            sds((rows, width), f32),
            sds((rows, width), f32),
            sds((rows, 128), f32),
            sds((rows, 128), f32),
        ],
        in_specs=[pl.BlockSpec(memory_space=pltpu.SMEM)] + [vm] * 7 + [hbm] * 6,
        out_specs=[vm] * 7,
        scratch_shapes=[
            pltpu.VMEM((width, width), bf16),
            pltpu.VMEM((steps, width, width), bf16),
            pltpu.VMEM((steps, width, width), bf16),
            pltpu.SemaphoreType.DMA((1 + 2 * steps,)),
        ],
        compiler_params=pltpu.CompilerParams(vmem_limit_bytes=VMEM_BYTES),
        cost_estimate=cost(10),
        name="rows_forward",
    )(ids, *pieces, u, *packs, own[0], other[0], own[1], other[1], own[2], other[2])


def norm_inward(unit, scaled, gain, upstream):
    d_unit = upstream * gain
    return scaled * (
        d_unit
        - jnp.mean(d_unit, axis=1, keepdims=True)
        - unit * jnp.mean(d_unit * unit, axis=1, keepdims=True)
    )


def rows_back_kernel(
    layer, ids, up, unit1, unit2, scale1, scale2, slope, pack_a, pack_b, wo_a, wo_b, wu_a, wu_b, wd_a, wd_b,
    first_o, d0, d1, d2, d3, keep_o, send_o, small_o,
    wo_s, wu_s, wd_s, sems,
):
    steps, cols = wu_s.shape[0], wu_s.shape[2]
    pairs = weight_pairs(steps, cols, wo_s, wu_s, wd_s)
    wait = fetch((wo_a, wu_a, wd_a), (wo_b, wu_b, wd_b), ids[4] != layer, pairs, sems)
    pack = jnp.where(ids[4] == layer, pack_a[...], pack_b[...])
    side = ids[4]
    half = first_o.shape[1] // 2
    ffh = keep_o.shape[1] - 2 * half

    def split(value, at):
        for s in range(2):

            @pl.when(side == s)
            def _(s=s):
                keep_o[:, at : at + half] = value[:, s * half : (s + 1) * half]
                send_o[:, at : at + half] = value[:, (1 - s) * half : (2 - s) * half]

    def total(value):
        return jnp.sum(value, axis=0, keepdims=True)

    upstream = up[...].astype(f32)
    unit = unit2[...]
    small_o[0:1, :] = total(upstream * unit)
    small_o[1:2, :] = total(upstream)
    d_second = norm_inward(unit, scale2[:, :1], pack[6:7, :], upstream)
    d_branch = d_second.astype(bf16)
    split(d_branch, ffh)
    small_o[5:6, :] = total(d_branch.astype(f32))
    d_mixed = d_second
    for j in range(steps):
        wait(2 + 2 * j)
        d_act = nt(d_branch, wd_s[j])
        d_pre = (d_act * slope[:, j * cols : (j + 1) * cols].astype(f32)).astype(bf16)
        small_o[6 + j : 7 + j, :] = total(d_pre.astype(f32))
        place = slice((j % (steps // 2)) * cols, (j % (steps // 2) + 1) * cols)

        @pl.when(side == j // (steps // 2))
        def _(d_pre=d_pre, place=place):
            keep_o[:, place] = d_pre

        @pl.when(side != j // (steps // 2))
        def _(d_pre=d_pre, place=place):
            send_o[:, place] = d_pre

        wait(1 + 2 * j)
        d_mixed += nt(d_pre, wu_s[j])
    unit = unit1[...]
    small_o[2:3, :] = total(d_mixed * unit)
    small_o[3:4, :] = total(d_mixed)
    d_first = norm_inward(unit, scale1[:, :1], pack[5:6, :], d_mixed)
    first_o[...] = d_first
    d_attn = d_first.astype(bf16)
    split(d_attn, ffh + half)
    small_o[4:5, :] = total(d_attn.astype(f32))
    small_o[10:, :] = jnp.zeros((small_o.shape[0] - 10, small_o.shape[1]), f32)
    wait(0)
    d_ctx = nt(d_attn, wo_s[...])
    hw = d0.shape[1]
    parts = [d_ctx[:, a * hw : (a + 1) * hw] for a in range(4)]
    for r, d_o in enumerate((d0, d1, d2, d3)):
        part = parts[0]
        for a in range(1, 4):
            part = jnp.where(ids[r] == a, parts[a], part)
        d_o[...] = part.astype(bf16)


def rows_back(layer, ids, upstream, kept, packs, own, other):
    rows, width = upstream.shape
    ff = own[1].shape[1]
    steps = ff // width
    hw = width // 4
    unit1, unit2, scale1, scale2, slope = kept
    vm = pl.BlockSpec(memory_space=pltpu.VMEM)
    hbm = pl.BlockSpec(memory_space=pl.ANY)
    sds = jax.ShapeDtypeStruct
    return pl.pallas_call(
        partial(rows_back_kernel, layer),
        out_shape=[sds((rows, width), f32)]
        + [sds((rows, hw), bf16)] * 4
        + [sds((rows, ff // 2 + width), bf16)] * 2
        + [sds((16, width), f32)],
        in_specs=[pl.BlockSpec(memory_space=pltpu.SMEM)] + [vm] * 8 + [hbm] * 6,
        out_specs=[vm] * 8,
        scratch_shapes=[
            pltpu.VMEM((width, width), bf16),
            pltpu.VMEM((steps, width, width), bf16),
            pltpu.VMEM((steps, width, width), bf16),
            pltpu.SemaphoreType.DMA((1 + 2 * steps,)),
        ],
        compiler_params=pltpu.CompilerParams(vmem_limit_bytes=VMEM_BYTES),
        cost_estimate=cost(11),
        name="rows_back",
    )(
        ids, upstream, unit1, unit2, scale1, scale2, slope, *packs,
        own[0], other[0], own[1], other[1], own[2], other[2],
    )


def rows_ahead(ids, pieces, u, pack, wait, weights, fwd_s, slope_s):
    wo_s, wu_s, wd_s = weights
    steps, cols = wu_s.shape[0], wu_s.shape[2]
    hw = pieces[0].shape[1]
    width = 4 * hw
    values = [c[...].astype(f32) for c in pieces]
    for a in range(4):
        part = values[0]
        for r in range(1, 4):
            part = jnp.where(ids[r] == a, values[r], part)
        fwd_s[:, width + a * hw : width + (a + 1) * hw] = part.astype(bf16)
    wait(0)
    attn = nn(fwd_s[:, width : 2 * width], wo_s[...]) + pack[4:5, :]
    unit1, scale1 = row_norm(u[...].astype(f32) + attn)
    mixed = unit1 * pack[5:6, :] + pack[7:8, :]
    low = mixed.astype(bf16)
    fwd_s[:, :width] = low
    branch = jnp.zeros(mixed.shape, f32)
    for j in range(steps):
        wait(1 + 2 * j)
        pre = nn(low, wu_s[j]) + pack[10 + j : 11 + j, :]
        gauss = 0.5 * (1.0 + lax.erf(pre * (2.0 ** -0.5)))
        act = (pre * gauss).astype(bf16)
        bell = jnp.exp(-0.5 * pre * pre) * ((2.0 * np.pi) ** -0.5)
        slope_s[:, j * cols : (j + 1) * cols] = (gauss + pre * bell).astype(bf16)
        fwd_s[:, 2 * width + j * cols : 2 * width + (j + 1) * cols] = act
        wait(2 + 2 * j)
        branch += nn(act, wd_s[j])
    unit2, scale2 = row_norm(mixed + (branch + pack[9:10, :]))
    return unit2 * pack[6:7, :] + pack[8:9, :], (unit1, scale1), (unit2, scale2)


def rows_behind(ids, upstream, norm1, norm2, pack, wait, weights, slope_s, outs):
    first_o, pieces, keep_s, send_s, small_o = outs
    wo_s, wu_s, wd_s = weights
    steps, cols = wu_s.shape[0], wu_s.shape[2]
    side = ids[4]
    half = first_o.shape[1] // 2
    ffh = keep_s.shape[1] - 2 * half

    def split(value, at):
        for s in range(2):

            @pl.when(side == s)
            def _(s=s):
                keep_s[:, at : at + half] = value[:, s * half : (s + 1) * half]
                send_s[:, at : at + half] = value[:, (1 - s) * half : (2 - s) * half]

    def total(value):
        return jnp.sum(value, axis=0, keepdims=True)

    unit, scaled = norm2
    small_o[0:1, :] = total(upstream * unit)
    small_o[1:2, :] = total(upstream)
    d_second = norm_inward(unit, scaled, pack[6:7, :], upstream)
    d_branch = d_second.astype(bf16)
    split(d_branch, ffh)
    small_o[5:6, :] = total(d_branch.astype(f32))
    d_mixed = d_second
    for j in range(steps):
        wait(2 + 2 * j)
        d_act = nt(d_branch, wd_s[j])
        d_pre = (d_act * slope_s[:, j * cols : (j + 1) * cols].astype(f32)).astype(bf16)
        small_o[6 + j : 7 + j, :] = total(d_pre.astype(f32))
        place = slice((j % (steps // 2)) * cols, (j % (steps // 2) + 1) * cols)

        @pl.when(side == j // (steps // 2))
        def _(d_pre=d_pre, place=place):
            keep_s[:, place] = d_pre

        @pl.when(side != j // (steps // 2))
        def _(d_pre=d_pre, place=place):
            send_s[:, place] = d_pre

        wait(1 + 2 * j)
        d_mixed += nt(d_pre, wu_s[j])
    unit, scaled = norm1
    small_o[2:3, :] = total(d_mixed * unit)
    small_o[3:4, :] = total(d_mixed)
    d_first = norm_inward(unit, scaled, pack[5:6, :], d_mixed)
    first_o[...] = d_first
    d_attn = d_first.astype(bf16)
    split(d_attn, ffh + half)
    small_o[4:5, :] = total(d_attn.astype(f32))
    small_o[10:, :] = jnp.zeros((small_o.shape[0] - 10, small_o.shape[1]), f32)
    wait(0)
    d_ctx = nt(d_attn, wo_s[...])
    hw = pieces[0].shape[1]
    parts = [d_ctx[:, a * hw : (a + 1) * hw] for a in range(4)]
    for r, d_o in enumerate(pieces):
        part = parts[0]
        for a in range(1, 4):
            part = jnp.where(ids[r] == a, parts[a], part)
        d_o[...] = part.astype(bf16)


def own_pack(layer, ids, pack_a, pack_b):
    return jnp.where(ids[4] == layer, pack_a[...], pack_b[...])


def rows_both_kernel(
    ids, c0, c1, c2, c3, u, up, pack_a, pack_b, wo_a, wo_b, wu_a, wu_b, wd_a, wd_b,
    y_o, first_o, d0, d1, d2, d3, small_o, keep_o, send_o, fwd_h,
    fwd_s, slope_s, out_sem, wo_s, wu_s, wd_s, sems,
):
    steps, cols = wu_s.shape[0], wu_s.shape[2]
    pairs = weight_pairs(steps, cols, wo_s, wu_s, wd_s)
    wait = fetch((wo_a, wu_a, wd_a), (wo_b, wu_b, wd_b), ids[4] != 1, pairs, sems)
    pack = own_pack(1, ids, pack_a, pack_b)
    weights = (wo_s, wu_s, wd_s)
    y, norm1, norm2 = rows_ahead(ids, (c0, c1, c2, c3), u, pack, wait, weights, fwd_s, slope_s)
    out = pltpu.make_async_copy(fwd_s, fwd_h, out_sem)
    out.start()
    y_o[...] = y.astype(bf16)
    rows_behind(
        ids, up[...].astype(f32), norm1, norm2, pack, lambda i: None, weights, slope_s,
        (first_o, (d0, d1, d2, d3), keep_o, send_o, small_o),
    )
    out.wait()


def rows_both(ids, pieces, u, upstream, packs, own, other):
    rows, width = u.shape
    ff = own[1].shape[1]
    steps = ff // width
    vm = pl.BlockSpec(memory_space=pltpu.VMEM)
    hbm = pl.BlockSpec(memory_space=pl.ANY)
    sds = jax.ShapeDtypeStruct
    res = pl.pallas_call(
        rows_both_kernel,
        out_shape=[sds((rows, width), bf16), sds((rows, width), f32)]
        + [sds((rows, width // 4), bf16)] * 4
        + [sds((16, width), f32)]
        + [sds((rows, ff // 2 + width), bf16)] * 2
        + [sds((rows, 2 * width + ff), bf16)],
        in_specs=[pl.BlockSpec(memory_space=pltpu.SMEM)] + [vm] * 8 + [hbm] * 6,
        out_specs=[vm] * 9 + [hbm],
        scratch_shapes=[
            pltpu.VMEM((rows, 2 * width + ff), bf16),
            pltpu.VMEM((rows, ff), bf16),
            pltpu.SemaphoreType.DMA,
            pltpu.VMEM((width, width), bf16),
            pltpu.VMEM((steps, width, width), bf16),
            pltpu.VMEM((steps, width, width), bf16),
            pltpu.SemaphoreType.DMA((1 + 2 * steps,)),
        ],
        compiler_params=pltpu.CompilerParams(vmem_limit_bytes=VMEM_BYTES),
        cost_estimate=cost(15),
        name="rows_both",
    )(
        ids, *pieces, u, upstream, *packs, own[0], other[0], own[1], other[1], own[2], other[2],
    )
    return res[0], res[9], res[1:9]


def grads_kernel(layer, ids, f0, f1, k0, k1, *refs):
    count = 1 if layer == 1 else 6
    targets, outs, (f, b, in_sems, out_sems) = refs[:count], refs[count : 2 * count], refs[2 * count :]
    rows = f0.shape[0]
    part = f0.shape[1] // 12
    width = 2 * part
    ffh = k0.shape[1] - width
    ins = []
    for at, n in [(None, None), (0, 2 * width)] + [(width * (2 + i), width) for i in range(4)]:
        for side, (fx, kx) in enumerate(((f0, k0), (f1, k1))):
            to = pl.ds(side * rows, rows)
            pair = (kx, b.at[to, :]) if at is None else (fx.at[:, pl.ds(at, n)], f.at[to, pl.ds(at, n)])
            ins += start_all(moves([pair], in_sems, len(ins)))
    wait_all(ins[:4])
    pre, branch, attn = b[:, :ffh], b[:, ffh : ffh + part], b[:, ffh + part :]
    if layer == 1:
        out, out_h = outs[0], targets[0]
        few, many = width // 16, 8 * part // 16
        blocks = ffh // part
        for j in range(2):
            at = j * part
            up = tn(f[:, at : at + part], pre).astype(bf16)
            last = tn(f[:, width + at : width + at + part], attn).astype(bf16)
            for s in range(8):
                cut = slice(s * few, (s + 1) * few)
                for i in range(blocks):
                    out[8 * j + s, i * few : (i + 1) * few, :] = up[cut, i * part : (i + 1) * part]
                out[8 * j + s, blocks * few : (blocks + 1) * few, :] = last[cut]
        sent = []
        for j in range(8):
            if j % 2 == 0:
                wait_all(ins[4 + j : 6 + j])
            at = 2 * width + j * part
            down = tn(f[:, at : at + part], branch).astype(bf16)
            for s in range(2):
                out[2 * j + s, (blocks + 1) * few :, :] = down[s * many : (s + 1) * many]
            pair = pl.ds(2 * j, 2)
            sent += start_all(moves([(out.at[pair], out_h.at[pair])], out_sems, j))
        wait_all(sent)
        return
    ua_o, ub_o, uk_o, da_o, db_o, dk_o = outs
    ua = ua_o.shape[1]
    small = dk_o.shape[1]
    sub = small // 2

    def rows_at(at):
        return f[:, pl.ds(pl.multiple_of(at, 128), part)]

    start = (1 - ids[5]) * part
    up = tn(rows_at(start), pre).astype(bf16)
    ua_o[...] = up[:, :ua]
    ub_o[:, : ffh - ua] = up[:, ua:]
    ub_o[:, ffh - ua :] = tn(rows_at(start + width), attn).astype(bf16)
    sent = start_all(moves(list(zip(outs[:2], targets[:2])), out_sems))
    start = ids[5] * part
    uk_o[:, :ffh] = tn(rows_at(start), pre).astype(bf16)
    uk_o[:, ffh:] = tn(rows_at(start + width), attn).astype(bf16)
    sent += start_all(moves([(uk_o, targets[2])], out_sems, 2))
    for j in range(8):
        if j % 2 == 0:
            wait_all(ins[4 + j : 6 + j])
        at = 2 * width + 2 * small * j
        down = tn(f[:, at : at + 2 * small], branch).astype(bf16)
        for low in range(2):
            block = down[small * low : small * (low + 1)]
            share = 2 * j + low
            place, mine = (share // 8) * 4 + share % 4, ids[6] == (share // 4) % 2

            @pl.when(mine)
            def _(block=block, place=place):
                dk_o[place] = block

            @pl.when(jnp.logical_not(mine))
            def _(block=block, place=place):
                da_o[place] = block[:sub]
                db_o[place] = block[sub:]

    wait_all(sent + start_all(moves(list(zip(outs[3:], targets[3:])), out_sems, 3)))


def grads(layer, ids, fwd, fwd_other, keep, got):
    width = HEAD * 12
    ff = 2 * (keep.shape[1] - width)
    part = width // 2
    ua = 1024
    small = ff // 16
    hbm = pl.BlockSpec(memory_space=pl.ANY)
    shapes = [
        (part, ua),
        (part, ff // 2 + part - ua),
        (part, ff // 2 + part),
        (8, small // 2, part),
        (8, small // 2, part),
        (8, small, part),
    ]
    if layer == 1:
        shapes = [(16, (ff // 2 // part + 1) * width // 16 + ff // 16, part)]
    return pl.pallas_call(
        partial(grads_kernel, layer),
        out_shape=[jax.ShapeDtypeStruct(shape, bf16) for shape in shapes],
        in_specs=[pl.BlockSpec(memory_space=pltpu.SMEM)] + [hbm] * 4,
        out_specs=[hbm] * len(shapes),
        scratch_shapes=[pltpu.VMEM(shape, bf16) for shape in shapes]
        + [
            pltpu.VMEM((2 * fwd.shape[0], fwd.shape[1]), bf16),
            pltpu.VMEM((2 * keep.shape[0], keep.shape[1]), bf16),
            pltpu.SemaphoreType.DMA((12,)),
            pltpu.SemaphoreType.DMA((8,)),
        ],
        compiler_params=pltpu.CompilerParams(vmem_limit_bytes=VMEM_BYTES),
        cost_estimate=cost(5),
        name="grads",
    )(ids, fwd, fwd_other, keep, got)


def proj_grads_kernel(ids, u_h, d_h, ra_h, rb_h, rk_h, u, d, ra_o, rb_o, rk_o, sems):
    wait_all(start_all(moves([(u_h, u), (d_h, d)], sems)))
    part = rk_o.shape[0]
    ra = ra_o.shape[1]
    rows = tn(u[:, pl.ds(pl.multiple_of((1 - ids[5]) * part, 128), part)], d[...]).astype(bf16)
    ra_o[...] = rows[:, :ra]
    rb_o[...] = rows[:, ra:]
    out = start_all(moves([(ra_o, ra_h), (rb_o, rb_h)], sems, 2))
    rk_o[...] = tn(u[:, pl.ds(pl.multiple_of(ids[5] * part, 128), part)], d[...]).astype(bf16)
    wait_all(out + start_all(moves([(rk_o, rk_h)], sems, 4)))


def proj_grads(ids, u, d):
    part = u.shape[1] // 2
    cols = d.shape[1]
    hbm = pl.BlockSpec(memory_space=pl.ANY)
    shapes = [(part, n) for n in (640, cols - 640, cols)]
    return pl.pallas_call(
        proj_grads_kernel,
        out_shape=[jax.ShapeDtypeStruct(shape, bf16) for shape in shapes],
        in_specs=[pl.BlockSpec(memory_space=pltpu.SMEM)] + [hbm] * 2,
        out_specs=[hbm] * 3,
        scratch_shapes=[pltpu.VMEM(shape, bf16) for shape in [u.shape, d.shape] + shapes]
        + [pltpu.SemaphoreType.DMA((5,))],
        compiler_params=pltpu.CompilerParams(vmem_limit_bytes=VMEM_BYTES),
        cost_estimate=cost(4),
        name="proj_grads",
    )(ids, u, d)


def assemble_kernel(sizes, ids, fk, fg, ak, ag, up_o, out_o, down_o, local_o, glob_o):
    share_w, share_f, ff, width = sizes
    part, hw = width // 2, width // 4
    core, x = ids[4], ids[6]
    for side in range(2):

        @pl.when(core == side)
        def _(side=side):
            halves = (fk, fg) if side == 0 else (fg, fk)
            for c, ref in enumerate(halves):
                for i in range(4):
                    to = c * (ff // 2) + i * part
                    up_o[:, to : to + part] = ref[i * share_w : (i + 1) * share_w, :]
                out_o[:, c * part : (c + 1) * part] = ref[4 * share_w : 5 * share_w, :]
                down_o[:, c * part : (c + 1) * part] = ref[5 * share_w :, :]

    held = []
    for group in range(4):
        pair = [jnp.where(core == group // 2, ak[i].astype(f32), ag[i].astype(f32)) for i in range(2)]
        held.append(jnp.where(x == group % 2, pair[0], pair[1]))
    for target, kinds in ((local_o, (0, 1, 2)), (glob_o, (5, 3, 4))):
        target[...] = jnp.concatenate(
            [held[g][:, k * hw : (k + 1) * hw] for k in kinds for g in range(4)], axis=1
        )


def assemble(ids, ffn_keep, ffn_got, att_keep, att_got, sizes):
    share_w, share_f, ff, width = sizes
    vm = pl.BlockSpec(memory_space=pltpu.VMEM)
    shapes = [(share_w, ff), (share_w, width), (share_f, width)] + [(share_w, 3 * width)] * 2
    return pl.pallas_call(
        partial(assemble_kernel, sizes),
        out_shape=[jax.ShapeDtypeStruct(shape, f32) for shape in shapes],
        in_specs=[pl.BlockSpec(memory_space=pltpu.SMEM)] + [vm] * 4,
        out_specs=[vm] * 5,
        compiler_params=pltpu.CompilerParams(vmem_limit_bytes=VMEM_BYTES),
        name="assemble",
    )(ids, ffn_keep, ffn_got, att_keep, att_got)


def core_flip(v):
    return lax.ppermute(v, SECTION, [(0, 1), (1, 0)])


def seq_flip(v, by):
    return lax.ppermute(v, SEQ, [(i, i ^ by) for i in range(4)])


def core_x_flip(v):
    return lax.ppermute(v, BOTH, [(i, i ^ 5) for i in range(8)])


def dp_flip(v, by):
    return lax.ppermute(v, DP, [(i, i ^ by) for i in range(lax.axis_size(DP))])


def pick(which, options):
    result = options[-1]
    for i in range(len(options) - 2, -1, -1):
        result = jnp.where(which == i, options[i], result)
    return result


def to_section(v, layer):
    near = [(y_ * 4 + 2 * y_ + x_, layer * 4 + 2 * y_ + x_) for y_ in (0, 1) for x_ in (0, 1)]
    far = [
        ((1 - y_) * 4 + 2 * y_ + x_, layer * 4 + 2 * (1 - y_) + x_) for y_ in (0, 1) for x_ in (0, 1)
    ]
    return lax.ppermute(v, BOTH, near), lax.ppermute(v, BOTH, far)


def by_micro(first, lower, upper, y):
    mine = jnp.where(first, lower[0], upper[0])
    away = jnp.where(first, lower[1], upper[1])
    return jnp.where(y == 0, jnp.stack([mine, away]), jnp.stack([away, mine]))


def two_chips(
    layer_in, cotangent, masked_rows, global_positions, local_weight, local_bias, global_weight,
    global_bias, out_weight, out_bias, norm_gain, norm_shift, up_weight, up_bias, down_weight,
    down_bias,
):
    c = lax.axis_index(SECTION)
    q = lax.axis_index(SEQ)
    z = lax.axis_index(DP)
    dp = lax.axis_size(DP)
    y, x = q // 2, q % 2
    g = 2 * c + x
    g_other = 2 * (1 - c) + x
    rows, width = layer_in.shape[2:]
    hw = width // 4
    ff = up_weight.shape[2]
    heads = hw // HEAD
    half_rows = rows // 2
    same = c == y
    first = c == 0

    block = layer_in[:, 0]

    def half_of(micro):
        return lax.dynamic_slice(block, (micro, c * half_rows, 0), (1, half_rows, width))[0]

    mine_part, away_part = half_of(y), half_of(1 - y)
    got = [seq_flip(mine_part, 1), seq_flip(away_part, 2), seq_flip(away_part, 3)]

    cot = cotangent[:, 0]
    marks = masked_rows[:, 0]

    def of_micro(v, micro):
        return lax.dynamic_index_in_dim(v, micro, 0, keepdims=False)

    cot_away = seq_flip(of_micro(cot, 1 - y), 2)
    marks_away = seq_flip(of_micro(marks, 1 - y), 2)

    ids = jnp.stack([g, g_other, 2 * c + 1 - x, 2 * (1 - c) + 1 - x, c, y, x, z]).astype(jnp.int32)
    ids, _ = lax.optimization_barrier((ids, (mine_part, away_part)))
    w_own, w_send, pack = prepare(
        ids,
        local_weight[0],
        global_weight[0],
        (local_bias[0], global_bias[0], out_bias, norm_gain[0], norm_shift[0], down_bias, up_bias),
    )
    own = (out_weight[0], up_weight[0], down_weight[0])
    other_up = core_flip(own[1])
    (w_own, w_send, pack), (got, other_up) = lax.optimization_barrier(
        ((w_own, w_send, pack), (got, other_up))
    )
    weights = (w_own, core_flip(w_send))
    packs = (pack, core_flip(pack))
    positions = of_micro(global_positions[:, 0], y)
    prow = positions[None, :]
    pcol = positions[:, None]
    parts = [block] + got + [core_flip(v) for v in got]
    own_late, _ = lax.optimization_barrier(((own[0], own[2]), (parts, weights, packs)))
    other_out, other_down = [core_flip(w) for w in own_late]
    other = (other_out, other_up, other_down)

    def exchange(pieces):
        return [pieces[0], core_flip(pieces[1]), seq_flip(pieces[2], 1), core_x_flip(pieces[3])]

    saved = []
    for layer in range(2):
        ctx, u_all, u_own, kept = attend(layer, ids, parts, weights, packs, prow, pcol)
        if layer == 0:
            ctx, other = lax.optimization_barrier((ctx, other))
        pieces = exchange(ctx)
        if layer == 0:
            res = rows_forward(layer, ids, pieces, u_own, packs, own, other)
            y_low, fwd, slope, *row_kept = res
            row_kept.append(slope)
            across = seq_flip(y_low, 1)
            across, (cot_away, marks_away, fwd_other) = lax.optimization_barrier(
                (across, (cot_away, marks_away, core_flip(fwd)))
            )
            parts = [y_low, core_flip(y_low), across, core_flip(across)]
            saved_low = y_low
            saved.append((u_all, kept, fwd, fwd_other, row_kept))
        else:
            pieces, out0 = lax.optimization_barrier((pieces, to_section(saved_low, 0)))
            cot_rows = jnp.where(same, of_micro(cot, y), cot_away)
            cot_marks = jnp.where(same, of_micro(marks, y), marks_away)
            row_hit = (g * rows + jnp.arange(rows))[:, None] == cot_marks[None, :]
            upstream = nn(row_hit.astype(bf16), cot_rows).astype(bf16)
            y_low, fwd, back = rows_both(ids, pieces, u_own, upstream, packs, own, other)

    flip_x = partial(seq_flip, by=1)
    flip_y = partial(seq_flip, by=2)
    flip_z1 = partial(dp_flip, by=1)
    flip_z2 = partial(dp_flip, by=2)
    low_z, high_z = z % 2, z // 2

    def after(value, others):
        return lax.optimization_barrier((value, others))

    def cut(value, axis, bit):
        return of_axis(value, axis, 1 - bit).astype(bf16), of_axis(value, axis, bit)

    def of_axis(value, axis, index):
        return lax.dynamic_index_in_dim(value, index, axis, keepdims=False)

    def plus(keep, got):
        return keep.astype(f32) + got.astype(f32)

    def bias_rows(small, bias):
        placed = jnp.concatenate([jnp.where(g == i, bias, 0.0) for i in range(4)], axis=1)
        return jnp.concatenate([small[:10], placed], axis=0)

    def inward(partials):
        low = [core_flip(partials[1]), core_flip(partials[3])]
        return plus(partials[0], low[0]), plus(partials[2], low[1]).astype(bf16)

    ua = 1024
    share_w = width // (4 * dp)
    share_f = ff // (4 * dp)
    sub = share_f // 2
    part = width // 2

    d_first, pieces, (small, keep, send) = back[0], exchange(back[1:5]), back[5:]
    gr = grads(1, ids, fwd, core_flip(fwd), keep, core_flip(send))
    pieces, gr = after(pieces, gr)
    ffn1 = lax.psum_scatter(gr[0], SEQ, scatter_dimension=0, tiled=True)
    res = attend_back(1, ids, pieces, kept, prow, pcol, weights)
    d_all, bias, partials = res
    small1 = bias_rows(small, bias)
    summed, send = inward(partials)
    across = flip_x(send)
    d_all, send = after(d_all, send)
    gr = proj_grads(ids, u_all, d_all)
    across, gr = after(across, gr)
    r1a, r1b, r1k = gr
    d_upper = (d_first + summed + across.astype(f32)).astype(bf16)

    got_r1a = flip_y(r1a)
    u_all, kept, fwd, fwd_other, row_kept = saved[0]
    res = rows_back(0, ids, d_upper, row_kept, packs, own, other)
    res, got_r1a = after(res, got_r1a)
    d_first, pieces, (keep, send, small) = res[0], exchange(res[1:5]), res[5:]
    got_r1b = flip_y(r1b)
    gr = grads(0, ids, fwd, fwd_other, keep, core_flip(send))
    pieces, gr = after(pieces, gr)
    u0a, u0b, u0k, d0a, d0b, d0k = gr
    got_u0a, got_d0a, got_u0b, got_d0b = flip_y(u0a), flip_x(d0a), flip_y(u0b), flip_x(d0b)
    res = attend_back(0, ids, pieces, kept, prow, pcol, weights)
    (res, y_low, d_upper), (got_u0a, got_d0a, got_r1b, ffn1) = after(
        (res, y_low, d_upper), (got_u0a, got_d0a, got_r1b, ffn1)
    )
    ffn1 = lax.psum_scatter(ffn1, DP, scatter_dimension=0, tiled=True)[0]
    d_all, bias, partials = res
    small0 = bias_rows(small, bias)

    def step(flights):
        sends = lax.optimization_barrier([send for _, send in flights])
        return [flip(send) for (flip, _), send in zip(flights, sends)]

    def end(got, *more):
        return lax.optimization_barrier((got, more))

    swapped = partial(jnp.where, first)
    small_keep, small_send = swapped(small0, small1), swapped(small1, small0)
    small = small_keep + core_flip(small_send)
    r1 = plus(r1k, jnp.concatenate([got_r1a, got_r1b], axis=1)).astype(bf16)
    r1_send, r1_keep = cut(r1.reshape(2, 2, 2, share_w, -1), 2, low_z)
    summed, d_send = inward(partials)
    got = step([(flip_x, d_send), (flip_z1, r1_send), (flip_x, small)])
    gr = proj_grads(ids, u_all, d_all)
    got, ends = end(got, got_u0b, got_d0b, gr)
    got_u0b, got_d0b, (r0a, r0b, r0k) = ends

    d_lower = (d_first + summed + got[0].astype(f32)).astype(bf16)
    u0 = plus(u0k, jnp.concatenate([got_u0a, got_u0b], axis=1)).astype(bf16)
    u0_send, u0_keep = cut(u0.reshape(2, 2, 2, share_w, -1), 2, low_z)
    r1_send, r1_keep = cut(plus(r1_keep, got[1]).astype(bf16), 1, high_z)
    small = small + got[2]
    got = step([(flip_y, r0a), (flip_z1, u0_send), (flip_y, r0b), (flip_z2, r1_send)])
    d0 = plus(d0k, jnp.concatenate([got_d0a, got_d0b], axis=1)).astype(bf16)
    d0_send, d0_keep = cut(d0.reshape(2, 2, 2, share_f, part), 0, y)
    got, ends = end(got, d0_send)
    d0_send = ends[0]

    u0_send, u0_keep = cut(plus(u0_keep, got[1]).astype(bf16), 1, high_z)
    r0 = plus(r0k, jnp.concatenate([got[0], got[2]], axis=1)).astype(bf16)
    r0_send, r0_keep = cut(r0.reshape(2, 2, 2, share_w, -1), 2, low_z)
    r1_send, r1_keep = cut(plus(r1_keep, got[3]).astype(bf16), 0, x)
    got = step([(flip_z2, u0_send), (flip_y, d0_send), (flip_z1, r0_send), (flip_z1, small)])
    in0 = to_section(d_lower, 0)
    got, ends = end(got, in0, ffn1)
    (near0, far0), ffn1 = ends

    u0_send, u0_keep = cut(plus(u0_keep, got[0]).astype(bf16), 0, x)
    d0_send, d0_keep = cut(plus(d0_keep, got[1]).astype(bf16), 1, low_z)
    r0_send, r0_keep = cut(plus(r0_keep, got[2]).astype(bf16), 1, high_z)
    small = small + got[3]
    got = step([(flip_z2, r0_send), (flip_z1, d0_send), (flip_x, u0_send), (flip_y, small), (flip_x, r1_send)])
    upper = to_section(jnp.stack([y_low, d_upper]), 1)
    got, ends = end(got, upper)
    out1, (near1, far1) = [(ends[0][0][i], ends[0][1][i]) for i in range(2)]
    r1_got = got[4]

    few = 5 * share_w
    one0 = plus(u0_keep, got[2])
    d0_send, d0_keep = cut(plus(d0_keep, got[1]).astype(bf16), 0, high_z)
    r0_send, r0_keep = cut(plus(r0_keep, got[0]).astype(bf16), 0, x)
    small = small + got[3]
    got = step([(flip_z2, d0_send), (flip_x, r0_send), (flip_z2, small)])
    got = end(got)[0]
    two0 = plus(d0_keep, got[0])
    small = small + got[2]

    lower = jnp.concatenate(
        [one0[:, i * part : (i + 1) * part] for i in range(5)] + [two0], axis=0
    )
    upper = ffn1.astype(f32)
    ffn_keep, ffn_send = swapped(lower, upper), swapped(upper, lower)
    att0, att1 = jnp.stack([r0_keep, got[1]]), jnp.stack([r1_keep, r1_got])
    att_keep, att_send = swapped(att0, att1), swapped(att1, att0)
    ffn_got, att_got = core_flip(ffn_send), core_flip(att_send)
    grad_up, grad_out, grad_down, grad_local, grad_glob = assemble(
        ids, ffn_keep, ffn_got, att_keep, att_got, (share_w, share_f, ff, width)
    )

    at = q * dp + z
    piece = partial(lax.dynamic_slice_in_dim, axis=0)
    outs = (
        grad_local,
        jnp.stack([small[10], small[11]]),
        grad_glob,
        jnp.stack([small[12], small[13]]),
        grad_out,
        piece(small[4], at * share_w, share_w),
        jnp.stack([small[2], small[0]]),
        jnp.stack([small[3], small[1]]),
        grad_up,
        piece(small[6:10].reshape(ff), at * (ff // (4 * dp)), ff // (4 * dp)),
        grad_down,
        piece(small[5], at * share_w, share_w),
    )
    layer_outputs = by_micro(first, out0, out1, y)
    in_grads = by_micro(first, (near0, far0), (near1, far1), y)
    return (layer_outputs[None, :, None], in_grads[None, :, None]) + tuple(o[None] for o in outs)


def fits_two_chips(mesh, layer_in):
    sizes = dict(mesh.shape)
    micro, _, length, width = layer_in.shape
    dp = sizes[DP]
    return (
        sizes[SECTION] == 2
        and sizes[SEQ] == 4
        and micro == 2
        and dp == 4
        and length == 4 * HALF
        and width == 12 * HEAD
    )


def solution(mesh):
    in_specs = (
        P(None, DP, SEQ, None),
        P(None, DP, SEQ, None),
        P(None, DP, SEQ),
        P(None, DP, None),
        P(SECTION, None, None),
        P(SECTION, None, None),
        P(SECTION, None, None),
        P(SECTION, None, None),
        P(SECTION, None, None),
        P(SECTION, None),
        P(SECTION, None, None),
        P(SECTION, None, None),
        P(SECTION, None, None),
        P(SECTION, None),
        P(SECTION, None, None),
        P(SECTION, None),
    )
    out_specs = (
        P(SECTION, None, DP, SEQ, None),
        P(SECTION, None, DP, SEQ, None),
        P(SECTION, (SEQ, DP), None),
        P(SECTION, None, None),
        P(SECTION, (SEQ, DP), None),
        P(SECTION, None, None),
        P(SECTION, (SEQ, DP), None),
        P(SECTION, (SEQ, DP)),
        P(SECTION, None, None),
        P(SECTION, None, None),
        P(SECTION, (SEQ, DP), None),
        P(SECTION, (SEQ, DP)),
        P(SECTION, (SEQ, DP), None),
        P(SECTION, (SEQ, DP)),
    )

    def run(layer_in, *rest):
        body = two_chips if fits_two_chips(mesh, layer_in) else on_device
        return jax.shard_map(
            body, mesh=mesh, in_specs=in_specs, out_specs=out_specs, check_vma=False
        )(layer_in, *rest)

    return run
```

```python
from functools import partial
from types import SimpleNamespace

import jax
import jax.numpy as jnp
import numpy as np
from jax import lax
from jax.experimental import pallas as pl
from jax.experimental.pallas import tpu as pltpu
from jax.sharding import PartitionSpec as P

HEAD = 64
HALF = 256

SECTION, SEQ, DP = "section", "seq", "dp"
BOTH = (SECTION, SEQ)


far_below = -1e30
norm_eps = 1e-05


def padded(block, sides, width):
    for axis, dim in sides:
        count = lax.axis_size(axis)
        forward = [(i, i + 1) for i in range(count - 1)]
        backward = [(target, source) for source, target in forward]
        low = lax.ppermute(
            lax.slice_in_dim(block, block.shape[dim] - width, None, axis=dim), axis, forward
        )
        high = lax.ppermute(lax.slice_in_dim(block, 0, width, axis=dim), axis, backward)
        block = jnp.concatenate([low, block, high], axis=dim)
    return block


def joined(value, axis, join):
    pieces = jax.tree.map(lambda part: lax.all_gather(part, axis), value)
    head = jax.tree.map(lambda part: part[0], pieces)
    tail = jax.tree.map(lambda part: part[1:], pieces)
    running, _ = lax.scan(lambda running, piece: (join(running, piece), None), head, tail)
    return running


def shifted(shard, axis, by):
    length = lax.axis_size(axis)
    pairs = [(i, i + by) for i in range(length) if 0 <= i + by < length]
    return lax.ppermute(shard, axis, pairs)


def band_mask(first_row, row_count, reach_rows, length, positions, dilated):
    rows_at = first_row + jnp.arange(row_count)
    cols_at = first_row - reach_rows + jnp.arange(row_count + 2 * reach_rows)
    offset = cols_at[None, :] - rows_at[:, None]
    inside = (jnp.abs(offset) <= reach_rows) & (cols_at >= 0)[None, :] & (cols_at < length)[None, :]
    plain_key = jnp.logical_not(jnp.any(cols_at[:, None] == positions[None, :], axis=1))
    usable = inside & plain_key[None, :]
    even_gap = offset % 2 == 0
    return usable[None, :, :] & (jnp.logical_not(dilated)[:, None, None] | even_gap[None, :, :])


def layer_norm(values, gain_row, shift_row):
    center = values - jnp.mean(values, axis=-1, keepdims=True)
    scaled = lax.rsqrt(jnp.mean(center * center, axis=-1, keepdims=True) + norm_eps)
    unit_rows = center * scaled
    return (unit_rows * gain_row + shift_row, unit_rows, scaled)


def norm_back(unit_rows, scaled, gain_row, upstream):
    d_unit = upstream * gain_row
    inward = scaled * (
        d_unit
        - jnp.mean(d_unit, axis=-1, keepdims=True)
        - unit_rows * jnp.mean(d_unit * unit_rows, axis=-1, keepdims=True)
    )
    return (inward, jnp.sum(upstream * unit_rows, axis=0), jnp.sum(upstream, axis=0))


def join_stats(first_pair, second_pair):
    top_value = jnp.maximum(first_pair[0], second_pair[0])
    merged = first_pair[1] * jnp.exp(first_pair[0] - top_value) + second_pair[1] * jnp.exp(
        second_pair[0] - top_value
    )
    return (top_value, merged)


def forward_layer(source, positions, weights, first_row, length, dilated, active):
    local_w, local_b, glob_w, glob_b, out_w, out_b, gains, shifts, up_w, up_b, down_w, down_b = (
        weights
    )
    row_count = source.shape[0]
    model_width = source.shape[1]
    ff_width = up_w.shape[1]
    head_count = dilated.shape[0]
    head_size = model_width // head_count
    glob_count = positions.shape[0]
    score_scale = head_size ** (-0.5)
    owner_hit = (first_row + jnp.arange(row_count))[:, None] == positions[None, :]
    owner_low = owner_hit.astype(jnp.bfloat16)
    owner_full = owner_hit.astype(jnp.float32)
    is_global = jnp.any(owner_hit, axis=1)
    picked = jnp.einsum("cg,cd->gd", owner_low, source, preferred_element_type=jnp.float32)
    global_rows = lax.psum(picked.astype(jnp.bfloat16), SEQ)
    proj = jnp.dot(source, local_w, preferred_element_type=jnp.float32)
    queries = (proj[:, :model_width] + local_b[0]).astype(jnp.bfloat16)
    keys_low = proj[:, model_width : 2 * model_width].astype(jnp.bfloat16)
    values_low = (proj[:, 2 * model_width :] + local_b[1]).astype(jnp.bfloat16)
    gproj = jnp.dot(source, glob_w[:, model_width:], preferred_element_type=jnp.float32)
    gkeys = gproj[:, :model_width].astype(jnp.bfloat16)
    gvalues = (gproj[:, model_width:] + glob_b[1]).astype(jnp.bfloat16)
    gqueries = (
        jnp.dot(global_rows, glob_w[:, :model_width], preferred_element_type=jnp.float32)
        + glob_b[0]
    ).astype(jnp.bfloat16)
    side_proj = jnp.dot(global_rows, local_w[:, model_width:], preferred_element_type=jnp.float32)
    extra_keys = (
        side_proj[:, :model_width].astype(jnp.bfloat16).reshape(glob_count, head_count, head_size)
    )
    extra_values = (
        (side_proj[:, model_width:] + local_b[1])
        .astype(jnp.bfloat16)
        .reshape(glob_count, head_count, head_size)
    )
    key_value = jnp.concatenate([keys_low, values_low], axis=1)
    widened = padded(key_value, ((SEQ, 0),), HALF)
    reach_rows = (widened.shape[0] - row_count) // 2
    wide_keys = widened[:, :model_width].reshape(-1, head_count, head_size)
    wide_values = widened[:, model_width:].reshape(-1, head_count, head_size)
    allowed = band_mask(first_row, row_count, reach_rows, length, positions, dilated)
    queries_h = queries.reshape(row_count, head_count, head_size)
    band_score = (
        jnp.einsum("qhd,khd->hqk", queries_h, wide_keys, preferred_element_type=jnp.float32)
        * score_scale
    )
    band_score = jnp.where(allowed, band_score, far_below)
    toward = (
        jnp.einsum("qhd,ghd->hqg", queries_h, extra_keys, preferred_element_type=jnp.float32)
        * score_scale
    )
    peak_score = jnp.maximum(jnp.max(band_score, axis=-1), jnp.max(toward, axis=-1))[..., None]
    band_exp = jnp.exp(band_score - peak_score)
    toward_exp = jnp.exp(toward - peak_score)
    totals = jnp.sum(band_exp, axis=-1, keepdims=True) + jnp.sum(toward_exp, axis=-1, keepdims=True)
    band_full = band_exp / totals
    toward_full = toward_exp / totals
    band_prob = band_full.astype(jnp.bfloat16)
    toward_prob = toward_full.astype(jnp.bfloat16)
    local_ctx = jnp.einsum(
        "hqk,khd->qhd", band_prob, wide_values, preferred_element_type=jnp.float32
    ) + jnp.einsum("hqg,ghd->qhd", toward_prob, extra_values, preferred_element_type=jnp.float32)
    gqueries_h = gqueries.reshape(glob_count, head_count, head_size)
    gkeys_h = gkeys.reshape(row_count, head_count, head_size)
    gvalues_h = gvalues.reshape(row_count, head_count, head_size)
    spread = (
        jnp.einsum("ghd,khd->hgk", gqueries_h, gkeys_h, preferred_element_type=jnp.float32)
        * score_scale
    )
    part_peak = jnp.max(spread, axis=-1)
    part_total = jnp.sum(jnp.exp(spread - part_peak[..., None]), axis=-1)
    glob_peak, glob_total = joined((part_peak, part_total), SEQ, join_stats)
    glob_full = jnp.exp(spread - glob_peak[..., None]) / glob_total[..., None]
    glob_prob = glob_full.astype(jnp.bfloat16)
    part_ctx = jnp.einsum("hgk,khd->ghd", glob_prob, gvalues_h, preferred_element_type=jnp.float32)
    glob_ctx = lax.psum(part_ctx.reshape(glob_count, model_width), SEQ)
    placed_ctx = jnp.dot(owner_full, glob_ctx, precision=lax.Precision.HIGHEST)
    context = jnp.where(is_global[:, None], placed_ctx, local_ctx.reshape(row_count, model_width))
    context_low = context.astype(jnp.bfloat16)
    attn_out = jnp.dot(context_low, out_w, preferred_element_type=jnp.float32) + out_b
    mixed, unit_one, scale_one = layer_norm(
        source.astype(jnp.float32) + attn_out, gains[0], shifts[0]
    )

    def feed_forward(hidden_in):
        pre_act = (
            jnp.dot(hidden_in.astype(jnp.bfloat16), up_w, preferred_element_type=jnp.float32) + up_b
        )
        lifted = jax.nn.gelu(pre_act, approximate=False).astype(jnp.bfloat16)
        return (
            pre_act,
            lifted,
            jnp.dot(lifted, down_w, preferred_element_type=jnp.float32) + down_b,
        )

    def skip_block(hidden_in):
        return (
            jnp.zeros((row_count, ff_width), jnp.float32),
            jnp.zeros((row_count, ff_width), jnp.bfloat16),
            jnp.zeros((row_count, model_width), jnp.float32),
        )

    pre_act, activated, branch = lax.cond(active, feed_forward, skip_block, mixed)
    result, unit_two, scale_two = layer_norm(mixed + branch, gains[1], shifts[1])
    return SimpleNamespace(
        source=source,
        owner_low=owner_low,
        owner_full=owner_full,
        is_global=is_global,
        queries_h=queries_h,
        wide_keys=wide_keys,
        wide_values=wide_values,
        extra_keys=extra_keys,
        extra_values=extra_values,
        band_full=band_full,
        toward_full=toward_full,
        band_prob=band_prob,
        toward_prob=toward_prob,
        gqueries_h=gqueries_h,
        gkeys_h=gkeys_h,
        gvalues_h=gvalues_h,
        glob_full=glob_full,
        glob_prob=glob_prob,
        context_low=context_low,
        unit_one=unit_one,
        scale_one=scale_one,
        mixed=mixed,
        pre_act=pre_act,
        activated=activated,
        unit_two=unit_two,
        scale_two=scale_two,
        result=result,
        reach_rows=reach_rows,
        score_scale=score_scale,
    )


def ffn_back(kept_values, weights, upstream, active):
    local_w, local_b, glob_w, glob_b, out_w, out_b, gains, shifts, up_w, up_b, down_w, down_b = (
        weights
    )
    d_second, gain_two, shift_two = norm_back(
        kept_values.unit_two, kept_values.scale_two, gains[1], upstream
    )
    d_branch = d_second.astype(jnp.bfloat16)

    def ffn_work(operands):
        pre_act, d_out = operands
        d_lifted = jnp.einsum("cd,fd->cf", d_out, down_w, preferred_element_type=jnp.float32)
        gelu_vals, gelu_back = jax.vjp(partial(jax.nn.gelu, approximate=False), pre_act)
        d_pre = gelu_back(d_lifted)[0].astype(jnp.bfloat16)
        d_hidden = jnp.einsum("cf,df->cd", d_pre, up_w, preferred_element_type=jnp.float32)
        return (d_hidden, d_pre)

    def ffn_spare(operands):
        return (
            jnp.zeros(upstream.shape, jnp.float32),
            jnp.zeros((upstream.shape[0], up_w.shape[1]), jnp.bfloat16),
        )

    d_hidden, d_pre = lax.cond(active, ffn_work, ffn_spare, (kept_values.pre_act, d_branch))
    return (d_second + d_hidden, d_pre, d_branch, (gain_two, shift_two))


def attention_back(kept_values, weights, d_mixed):
    local_w, local_b, glob_w, glob_b, out_w, out_b, gains, shifts, up_w, up_b, down_w, down_b = (
        weights
    )
    row_count, model_width = kept_values.source.shape
    queries_h = kept_values.queries_h
    head_count, head_size = (queries_h.shape[1], queries_h.shape[2])
    glob_count = kept_values.owner_full.shape[1]
    reach_rows = kept_values.reach_rows
    score_scale = kept_values.score_scale
    d_first, gain_one, shift_one = norm_back(
        kept_values.unit_one, kept_values.scale_one, gains[0], d_mixed
    )
    d_attn = d_first.astype(jnp.bfloat16)
    d_context = jnp.einsum("ce,de->cd", d_attn, out_w, preferred_element_type=jnp.float32).astype(
        jnp.bfloat16
    )
    glob_part = jnp.einsum(
        "cg,cd->gd", kept_values.owner_low, d_context, preferred_element_type=jnp.float32
    )
    d_glob_ctx = lax.psum(glob_part.astype(jnp.bfloat16), SEQ)
    d_local = jnp.where(kept_values.is_global[:, None], jnp.zeros_like(d_context), d_context)
    d_local = d_local.reshape(row_count, head_count, head_size)
    band_full = kept_values.band_full
    toward_full = kept_values.toward_full
    d_band = jnp.einsum(
        "qhd,khd->hqk", d_local, kept_values.wide_values, preferred_element_type=jnp.float32
    )
    d_toward = jnp.einsum(
        "qhd,ghd->hqg", d_local, kept_values.extra_values, preferred_element_type=jnp.float32
    )
    inner_sum = jnp.sum(band_full * d_band, axis=-1) + jnp.sum(toward_full * d_toward, axis=-1)
    grad_band = (band_full * (d_band - inner_sum[..., None])).astype(jnp.bfloat16)
    grad_toward = (toward_full * (d_toward - inner_sum[..., None])).astype(jnp.bfloat16)
    d_queries = (
        jnp.einsum(
            "hqk,khd->qhd", grad_band, kept_values.wide_keys, preferred_element_type=jnp.float32
        )
        + jnp.einsum(
            "hqg,ghd->qhd",
            grad_toward,
            kept_values.extra_keys,
            preferred_element_type=jnp.float32,
        )
    ) * score_scale
    d_wide_keys = (
        jnp.einsum("hqk,qhd->khd", grad_band, queries_h, preferred_element_type=jnp.float32)
        * score_scale
    )
    d_wide_values = jnp.einsum(
        "hqk,qhd->khd", kept_values.band_prob, d_local, preferred_element_type=jnp.float32
    )
    d_extra_keys = (
        jnp.einsum("hqg,qhd->ghd", grad_toward, queries_h, preferred_element_type=jnp.float32)
        * score_scale
    )
    d_extra_values = jnp.einsum(
        "hqg,qhd->ghd", kept_values.toward_prob, d_local, preferred_element_type=jnp.float32
    )
    glob_full = kept_values.glob_full
    d_glob_h = d_glob_ctx.reshape(glob_count, head_count, head_size)
    d_spread = jnp.einsum(
        "ghd,khd->hgk", d_glob_h, kept_values.gvalues_h, preferred_element_type=jnp.float32
    )
    part_inner = jnp.sum(glob_full * d_spread, axis=-1)
    glob_inner, sum_extra_keys, sum_extra_values = (
        lax.psum(part_inner.astype(jnp.bfloat16), SEQ).astype(jnp.float32),
        lax.psum(d_extra_keys.reshape(glob_count, model_width).astype(jnp.bfloat16), SEQ).astype(
            jnp.float32
        ),
        lax.psum(
            d_extra_values.reshape(glob_count, model_width).astype(jnp.bfloat16), SEQ
        ).astype(jnp.float32),
    )
    grad_spread = (glob_full * (d_spread - glob_inner[..., None])).astype(jnp.bfloat16)
    part_query = (
        jnp.einsum(
            "hgk,khd->ghd", grad_spread, kept_values.gkeys_h, preferred_element_type=jnp.float32
        )
        * score_scale
    )
    d_gkeys = (
        jnp.einsum(
            "hgk,ghd->khd",
            grad_spread,
            kept_values.gqueries_h,
            preferred_element_type=jnp.float32,
        )
        * score_scale
    )
    d_gvalues = jnp.einsum(
        "hgk,ghd->khd", kept_values.glob_prob, d_glob_h, preferred_element_type=jnp.float32
    )
    d_gqueries = lax.psum(
        part_query.reshape(glob_count, model_width).astype(jnp.bfloat16), SEQ
    ).astype(jnp.float32)
    d_wide = jnp.concatenate(
        [d_wide_keys.reshape(-1, model_width), d_wide_values.reshape(-1, model_width)], axis=1
    )
    rim_grads = jnp.concatenate([d_wide[:reach_rows], d_wide[reach_rows + row_count :]], axis=0)
    incoming = padded(rim_grads.astype(jnp.bfloat16), ((SEQ, 0),), HALF).astype(rim_grads.dtype)
    own_part = (
        d_wide[reach_rows : reach_rows + row_count]
        + incoming[:reach_rows]
        + incoming[3 * reach_rows :]
    )
    owner_full = kept_values.owner_full
    d_keys_low = (
        own_part[:, :model_width]
        + jnp.dot(owner_full, sum_extra_keys, precision=lax.Precision.HIGHEST)
    ).astype(jnp.bfloat16)
    d_values_low = (
        own_part[:, model_width:]
        + jnp.dot(owner_full, sum_extra_values, precision=lax.Precision.HIGHEST)
    ).astype(jnp.bfloat16)
    d_queries_low = d_queries.reshape(row_count, model_width).astype(jnp.bfloat16)
    d_proj = jnp.concatenate([d_queries_low, d_keys_low, d_values_low], axis=1)
    d_gq_rows = jnp.dot(owner_full, d_gqueries, precision=lax.Precision.HIGHEST).astype(
        jnp.bfloat16
    )
    d_gproj = jnp.concatenate(
        [
            d_gq_rows,
            d_gkeys.reshape(row_count, model_width).astype(jnp.bfloat16),
            d_gvalues.reshape(row_count, model_width).astype(jnp.bfloat16),
        ],
        axis=1,
    )
    d_source = (
        d_first
        + jnp.einsum("ce,de->cd", d_proj, local_w, preferred_element_type=jnp.float32)
        + jnp.einsum("ce,de->cd", d_gproj, glob_w, preferred_element_type=jnp.float32)
    )
    return (d_source, d_proj, d_gproj, d_attn, (gain_one, shift_one))


def ffn_terms(mixed_buf, pre_buf, act_buf, branch_buf, count):
    return (
        jnp.einsum(
            "mcd,mcf->df", mixed_buf[:count], pre_buf[:count], preferred_element_type=jnp.float32
        ),
        jnp.sum(pre_buf[:count].astype(jnp.float32), axis=(0, 1)),
        jnp.einsum(
            "mcf,mcd->fd", act_buf[:count], branch_buf[:count], preferred_element_type=jnp.float32
        ),
        jnp.sum(branch_buf[:count].astype(jnp.float32), axis=(0, 1)),
    )


def on_device(
    layer_in,
    cotangent,
    masked_rows,
    global_positions,
    local_weight,
    local_bias,
    global_weight,
    global_bias,
    out_weight,
    out_bias,
    norm_gain,
    norm_shift,
    up_weight,
    up_bias,
    down_weight,
    down_bias,
):
    weights = (
        local_weight[0],
        local_bias[0],
        global_weight[0],
        global_bias[0],
        out_weight[0],
        out_bias[0],
        norm_gain[0],
        norm_shift[0],
        up_weight[0],
        up_bias[0],
        down_weight[0],
        down_bias[0],
    )
    section_index = lax.axis_index(SECTION)
    seq_index = lax.axis_index(SEQ)
    micro_count = layer_in.shape[0]
    row_count = layer_in.shape[2]
    model_width = layer_in.shape[3]
    ff_width = up_weight.shape[2]
    length = row_count * lax.axis_size(SEQ)
    first_row = seq_index * row_count
    head_count = model_width // HEAD
    dilated = (jnp.arange(head_count) >= head_count - 2) & (section_index == 1)
    kept_inputs = jnp.zeros((micro_count, row_count, model_width), jnp.bfloat16)
    outputs = jnp.zeros_like(kept_inputs)
    arrived = jnp.zeros((row_count, model_width), jnp.bfloat16)
    for step_index in range(micro_count + 1):
        micro_index = step_index - section_index
        in_range = (micro_index >= 0) & (micro_index < micro_count)
        slot_index = jnp.clip(micro_index, 0, micro_count - 1)
        fresh = lax.dynamic_index_in_dim(layer_in, slot_index, 0, keepdims=False)[0]
        source = jnp.where(section_index == 0, fresh, arrived)
        positions = lax.dynamic_index_in_dim(global_positions, slot_index, 0, keepdims=False)[0]
        kept_values = forward_layer(
            source, positions, weights, first_row, length, dilated, in_range
        )
        result = kept_values.result.astype(jnp.bfloat16)
        kept_inputs = jnp.where(
            in_range,
            lax.dynamic_update_index_in_dim(kept_inputs, source, slot_index, 0),
            kept_inputs,
        )
        outputs = jnp.where(
            in_range, lax.dynamic_update_index_in_dim(outputs, result, slot_index, 0), outputs
        )
        if step_index < micro_count:
            arrived = shifted(result, SECTION, 1)
    slots = micro_count + 1
    proj_buf = jnp.zeros((slots, row_count, 3 * model_width), jnp.bfloat16)
    gproj_buf = jnp.zeros_like(proj_buf)
    ctx_buf = jnp.zeros((slots, row_count, model_width), jnp.bfloat16)
    attn_buf = jnp.zeros_like(ctx_buf)
    mixed_buf = jnp.zeros_like(ctx_buf)
    branch_buf = jnp.zeros_like(ctx_buf)
    pre_buf = jnp.zeros((slots, row_count, ff_width), jnp.bfloat16)
    act_buf = jnp.zeros_like(pre_buf)
    gain_total = jnp.zeros((2, model_width), jnp.float32)
    shift_total = jnp.zeros((2, model_width), jnp.float32)
    back_arrived = jnp.zeros((row_count, model_width), jnp.bfloat16)
    in_grads = jnp.zeros_like(kept_inputs)
    for step_index in range(micro_count + 1):
        micro_index = step_index - 1 + section_index
        in_range = (micro_index >= 0) & (micro_index < micro_count)
        slot_index = jnp.clip(micro_index, 0, micro_count - 1)
        store = jnp.where(in_range, micro_index, micro_count)
        source = lax.dynamic_index_in_dim(kept_inputs, slot_index, 0, keepdims=False)
        positions = lax.dynamic_index_in_dim(global_positions, slot_index, 0, keepdims=False)[0]
        picked_rows = lax.dynamic_index_in_dim(masked_rows, slot_index, 0, keepdims=False)[0]
        picked_grads = lax.dynamic_index_in_dim(cotangent, slot_index, 0, keepdims=False)[0]
        row_hit = ((first_row + jnp.arange(row_count))[:, None] == picked_rows[None, :]).astype(
            jnp.bfloat16
        )
        placed = jnp.dot(row_hit, picked_grads, preferred_element_type=jnp.float32)
        upstream = jnp.where(section_index == 1, placed, back_arrived.astype(jnp.float32))
        kept_values = forward_layer(
            source, positions, weights, first_row, length, dilated, in_range
        )
        d_mixed, d_pre, d_branch, norm_two = ffn_back(kept_values, weights, upstream, in_range)
        mixed_buf = lax.dynamic_update_index_in_dim(
            mixed_buf, kept_values.mixed.astype(jnp.bfloat16), store, 0
        )
        pre_buf = lax.dynamic_update_index_in_dim(pre_buf, d_pre, store, 0)
        act_buf = lax.dynamic_update_index_in_dim(act_buf, kept_values.activated, store, 0)
        branch_buf = lax.dynamic_update_index_in_dim(branch_buf, d_branch, store, 0)
        d_source, d_proj, d_gproj, d_attn, norm_one = attention_back(kept_values, weights, d_mixed)
        proj_buf = lax.dynamic_update_index_in_dim(proj_buf, d_proj, store, 0)
        gproj_buf = lax.dynamic_update_index_in_dim(gproj_buf, d_gproj, store, 0)
        ctx_buf = lax.dynamic_update_index_in_dim(ctx_buf, kept_values.context_low, store, 0)
        attn_buf = lax.dynamic_update_index_in_dim(attn_buf, d_attn, store, 0)
        gain_total = gain_total + jnp.where(in_range, jnp.stack([norm_one[0], norm_two[0]]), 0.0)
        shift_total = shift_total + jnp.where(in_range, jnp.stack([norm_one[1], norm_two[1]]), 0.0)
        d_low = d_source.astype(jnp.bfloat16)
        in_grads = jnp.where(
            in_range, lax.dynamic_update_index_in_dim(in_grads, d_low, slot_index, 0), in_grads
        )
        if step_index < micro_count:
            back_arrived = shifted(d_low, SECTION, -1)
    used_proj = proj_buf[:micro_count]
    used_gproj = gproj_buf[:micro_count]
    grad_local = jnp.einsum(
        "mcd,mce->de", kept_inputs, used_proj, preferred_element_type=jnp.float32
    )
    grad_glob = jnp.einsum(
        "mcd,mce->de", kept_inputs, used_gproj, preferred_element_type=jnp.float32
    )
    grad_out = jnp.einsum(
        "mcd,mce->de",
        ctx_buf[:micro_count],
        attn_buf[:micro_count],
        preferred_element_type=jnp.float32,
    )
    grad_out_b = jnp.sum(attn_buf[:micro_count].astype(jnp.float32), axis=(0, 1))
    local_b_grad = jnp.stack(
        [
            jnp.sum(used_proj[:, :, :model_width].astype(jnp.float32), axis=(0, 1)),
            jnp.sum(used_proj[:, :, 2 * model_width :].astype(jnp.float32), axis=(0, 1)),
        ]
    )
    glob_b_grad = jnp.stack(
        [
            jnp.sum(used_gproj[:, :, :model_width].astype(jnp.float32), axis=(0, 1)),
            jnp.sum(used_gproj[:, :, 2 * model_width :].astype(jnp.float32), axis=(0, 1)),
        ]
    )
    small_sums = lax.psum((local_b_grad, glob_b_grad, gain_total, shift_total), (SEQ, DP))
    ffn_parts = ffn_terms(mixed_buf, pre_buf, act_buf, branch_buf, micro_count)
    large_sums = (
        lax.psum_scatter(grad_local, (SEQ, DP), scatter_dimension=0, tiled=True),
        lax.psum_scatter(grad_glob, (SEQ, DP), scatter_dimension=0, tiled=True),
        lax.psum_scatter(grad_out, (SEQ, DP), scatter_dimension=0, tiled=True),
        lax.psum_scatter(grad_out_b, (SEQ, DP), scatter_dimension=0, tiled=True),
        lax.psum_scatter(ffn_parts[0], (SEQ, DP), scatter_dimension=0, tiled=True),
        lax.psum_scatter(ffn_parts[1], (SEQ, DP), scatter_dimension=0, tiled=True),
        lax.psum_scatter(ffn_parts[2], (SEQ, DP), scatter_dimension=0, tiled=True),
        lax.psum_scatter(ffn_parts[3], (SEQ, DP), scatter_dimension=0, tiled=True),
    )
    summed = (
        large_sums[0],
        small_sums[0],
        large_sums[1],
        small_sums[1],
        large_sums[2],
        large_sums[3],
        small_sums[2],
        small_sums[3],
        large_sums[4],
        large_sums[5],
        large_sums[6],
        large_sums[7],
    )
    return (outputs[None, :, None], in_grads[None, :, None]) + tuple(
        (member[None] for member in summed)
    )


bf16 = jnp.bfloat16
f32 = jnp.float32
VMEM_BYTES = 50 * 1024 * 1024


def nn(a, b):
    return jnp.dot(a, b, preferred_element_type=f32)


def nt(a, b):
    return lax.dot_general(a, b, (((1,), (1,)), ((), ())), preferred_element_type=f32)


def tn(a, b):
    return lax.dot_general(a, b, (((0,), (0,)), ((), ())), preferred_element_type=f32)


def owner_rows(prow, chunk, rows):
    at = lax.broadcasted_iota(jnp.int32, (rows, prow.shape[1]), 0) + chunk * rows
    return (at == prow[...]).astype(f32)


def owner_cols(pcol, chunk, rows):
    at = lax.broadcasted_iota(jnp.int32, (pcol.shape[0], rows), 1) + chunk * rows
    return (at == pcol[...]).astype(f32)


def is_dilated(layer, group, h):
    return ((3 * group + h >= 10) & (layer == 1)).astype(jnp.int32)


def band_masks(mask_s, dilated, rows):
    row = lax.broadcasted_iota(jnp.int32, (rows, rows), 0)
    col = lax.broadcasted_iota(jnp.int32, (rows, rows), 1)
    odd = ((row + col) % 2).astype(f32)
    level = odd * (dilated.astype(f32) * far_below)
    mask_s[0] = jnp.where(row >= col, level, far_below)
    mask_s[1] = level
    mask_s[2] = jnp.where(row <= col, level, far_below)


def neighbours(block, count):
    return [b for b in (block - 1, block, block + 1) if 0 <= b < count]


def cost(us):
    return pl.CostEstimate(
        flops=int(us * 1e9), transcendentals=0, bytes_accessed=int(us * 3.5e6)
    )


def start_all(copies):
    for copy in copies:
        copy.start()
    return copies


def wait_all(copies):
    for copy in copies:
        copy.wait()


def moves(pairs, sems, at=0):
    return [pltpu.make_async_copy(a, b, sems.at[at + i]) for i, (a, b) in enumerate(pairs)]


def choose(flag, first, second, target, sem):
    for value, source in ((0, first), (1, second)):

        @pl.when(flag == value)
        def _(source=source):
            pltpu.make_async_copy(source, target, sem).start()

    return pltpu.make_async_copy(first, target, sem)


def prepare_kernel(ids, lw, gw, own_o, send_o, win_s, sems):
    width = lw.shape[0]
    hw = width // 4
    sources = [(lw, 0), (lw, 1), (lw, 2), (gw, 1), (gw, 2), (gw, 0)]
    copies = []
    for t, group in enumerate((ids[1], ids[0])):
        for i, (ref, part) in enumerate(sources):
            start = pl.multiple_of(part * width + 128 * ((3 * group) // 2), 128)
            copies.append(
                pltpu.make_async_copy(
                    ref.at[:, pl.ds(start, 256)], win_s.at[t, i], sems.at[6 * t + i]
                )
            )
            copies[-1].start()
    for t, target in enumerate((send_o, own_o)):
        for i in range(6):
            copies[6 * t + i].wait()
        for odd in range(2):

            @pl.when(ids[6] == odd)
            def _(t=t, target=target, odd=odd):
                parts = [win_s[t, i][:, 64 * odd : 64 * odd + hw] for i in range(6)]
                target[...] = jnp.concatenate(parts, axis=1)


def pack_kernel(lb, gb, ob, ng, ns, db, ub, pack_o):
    width = pack_o.shape[1]
    pack_o[...] = jnp.zeros(pack_o.shape, f32)
    at = 0
    for ref in (lb, gb, ob, ng, ns, db):
        pack_o[at : at + ref.shape[0], :] = ref[...].astype(f32)
        at += ref.shape[0]
    for i in range(ub.shape[1] // width):
        pack_o[at + i : at + i + 1, :] = ub[:, i * width : (i + 1) * width].astype(f32)


def packed(rows, width):
    return pl.pallas_call(
        pack_kernel,
        out_shape=jax.ShapeDtypeStruct((16, width), f32),
        in_specs=[pl.BlockSpec(memory_space=pltpu.VMEM)] * 7,
        out_specs=pl.BlockSpec(memory_space=pltpu.VMEM),
        compiler_params=pltpu.CompilerParams(vmem_limit_bytes=VMEM_BYTES),
        name="packed",
    )(*rows)


def prepare(ids, local_w, global_w):
    width = local_w.shape[0]
    vm = pl.BlockSpec(memory_space=pltpu.VMEM)
    hbm = pl.BlockSpec(memory_space=pl.ANY)
    chosen = jax.ShapeDtypeStruct((width, 6 * width // 4), bf16)
    return pl.pallas_call(
        prepare_kernel,
        out_shape=[chosen, chosen],
        in_specs=[pl.BlockSpec(memory_space=pltpu.SMEM), hbm, hbm],
        out_specs=[vm] * 2,
        scratch_shapes=[
            pltpu.VMEM((2, 6, width, 256), bf16),
            pltpu.SemaphoreType.DMA((12,)),
        ],
        compiler_params=pltpu.CompilerParams(vmem_limit_bytes=VMEM_BYTES),
        cost_estimate=cost(3),
        name="prepare",
    )(ids, local_w, global_w)


def attend_kernel(layer, *refs):
    count = 4
    sources = 7 if layer == 0 else 4
    ids, parts, refs = refs[0], refs[1 : 1 + sources], refs[1 + sources :]
    (
        w_a, w_b, pack_a, pack_b, prow, pcol,
        c0, c1, c2, c3, u_o, own_o, q_o, k_o, v_o, gk_o, gv_o, gq_o, kg_o, vg_o, lse_o,
        w_s, sem, vt_s, mask_s, ctx_s, gctx_s,
    ) = refs
    rows = c0.shape[0]
    heads = q_o.shape[0]
    hw = heads * HEAD
    scale = HEAD ** (-0.5)
    glob = prow.shape[1]
    group, core = ids[0], ids[4]
    w_copy = choose((core != layer).astype(jnp.int32), w_a, w_b, w_s, sem)
    if layer == 0:
        block = parts[0]
        half = rows // 2
        u_o[pl.ds(pl.multiple_of((2 * ids[5] + ids[6]) * rows, rows), rows), :] = block[ids[5]]
        places = (
            2 * ids[5] + 1 - ids[6],
            2 * (1 - ids[5]) + ids[6],
            2 * (1 - ids[5]) + 1 - ids[6],
        )
        for i, place in enumerate(places):
            for part, side in ((parts[1 + i], core), (parts[4 + i], 1 - core)):
                at = pl.multiple_of(place * rows + side * half, half)
                u_o[pl.ds(at, half), :] = part[...]
    else:
        for r in range(count):
            u_o[pl.ds(pl.multiple_of(ids[r] * rows, rows), rows), :] = parts[r][...]
    own_o[...] = u_o[pl.ds(pl.multiple_of(group * rows, rows), rows), :]
    pack = jnp.where(core == layer, pack_a[...], pack_b[...])[:4]
    hb = pack[:, :hw]
    for i in range(1, 4):
        hb = jnp.where(group == i, pack[:, i * hw : (i + 1) * hw], hb)
    kg_all = jnp.zeros((glob, hw), f32)
    vg_all = jnp.zeros((glob, hw), f32)
    ug_all = jnp.zeros((glob, u_o.shape[1]), f32)
    first = lax.broadcasted_iota(jnp.int32, (rows, HEAD), 1) == 0
    w_copy.wait()
    w = w_s
    for chunk in range(count):
        at = slice(chunk * rows, (chunk + 1) * rows)
        x = u_o[at, :]
        p = nn(x, w[:, : 5 * hw])
        queries = (p[:, :hw] + hb[0:1, :]).astype(bf16).astype(f32) * scale
        keys = p[:, hw : 2 * hw]
        values = p[:, 2 * hw : 3 * hw] + hb[1:2, :]
        gkeys = p[:, 3 * hw : 4 * hw]
        gvalues = p[:, 4 * hw : 5 * hw] + hb[3:4, :]
        is_global = jnp.max(owner_rows(prow, chunk, rows), axis=1, keepdims=True)
        tail_k = jnp.where(first, is_global * far_below, 0.0)
        tail_q = jnp.where(first, 1.0, 0.0)
        for h in range(heads):
            cut = slice(HEAD * h, HEAD * h + HEAD)
            q_o[h, at, :] = jnp.concatenate([queries[:, cut], tail_q], axis=1).astype(bf16)
            k_o[h, at, :] = jnp.concatenate([keys[:, cut], tail_k], axis=1).astype(bf16)
            v_o[h, at, :] = values[:, cut].astype(bf16)
            gk_o[h, at, :] = gkeys[:, cut].astype(bf16)
            gv_o[h, at, :] = gvalues[:, cut].astype(bf16)
            vt_s[h, chunk] = values[:, cut].T.astype(bf16)
        hit = owner_cols(pcol, chunk, rows).astype(bf16)
        kg_all += nn(hit, keys.astype(bf16))
        vg_all += nn(hit, values.astype(bf16))
        ug_all += nn(hit, x)
    gq_all = (nn(ug_all.astype(bf16), w[:, 5 * hw :]) + hb[2:3, :]).astype(bf16).astype(f32) * scale
    none = jnp.zeros((glob, HEAD), f32)
    for h in range(heads):
        cut = slice(HEAD * h, HEAD * h + HEAD)
        gq_o[h] = gq_all[:, cut].astype(bf16)
        kg_o[h] = jnp.concatenate([kg_all[:, cut], none], axis=1).astype(bf16)
        vg_o[h] = vg_all[:, cut].astype(bf16)

    def head(h, carry):
        band_masks(mask_s, is_dilated(layer, group, h), rows)
        kg = kg_o[h]
        vgt = vg_o[h].astype(f32).T.astype(bf16)
        for qb in range(count):
            q = q_o[h, qb * rows : (qb + 1) * rows, :]
            near = neighbours(qb, count)
            scores = [
                nt(k_o[h, kb * rows : (kb + 1) * rows, :], q) + mask_s[kb - qb + 1] for kb in near
            ]
            side = nt(kg, q)
            peak = jnp.max(side, axis=0, keepdims=True)
            for s in scores:
                peak = jnp.maximum(peak, jnp.max(s, axis=0, keepdims=True))
            side = jnp.exp(side - peak)
            scores = [jnp.exp(s - peak) for s in scores]
            total = jnp.sum(side, axis=0, keepdims=True)
            for s in scores:
                total += jnp.sum(s, axis=0, keepdims=True)
            inverse = 1.0 / total
            ctx = nn(vgt, (side * inverse).astype(bf16))
            for kb, s in zip(near, scores):
                ctx += nn(vt_s[h, kb], (s * inverse).astype(bf16))
            ctx_s[h, qb * rows : (qb + 1) * rows, :] = ctx.T
            lse_o[h, qb : qb + 1, :] = peak + jnp.log(total)
        spread = nt(gq_o[h], gk_o[h])
        e = jnp.exp(spread - jnp.max(spread, axis=1, keepdims=True))
        prob = (e / jnp.sum(e, axis=1, keepdims=True)).astype(bf16)
        gctx_s[h] = nn(prob, gv_o[h])
        return carry

    lax.fori_loop(0, heads, head, 0)
    gctx = jnp.concatenate([gctx_s[h] for h in range(heads)], axis=1).astype(bf16)
    for r, c_o in enumerate((c0, c1, c2, c3)):
        chunk = ids[r]
        at = pl.ds(pl.multiple_of(chunk * rows, rows), rows)
        hit = owner_rows(prow, chunk, rows)
        placed = nn(hit.astype(bf16), gctx)
        local = jnp.concatenate([ctx_s[h, at, :] for h in range(heads)], axis=1)
        c_o[...] = jnp.where(jnp.max(hit, axis=1, keepdims=True) > 0, placed, local).astype(bf16)


def attend(layer, ids, parts, weights, packs, prow, pcol):
    width = weights[0].shape[0]
    hw = weights[0].shape[1] // 6
    heads = hw // HEAD
    glob = prow.shape[1]
    rows = HALF
    full = 4 * rows
    sds = jax.ShapeDtypeStruct
    outs = [sds((rows, hw), bf16)] * 4 + [
        sds((full, width), bf16),
        sds((rows, width), bf16),
        sds((heads, full, 2 * HEAD), bf16),
        sds((heads, full, 2 * HEAD), bf16),
        sds((heads, full, HEAD), bf16),
        sds((heads, full, HEAD), bf16),
        sds((heads, full, HEAD), bf16),
        sds((heads, glob, HEAD), bf16),
        sds((heads, glob, 2 * HEAD), bf16),
        sds((heads, glob, HEAD), bf16),
        sds((heads, 4, rows), f32),
    ]
    vm = pl.BlockSpec(memory_space=pltpu.VMEM)
    hbm = pl.BlockSpec(memory_space=pl.ANY)
    res = pl.pallas_call(
        partial(attend_kernel, layer),
        out_shape=outs,
        in_specs=[pl.BlockSpec(memory_space=pltpu.SMEM)]
        + [vm] * len(parts)
        + [hbm] * 2
        + [vm] * 4,
        out_specs=[vm] * len(outs),
        scratch_shapes=[
            pltpu.VMEM(weights[0].shape, bf16),
            pltpu.SemaphoreType.DMA,
            pltpu.VMEM((heads, 4, HEAD, rows), bf16),
            pltpu.VMEM((3, rows, rows), f32),
            pltpu.VMEM((heads, full, HEAD), f32),
            pltpu.VMEM((heads, glob, HEAD), f32),
        ],
        compiler_params=pltpu.CompilerParams(vmem_limit_bytes=VMEM_BYTES),
        cost_estimate=cost(14),
        name="attend",
    )(ids, *parts, *weights, *packs, prow, pcol)
    return res[:4], res[4], res[5], res[6:]


def attend_back_kernel(
    layer, ids, d0, d1, d2, d3, q, k, v, gk, gv, gq, kg, vg, lse, prow, pcol, w_a, w_b,
    d_o, bias_o, p0, p1, p2, p3,
    w_s, sem, mask_s, do_s, dog_s, dq_s, dk_s, dv_s, dkg_s, dvg_s, dgk_s, dgv_s, dgq_s,
):
    rows = d0.shape[0]
    heads = q.shape[0]
    count = 4
    scale = HEAD ** (-0.5)
    glob = prow.shape[1]
    w_copy = choose((ids[4] != layer).astype(jnp.int32), w_a, w_b, w_s, sem)
    dg_all = jnp.zeros((glob, heads * HEAD), f32)
    for r, d in enumerate((d0, d1, d2, d3)):
        chunk = ids[r]
        at = pl.ds(pl.multiple_of(chunk * rows, rows), rows)
        dx = d[...]
        dg_all += nn(owner_cols(pcol, chunk, rows).astype(bf16), dx)
        is_global = jnp.max(owner_rows(prow, chunk, rows), axis=1, keepdims=True)
        local = jnp.where(is_global > 0, 0.0, dx.astype(f32))
        for h in range(heads):
            do_s[h, at, :] = local[:, HEAD * h : HEAD * h + HEAD].astype(bf16)
    for h in range(heads):
        dog_s[h] = dg_all[:, HEAD * h : HEAD * h + HEAD].astype(bf16)

    def head(h, carry):
        band_masks(mask_s, is_dilated(layer, ids[0], h), rows)
        kgh = kg[h]
        vgh = vg[h]
        kgt = kgh[:, :HEAD].astype(f32).T.astype(bf16)
        kt = [
            k[h, b * rows : (b + 1) * rows, :][:, :HEAD].astype(f32).T.astype(bf16)
            for b in range(count)
        ]
        dk = [jnp.zeros((rows, 2 * HEAD), f32) for _ in range(count)]
        dv = [jnp.zeros((rows, HEAD), f32) for _ in range(count)]
        dkg = jnp.zeros((glob, 2 * HEAD), f32)
        dvg = jnp.zeros((glob, HEAD), f32)
        for qb in range(count):
            span = slice(qb * rows, (qb + 1) * rows)
            qq = q[h, span, :]
            do = do_s[h, span, :]
            row = lse[h, qb : qb + 1, :]
            near = neighbours(qb, count)
            prob = [
                jnp.exp(nt(k[h, b * rows : (b + 1) * rows, :], qq) + mask_s[b - qb + 1] - row)
                for b in near
            ]
            side = jnp.exp(nt(kgh, qq) - row)
            dprob = [nt(v[h, b * rows : (b + 1) * rows, :], do) for b in near]
            dside = nt(vgh, do)
            inner = jnp.sum(side * dside, axis=0, keepdims=True)
            for p, dp in zip(prob, dprob):
                inner += jnp.sum(p * dp, axis=0, keepdims=True)
            ds = (side * (dside - inner)).astype(bf16)
            dvg += nn(side.astype(bf16), do)
            dkg += nn(ds, qq)
            dq = nn(kgt, ds)
            for b, p, dp in zip(near, prob, dprob):
                ds = (p * (dp - inner)).astype(bf16)
                dv[b] += nn(p.astype(bf16), do)
                dk[b] += nn(ds, qq)
                dq += nn(kt[b], ds)
            dq_s[h, span, :] = dq.T * scale
        for b in range(count):
            dk_s[h, b * rows : (b + 1) * rows, :] = dk[b][:, :HEAD]
            dv_s[h, b * rows : (b + 1) * rows, :] = dv[b]
        dkg_s[h] = dkg[:, :HEAD]
        dvg_s[h] = dvg
        spread = nt(gk[h], gq[h])
        e = jnp.exp(spread - jnp.max(spread, axis=0, keepdims=True))
        p = e / jnp.sum(e, axis=0, keepdims=True)
        dog = dog_s[h]
        dp = nt(gv[h], dog)
        ds = (p * (dp - jnp.sum(p * dp, axis=0, keepdims=True))).astype(bf16)
        dgv_s[h] = nn(p.astype(bf16), dog)
        dgk_s[h] = nn(ds, gq[h])
        dgq_s[h] = tn(ds, gk[h]) * scale
        return carry

    lax.fori_loop(0, heads, head, 0)

    def wide(ref, at=None):
        parts = [ref[h] if at is None else ref[h, at, :] for h in range(heads)]
        return jnp.concatenate(parts, axis=1)

    dkg_all = wide(dkg_s).astype(bf16)
    dvg_all = wide(dvg_s).astype(bf16)
    dgq_all = wide(dgq_s).astype(bf16)
    sums = [jnp.zeros((1, heads * HEAD), f32) for _ in range(4)]
    w_copy.wait()
    for r, p_o in enumerate((p0, p1, p2, p3)):
        chunk = ids[r]
        at = pl.ds(pl.multiple_of(chunk * rows, rows), rows)
        hit = owner_rows(prow, chunk, rows).astype(bf16)
        dq = wide(dq_s, at)
        dk = wide(dk_s, at) + nn(hit, dkg_all)
        dv = wide(dv_s, at) + nn(hit, dvg_all)
        dgk = wide(dgk_s, at)
        dgv = wide(dgv_s, at)
        dgq = nn(hit, dgq_all)
        joint = jnp.concatenate([dq, dk, dv, dgk, dgv, dgq], axis=1).astype(bf16)
        d_o[at, :] = joint
        p_o[...] = nt(joint, w_s[...]).astype(p_o.dtype)
        for i, part in enumerate((dq, dv, dgq, dgv)):
            sums[i] += jnp.sum(part, axis=0, keepdims=True)
    bias_o[...] = jnp.concatenate(sums, axis=0)


def attend_back(layer, ids, pieces, kept, prow, pcol, weights):
    rows, hw = pieces[0].shape
    width = weights[0].shape[0]
    heads = hw // HEAD
    glob = prow.shape[1]
    full = 4 * rows
    vm = pl.BlockSpec(memory_space=pltpu.VMEM)
    hbm = pl.BlockSpec(memory_space=pl.ANY)
    big = (heads, full, HEAD)
    small = (heads, glob, HEAD)
    res = pl.pallas_call(
        partial(attend_back_kernel, layer),
        out_shape=[
            jax.ShapeDtypeStruct((full, 6 * hw), bf16),
            jax.ShapeDtypeStruct((4, hw), f32),
        ]
        + [jax.ShapeDtypeStruct((rows, width), t) for t in (f32, bf16, f32, bf16)],
        in_specs=[pl.BlockSpec(memory_space=pltpu.SMEM)] + [vm] * 15 + [hbm] * 2,
        out_specs=[vm] * 6,
        scratch_shapes=[
            pltpu.VMEM(weights[0].shape, bf16),
            pltpu.SemaphoreType.DMA,
            pltpu.VMEM((3, rows, rows), f32),
            pltpu.VMEM(big, bf16),
            pltpu.VMEM(small, bf16),
            pltpu.VMEM(big, f32),
            pltpu.VMEM(big, f32),
            pltpu.VMEM(big, f32),
            pltpu.VMEM(small, f32),
            pltpu.VMEM(small, f32),
            pltpu.VMEM(big, f32),
            pltpu.VMEM(big, f32),
            pltpu.VMEM(small, f32),
        ],
        compiler_params=pltpu.CompilerParams(vmem_limit_bytes=VMEM_BYTES),
        cost_estimate=cost(18),
        name="attend_back",
    )(ids, *pieces, *kept, prow, pcol, *weights)
    return res[0], res[1], res[2:]


def fetch(first, second, use_second, pairs, sems):
    for flag, source in ((0, first), (1, second)):

        @pl.when(use_second.astype(jnp.int32) == flag)
        def _(source=source):
            for i, (pick, target) in enumerate(pairs):
                pltpu.make_async_copy(pick(source), target, sems.at[i]).start()

    def wait(i):
        pick, target = pairs[i]
        pltpu.make_async_copy(pick(first), target, sems.at[i]).wait()

    return wait


def weight_pairs(steps, cols, wo_s, wu_s, wd_s):
    pairs = [(lambda w: w[0], wo_s)]
    for j in range(steps):
        pairs.append((lambda w, j=j: w[1].at[:, pl.ds(j * cols, cols)], wu_s.at[j]))
        pairs.append((lambda w, j=j: w[2].at[pl.ds(j * cols, cols), :], wd_s.at[j]))
    return pairs


def row_norm(z):
    center = z - jnp.mean(z, axis=1, keepdims=True)
    scaled = lax.rsqrt(jnp.mean(center * center, axis=1, keepdims=True) + norm_eps)
    return center * scaled, scaled


def rows_kernel(
    layer, ids, c0, c1, c2, c3, u, pack_a, pack_b, wo_a, wo_b, wu_a, wu_b, wd_a, wd_b,
    y_o, fwd_o, slope_o, unit1_o, unit2_o, scale1_o, scale2_o,
    wo_s, wu_s, wd_s, sems,
):
    steps, cols = wu_s.shape[0], wu_s.shape[2]
    pairs = weight_pairs(steps, cols, wo_s, wu_s, wd_s)
    wait = fetch((wo_a, wu_a, wd_a), (wo_b, wu_b, wd_b), ids[4] != layer, pairs, sems)
    pack = jnp.where(ids[4] == layer, pack_a[...], pack_b[...])
    hw = c0.shape[1]
    width = 4 * hw
    pieces = [c[...] for c in (c0, c1, c2, c3)]
    for a in range(4):
        part = pieces[0]
        for r in range(1, 4):
            part = jnp.where(ids[r] == a, pieces[r].astype(f32), part.astype(f32))
        fwd_o[:, width + a * hw : width + (a + 1) * hw] = part.astype(bf16)
    wait(0)
    attn = nn(fwd_o[:, width : 2 * width], wo_s[...]) + pack[4:5, :]
    unit1, scale1 = row_norm(u[...].astype(f32) + attn)
    mixed = unit1 * pack[5:6, :] + pack[7:8, :]
    low = mixed.astype(bf16)
    fwd_o[:, :width] = low
    unit1_o[...] = unit1
    scale1_o[...] = jnp.broadcast_to(scale1, scale1_o.shape)
    branch = jnp.zeros(mixed.shape, f32)
    for j in range(steps):
        wait(1 + 2 * j)
        pre = nn(low, wu_s[j]) + pack[10 + j : 11 + j, :]
        gauss = 0.5 * (1.0 + lax.erf(pre * (2.0 ** -0.5)))
        act = (pre * gauss).astype(bf16)
        bell = jnp.exp(-0.5 * pre * pre) * ((2.0 * np.pi) ** -0.5)
        slope_o[:, j * cols : (j + 1) * cols] = (gauss + pre * bell).astype(bf16)
        fwd_o[:, 2 * width + j * cols : 2 * width + (j + 1) * cols] = act
        wait(2 + 2 * j)
        branch += nn(act, wd_s[j])
    unit2, scale2 = row_norm(mixed + (branch + pack[9:10, :]))
    unit2_o[...] = unit2
    scale2_o[...] = jnp.broadcast_to(scale2, scale2_o.shape)
    y_o[...] = (unit2 * pack[6:7, :] + pack[8:9, :]).astype(bf16)


def rows_forward(layer, ids, pieces, u, packs, own, other):
    rows, width = u.shape
    ff = own[1].shape[1]
    steps = ff // width
    vm = pl.BlockSpec(memory_space=pltpu.VMEM)
    hbm = pl.BlockSpec(memory_space=pl.ANY)
    sds = jax.ShapeDtypeStruct
    return pl.pallas_call(
        partial(rows_kernel, layer),
        out_shape=[
            sds((rows, width), bf16),
            sds((rows, 2 * width + ff), bf16),
            sds((rows, ff), bf16),
            sds((rows, width), f32),
            sds((rows, width), f32),
            sds((rows, 128), f32),
            sds((rows, 128), f32),
        ],
        in_specs=[pl.BlockSpec(memory_space=pltpu.SMEM)] + [vm] * 7 + [hbm] * 6,
        out_specs=[vm] * 7,
        scratch_shapes=[
            pltpu.VMEM((width, width), bf16),
            pltpu.VMEM((steps, width, width), bf16),
            pltpu.VMEM((steps, width, width), bf16),
            pltpu.SemaphoreType.DMA((1 + 2 * steps,)),
        ],
        compiler_params=pltpu.CompilerParams(vmem_limit_bytes=VMEM_BYTES),
        cost_estimate=cost(10),
        name="rows_forward",
    )(ids, *pieces, u, *packs, own[0], other[0], own[1], other[1], own[2], other[2])


def norm_inward(unit, scaled, gain, upstream):
    d_unit = upstream * gain
    return scaled * (
        d_unit
        - jnp.mean(d_unit, axis=1, keepdims=True)
        - unit * jnp.mean(d_unit * unit, axis=1, keepdims=True)
    )


def rows_back_kernel(
    layer, ids, up, unit1, unit2, scale1, scale2, slope, pack_a, pack_b, wo_a, wo_b, wu_a, wu_b, wd_a, wd_b,
    first_o, d0, d1, d2, d3, keep_o, send_o, small_o,
    wo_s, wu_s, wd_s, sems,
):
    steps, cols = wu_s.shape[0], wu_s.shape[2]
    pairs = weight_pairs(steps, cols, wo_s, wu_s, wd_s)
    wait = fetch((wo_a, wu_a, wd_a), (wo_b, wu_b, wd_b), ids[4] != layer, pairs, sems)
    pack = jnp.where(ids[4] == layer, pack_a[...], pack_b[...])
    side = ids[4]
    half = first_o.shape[1] // 2
    ffh = keep_o.shape[1] - 2 * half

    def split(value, at):
        for s in range(2):

            @pl.when(side == s)
            def _(s=s):
                keep_o[:, at : at + half] = value[:, s * half : (s + 1) * half]
                send_o[:, at : at + half] = value[:, (1 - s) * half : (2 - s) * half]

    def total(value):
        return jnp.sum(value, axis=0, keepdims=True)

    upstream = up[...].astype(f32)
    unit = unit2[...]
    small_o[0:1, :] = total(upstream * unit)
    small_o[1:2, :] = total(upstream)
    d_second = norm_inward(unit, scale2[:, :1], pack[6:7, :], upstream)
    d_branch = d_second.astype(bf16)
    split(d_branch, ffh)
    small_o[5:6, :] = total(d_branch.astype(f32))
    d_mixed = d_second
    for j in range(steps):
        wait(2 + 2 * j)
        d_act = nt(d_branch, wd_s[j])
        d_pre = (d_act * slope[:, j * cols : (j + 1) * cols].astype(f32)).astype(bf16)
        small_o[6 + j : 7 + j, :] = total(d_pre.astype(f32))
        place = slice((j % (steps // 2)) * cols, (j % (steps // 2) + 1) * cols)

        @pl.when(side == j // (steps // 2))
        def _(d_pre=d_pre, place=place):
            keep_o[:, place] = d_pre

        @pl.when(side != j // (steps // 2))
        def _(d_pre=d_pre, place=place):
            send_o[:, place] = d_pre

        wait(1 + 2 * j)
        d_mixed += nt(d_pre, wu_s[j])
    unit = unit1[...]
    small_o[2:3, :] = total(d_mixed * unit)
    small_o[3:4, :] = total(d_mixed)
    d_first = norm_inward(unit, scale1[:, :1], pack[5:6, :], d_mixed)
    first_o[...] = d_first
    d_attn = d_first.astype(bf16)
    split(d_attn, ffh + half)
    small_o[4:5, :] = total(d_attn.astype(f32))
    small_o[10:, :] = jnp.zeros((small_o.shape[0] - 10, small_o.shape[1]), f32)
    wait(0)
    d_ctx = nt(d_attn, wo_s[...])
    hw = d0.shape[1]
    parts = [d_ctx[:, a * hw : (a + 1) * hw] for a in range(4)]
    for r, d_o in enumerate((d0, d1, d2, d3)):
        part = parts[0]
        for a in range(1, 4):
            part = jnp.where(ids[r] == a, parts[a], part)
        d_o[...] = part.astype(bf16)


def rows_back(layer, ids, upstream, kept, packs, own, other):
    rows, width = upstream.shape
    ff = own[1].shape[1]
    steps = ff // width
    hw = width // 4
    unit1, unit2, scale1, scale2, slope = kept
    vm = pl.BlockSpec(memory_space=pltpu.VMEM)
    hbm = pl.BlockSpec(memory_space=pl.ANY)
    sds = jax.ShapeDtypeStruct
    return pl.pallas_call(
        partial(rows_back_kernel, layer),
        out_shape=[sds((rows, width), f32)]
        + [sds((rows, hw), bf16)] * 4
        + [sds((rows, ff // 2 + width), bf16)] * 2
        + [sds((16, width), f32)],
        in_specs=[pl.BlockSpec(memory_space=pltpu.SMEM)] + [vm] * 8 + [hbm] * 6,
        out_specs=[vm] * 8,
        scratch_shapes=[
            pltpu.VMEM((width, width), bf16),
            pltpu.VMEM((steps, width, width), bf16),
            pltpu.VMEM((steps, width, width), bf16),
            pltpu.SemaphoreType.DMA((1 + 2 * steps,)),
        ],
        compiler_params=pltpu.CompilerParams(vmem_limit_bytes=VMEM_BYTES),
        cost_estimate=cost(11),
        name="rows_back",
    )(
        ids, upstream, unit1, unit2, scale1, scale2, slope, *packs,
        own[0], other[0], own[1], other[1], own[2], other[2],
    )


def rows_ahead(ids, pieces, u, pack, wait, weights, fwd_s, slope_s):
    wo_s, wu_s, wd_s = weights
    steps, cols = wu_s.shape[0], wu_s.shape[2]
    hw = pieces[0].shape[1]
    width = 4 * hw
    values = [c[...].astype(f32) for c in pieces]
    for a in range(4):
        part = values[0]
        for r in range(1, 4):
            part = jnp.where(ids[r] == a, values[r], part)
        fwd_s[:, width + a * hw : width + (a + 1) * hw] = part.astype(bf16)
    wait(0)
    attn = nn(fwd_s[:, width : 2 * width], wo_s[...]) + pack[4:5, :]
    unit1, scale1 = row_norm(u[...].astype(f32) + attn)
    mixed = unit1 * pack[5:6, :] + pack[7:8, :]
    low = mixed.astype(bf16)
    fwd_s[:, :width] = low
    branch = jnp.zeros(mixed.shape, f32)
    for j in range(steps):
        wait(1 + 2 * j)
        pre = nn(low, wu_s[j]) + pack[10 + j : 11 + j, :]
        gauss = 0.5 * (1.0 + lax.erf(pre * (2.0 ** -0.5)))
        act = (pre * gauss).astype(bf16)
        bell = jnp.exp(-0.5 * pre * pre) * ((2.0 * np.pi) ** -0.5)
        slope_s[:, j * cols : (j + 1) * cols] = (gauss + pre * bell).astype(bf16)
        fwd_s[:, 2 * width + j * cols : 2 * width + (j + 1) * cols] = act
        wait(2 + 2 * j)
        branch += nn(act, wd_s[j])
    unit2, scale2 = row_norm(mixed + (branch + pack[9:10, :]))
    return unit2 * pack[6:7, :] + pack[8:9, :], (unit1, scale1), (unit2, scale2)


def rows_behind(ids, upstream, norm1, norm2, pack, wait, weights, slope_s, outs):
    first_o, pieces, keep_s, send_s, small_o = outs
    wo_s, wu_s, wd_s = weights
    steps, cols = wu_s.shape[0], wu_s.shape[2]
    side = ids[4]
    half = first_o.shape[1] // 2
    ffh = keep_s.shape[1] - 2 * half

    def split(value, at):
        for s in range(2):

            @pl.when(side == s)
            def _(s=s):
                keep_s[:, at : at + half] = value[:, s * half : (s + 1) * half]
                send_s[:, at : at + half] = value[:, (1 - s) * half : (2 - s) * half]

    def total(value):
        return jnp.sum(value, axis=0, keepdims=True)

    unit, scaled = norm2
    small_o[0:1, :] = total(upstream * unit)
    small_o[1:2, :] = total(upstream)
    d_second = norm_inward(unit, scaled, pack[6:7, :], upstream)
    d_branch = d_second.astype(bf16)
    split(d_branch, ffh)
    small_o[5:6, :] = total(d_branch.astype(f32))
    d_mixed = d_second
    for j in range(steps):
        wait(2 + 2 * j)
        d_act = nt(d_branch, wd_s[j])
        d_pre = (d_act * slope_s[:, j * cols : (j + 1) * cols].astype(f32)).astype(bf16)
        small_o[6 + j : 7 + j, :] = total(d_pre.astype(f32))
        place = slice((j % (steps // 2)) * cols, (j % (steps // 2) + 1) * cols)

        @pl.when(side == j // (steps // 2))
        def _(d_pre=d_pre, place=place):
            keep_s[:, place] = d_pre

        @pl.when(side != j // (steps // 2))
        def _(d_pre=d_pre, place=place):
            send_s[:, place] = d_pre

        wait(1 + 2 * j)
        d_mixed += nt(d_pre, wu_s[j])
    unit, scaled = norm1
    small_o[2:3, :] = total(d_mixed * unit)
    small_o[3:4, :] = total(d_mixed)
    d_first = norm_inward(unit, scaled, pack[5:6, :], d_mixed)
    first_o[...] = d_first
    d_attn = d_first.astype(bf16)
    split(d_attn, ffh + half)
    small_o[4:5, :] = total(d_attn.astype(f32))
    small_o[10:, :] = jnp.zeros((small_o.shape[0] - 10, small_o.shape[1]), f32)
    wait(0)
    d_ctx = nt(d_attn, wo_s[...])
    hw = pieces[0].shape[1]
    parts = [d_ctx[:, a * hw : (a + 1) * hw] for a in range(4)]
    for r, d_o in enumerate(pieces):
        part = parts[0]
        for a in range(1, 4):
            part = jnp.where(ids[r] == a, parts[a], part)
        d_o[...] = part.astype(bf16)


def own_pack(layer, ids, pack_a, pack_b):
    return jnp.where(ids[4] == layer, pack_a[...], pack_b[...])


def rows_both_kernel(
    ids, c0, c1, c2, c3, u, up, pack_a, pack_b, wo_a, wo_b, wu_a, wu_b, wd_a, wd_b,
    y_o, first_o, d0, d1, d2, d3, small_o, keep_o, send_o, fwd_h,
    fwd_s, slope_s, out_sem, wo_s, wu_s, wd_s, sems,
):
    steps, cols = wu_s.shape[0], wu_s.shape[2]
    pairs = weight_pairs(steps, cols, wo_s, wu_s, wd_s)
    wait = fetch((wo_a, wu_a, wd_a), (wo_b, wu_b, wd_b), ids[4] != 1, pairs, sems)
    pack = own_pack(1, ids, pack_a, pack_b)
    weights = (wo_s, wu_s, wd_s)
    y, norm1, norm2 = rows_ahead(ids, (c0, c1, c2, c3), u, pack, wait, weights, fwd_s, slope_s)
    out = pltpu.make_async_copy(fwd_s, fwd_h, out_sem)
    out.start()
    y_o[...] = y.astype(bf16)
    rows_behind(
        ids, up[...].astype(f32), norm1, norm2, pack, lambda i: None, weights, slope_s,
        (first_o, (d0, d1, d2, d3), keep_o, send_o, small_o),
    )
    out.wait()


def rows_both(ids, pieces, u, upstream, packs, own, other):
    rows, width = u.shape
    ff = own[1].shape[1]
    steps = ff // width
    vm = pl.BlockSpec(memory_space=pltpu.VMEM)
    hbm = pl.BlockSpec(memory_space=pl.ANY)
    sds = jax.ShapeDtypeStruct
    res = pl.pallas_call(
        rows_both_kernel,
        out_shape=[sds((rows, width), bf16), sds((rows, width), f32)]
        + [sds((rows, width // 4), bf16)] * 4
        + [sds((16, width), f32)]
        + [sds((rows, ff // 2 + width), bf16)] * 2
        + [sds((rows, 2 * width + ff), bf16)],
        in_specs=[pl.BlockSpec(memory_space=pltpu.SMEM)] + [vm] * 8 + [hbm] * 6,
        out_specs=[vm] * 9 + [hbm],
        scratch_shapes=[
            pltpu.VMEM((rows, 2 * width + ff), bf16),
            pltpu.VMEM((rows, ff), bf16),
            pltpu.SemaphoreType.DMA,
            pltpu.VMEM((width, width), bf16),
            pltpu.VMEM((steps, width, width), bf16),
            pltpu.VMEM((steps, width, width), bf16),
            pltpu.SemaphoreType.DMA((1 + 2 * steps,)),
        ],
        compiler_params=pltpu.CompilerParams(vmem_limit_bytes=VMEM_BYTES),
        cost_estimate=cost(15),
        name="rows_both",
    )(
        ids, *pieces, u, upstream, *packs, own[0], other[0], own[1], other[1], own[2], other[2],
    )
    return res[0], res[9], res[1:9]


def grads_kernel(layer, ids, f0, f1, k0, k1, *refs):
    count = 1 if layer == 1 else 6
    targets, outs, (f, b, in_sems, out_sems) = refs[:count], refs[count : 2 * count], refs[2 * count :]
    rows = f0.shape[0]
    part = f0.shape[1] // 12
    width = 2 * part
    ffh = k0.shape[1] - width
    ins = []
    for at, n in [(None, None), (0, 2 * width)] + [(width * (2 + i), width) for i in range(4)]:
        for side, (fx, kx) in enumerate(((f0, k0), (f1, k1))):
            to = pl.ds(side * rows, rows)
            pair = (kx, b.at[to, :]) if at is None else (fx.at[:, pl.ds(at, n)], f.at[to, pl.ds(at, n)])
            ins += start_all(moves([pair], in_sems, len(ins)))
    wait_all(ins[:4])
    pre, branch, attn = b[:, :ffh], b[:, ffh : ffh + part], b[:, ffh + part :]
    if layer == 1:
        out, out_h = outs[0], targets[0]
        few, many = width // 16, 8 * part // 16
        blocks = ffh // part
        for j in range(2):
            at = j * part
            up = tn(f[:, at : at + part], pre).astype(bf16)
            last = tn(f[:, width + at : width + at + part], attn).astype(bf16)
            for s in range(8):
                cut = slice(s * few, (s + 1) * few)
                for i in range(blocks):
                    out[8 * j + s, i * few : (i + 1) * few, :] = up[cut, i * part : (i + 1) * part]
                out[8 * j + s, blocks * few : (blocks + 1) * few, :] = last[cut]
        sent = []
        for j in range(8):
            if j % 2 == 0:
                wait_all(ins[4 + j : 6 + j])
            at = 2 * width + j * part
            down = tn(f[:, at : at + part], branch).astype(bf16)
            for s in range(2):
                out[2 * j + s, (blocks + 1) * few :, :] = down[s * many : (s + 1) * many]
            pair = pl.ds(2 * j, 2)
            sent += start_all(moves([(out.at[pair], out_h.at[pair])], out_sems, j))
        wait_all(sent)
        return
    ua_o, ub_o, uk_o, da_o, db_o, dk_o = outs
    ua = ua_o.shape[1]
    small = dk_o.shape[1]
    sub = small // 2

    def rows_at(at):
        return f[:, pl.ds(pl.multiple_of(at, 128), part)]

    start = (1 - ids[5]) * part
    up = tn(rows_at(start), pre).astype(bf16)
    ua_o[...] = up[:, :ua]
    ub_o[:, : ffh - ua] = up[:, ua:]
    ub_o[:, ffh - ua :] = tn(rows_at(start + width), attn).astype(bf16)
    sent = start_all(moves(list(zip(outs[:2], targets[:2])), out_sems))
    start = ids[5] * part
    uk_o[:, :ffh] = tn(rows_at(start), pre).astype(bf16)
    uk_o[:, ffh:] = tn(rows_at(start + width), attn).astype(bf16)
    sent += start_all(moves([(uk_o, targets[2])], out_sems, 2))
    for j in range(8):
        if j % 2 == 0:
            wait_all(ins[4 + j : 6 + j])
        at = 2 * width + 2 * small * j
        down = tn(f[:, at : at + 2 * small], branch).astype(bf16)
        for low in range(2):
            block = down[small * low : small * (low + 1)]
            share = 2 * j + low
            place, mine = (share // 8) * 4 + share % 4, ids[6] == (share // 4) % 2

            @pl.when(mine)
            def _(block=block, place=place):
                dk_o[place] = block

            @pl.when(jnp.logical_not(mine))
            def _(block=block, place=place):
                da_o[place] = block[:sub]
                db_o[place] = block[sub:]

    wait_all(sent + start_all(moves(list(zip(outs[3:], targets[3:])), out_sems, 3)))


def grads(layer, ids, fwd, fwd_other, keep, got):
    width = HEAD * 12
    ff = 2 * (keep.shape[1] - width)
    part = width // 2
    ua = 1024
    small = ff // 16
    hbm = pl.BlockSpec(memory_space=pl.ANY)
    shapes = [
        (part, ua),
        (part, ff // 2 + part - ua),
        (part, ff // 2 + part),
        (8, small // 2, part),
        (8, small // 2, part),
        (8, small, part),
    ]
    if layer == 1:
        shapes = [(16, (ff // 2 // part + 1) * width // 16 + ff // 16, part)]
    return pl.pallas_call(
        partial(grads_kernel, layer),
        out_shape=[jax.ShapeDtypeStruct(shape, bf16) for shape in shapes],
        in_specs=[pl.BlockSpec(memory_space=pltpu.SMEM)] + [hbm] * 4,
        out_specs=[hbm] * len(shapes),
        scratch_shapes=[pltpu.VMEM(shape, bf16) for shape in shapes]
        + [
            pltpu.VMEM((2 * fwd.shape[0], fwd.shape[1]), bf16),
            pltpu.VMEM((2 * keep.shape[0], keep.shape[1]), bf16),
            pltpu.SemaphoreType.DMA((12,)),
            pltpu.SemaphoreType.DMA((8,)),
        ],
        compiler_params=pltpu.CompilerParams(vmem_limit_bytes=VMEM_BYTES),
        cost_estimate=cost(5),
        name="grads",
    )(ids, fwd, fwd_other, keep, got)


def proj_grads_kernel(ids, u_h, d_h, ra_h, rb_h, rk_h, u, d, ra_o, rb_o, rk_o, sems):
    wait_all(start_all(moves([(u_h, u), (d_h, d)], sems)))
    part = rk_o.shape[0]
    ra = ra_o.shape[1]
    rows = tn(u[:, pl.ds(pl.multiple_of((1 - ids[5]) * part, 128), part)], d[...]).astype(bf16)
    ra_o[...] = rows[:, :ra]
    rb_o[...] = rows[:, ra:]
    out = start_all(moves([(ra_o, ra_h), (rb_o, rb_h)], sems, 2))
    rk_o[...] = tn(u[:, pl.ds(pl.multiple_of(ids[5] * part, 128), part)], d[...]).astype(bf16)
    wait_all(out + start_all(moves([(rk_o, rk_h)], sems, 4)))


def proj_grads(ids, u, d):
    part = u.shape[1] // 2
    cols = d.shape[1]
    hbm = pl.BlockSpec(memory_space=pl.ANY)
    shapes = [(part, n) for n in (640, cols - 640, cols)]
    return pl.pallas_call(
        proj_grads_kernel,
        out_shape=[jax.ShapeDtypeStruct(shape, bf16) for shape in shapes],
        in_specs=[pl.BlockSpec(memory_space=pltpu.SMEM)] + [hbm] * 2,
        out_specs=[hbm] * 3,
        scratch_shapes=[pltpu.VMEM(shape, bf16) for shape in [u.shape, d.shape] + shapes]
        + [pltpu.SemaphoreType.DMA((5,))],
        compiler_params=pltpu.CompilerParams(vmem_limit_bytes=VMEM_BYTES),
        cost_estimate=cost(4),
        name="proj_grads",
    )(ids, u, d)


def assemble_kernel(sizes, ids, fk, fg, ak, ag, up_o, out_o, down_o, local_o, glob_o):
    share_w, share_f, ff, width = sizes
    part, hw = width // 2, width // 4
    core, x = ids[4], ids[6]
    for side in range(2):

        @pl.when(core == side)
        def _(side=side):
            halves = (fk, fg) if side == 0 else (fg, fk)
            for c, ref in enumerate(halves):
                for i in range(4):
                    to = c * (ff // 2) + i * part
                    up_o[:, to : to + part] = ref[i * share_w : (i + 1) * share_w, :]
                out_o[:, c * part : (c + 1) * part] = ref[4 * share_w : 5 * share_w, :]
                down_o[:, c * part : (c + 1) * part] = ref[5 * share_w :, :]

    held = []
    for group in range(4):
        pair = [jnp.where(core == group // 2, ak[i].astype(f32), ag[i].astype(f32)) for i in range(2)]
        held.append(jnp.where(x == group % 2, pair[0], pair[1]))
    for target, kinds in ((local_o, (0, 1, 2)), (glob_o, (5, 3, 4))):
        target[...] = jnp.concatenate(
            [held[g][:, k * hw : (k + 1) * hw] for k in kinds for g in range(4)], axis=1
        )


def assemble(ids, ffn_keep, ffn_got, att_keep, att_got, sizes):
    share_w, share_f, ff, width = sizes
    vm = pl.BlockSpec(memory_space=pltpu.VMEM)
    shapes = [(share_w, ff), (share_w, width), (share_f, width)] + [(share_w, 3 * width)] * 2
    return pl.pallas_call(
        partial(assemble_kernel, sizes),
        out_shape=[jax.ShapeDtypeStruct(shape, f32) for shape in shapes],
        in_specs=[pl.BlockSpec(memory_space=pltpu.SMEM)] + [vm] * 4,
        out_specs=[vm] * 5,
        compiler_params=pltpu.CompilerParams(vmem_limit_bytes=VMEM_BYTES),
        name="assemble",
    )(ids, ffn_keep, ffn_got, att_keep, att_got)


def core_flip(v):
    return lax.ppermute(v, SECTION, [(0, 1), (1, 0)])


def seq_flip(v, by):
    return lax.ppermute(v, SEQ, [(i, i ^ by) for i in range(4)])


def core_x_flip(v):
    return lax.ppermute(v, BOTH, [(i, i ^ 5) for i in range(8)])


def dp_flip(v, by):
    return lax.ppermute(v, DP, [(i, i ^ by) for i in range(lax.axis_size(DP))])


def pick(which, options):
    result = options[-1]
    for i in range(len(options) - 2, -1, -1):
        result = jnp.where(which == i, options[i], result)
    return result


def to_section(v, layer):
    near = [(y_ * 4 + 2 * y_ + x_, layer * 4 + 2 * y_ + x_) for y_ in (0, 1) for x_ in (0, 1)]
    far = [
        ((1 - y_) * 4 + 2 * y_ + x_, layer * 4 + 2 * (1 - y_) + x_) for y_ in (0, 1) for x_ in (0, 1)
    ]
    return lax.ppermute(v, BOTH, near), lax.ppermute(v, BOTH, far)


def by_micro(first, lower, upper, y):
    mine = jnp.where(first, lower[0], upper[0])
    away = jnp.where(first, lower[1], upper[1])
    return jnp.where(y == 0, jnp.stack([mine, away]), jnp.stack([away, mine]))


def two_chips(
    layer_in, cotangent, masked_rows, global_positions, local_weight, local_bias, global_weight,
    global_bias, out_weight, out_bias, norm_gain, norm_shift, up_weight, up_bias, down_weight,
    down_bias,
):
    c = lax.axis_index(SECTION)
    q = lax.axis_index(SEQ)
    z = lax.axis_index(DP)
    dp = lax.axis_size(DP)
    y, x = q // 2, q % 2
    g = 2 * c + x
    g_other = 2 * (1 - c) + x
    rows, width = layer_in.shape[2:]
    hw = width // 4
    ff = up_weight.shape[2]
    heads = hw // HEAD
    half_rows = rows // 2
    same = c == y
    first = c == 0

    block = layer_in[:, 0]

    def half_of(micro):
        return lax.dynamic_slice(block, (micro, c * half_rows, 0), (1, half_rows, width))[0]

    mine_part, away_part = half_of(y), half_of(1 - y)
    got = [seq_flip(mine_part, 1), seq_flip(away_part, 2), seq_flip(away_part, 3)]

    cot = cotangent[:, 0]
    marks = masked_rows[:, 0]

    def of_micro(v, micro):
        return lax.dynamic_index_in_dim(v, micro, 0, keepdims=False)

    cot_away = seq_flip(of_micro(cot, 1 - y), 2)
    marks_away = seq_flip(of_micro(marks, 1 - y), 2)

    ids = jnp.stack([g, g_other, 2 * c + 1 - x, 2 * (1 - c) + 1 - x, c, y, x, z]).astype(jnp.int32)
    ids, _ = lax.optimization_barrier((ids, (mine_part, away_part)))
    w_own, w_send = prepare(ids, local_weight[0], global_weight[0])
    pack = packed(
        (local_bias[0], global_bias[0], out_bias, norm_gain[0], norm_shift[0], down_bias, up_bias),
        width,
    )
    own = (out_weight[0], up_weight[0], down_weight[0])
    other_up = core_flip(own[1])
    (w_own, pack), (got, other_up) = lax.optimization_barrier(((w_own, pack), (got, other_up)))
    weights = (w_own, core_flip(w_send))
    packs = (pack, core_flip(pack))
    positions = of_micro(global_positions[:, 0], y)
    prow = positions[None, :]
    pcol = positions[:, None]
    parts = [block] + got + [core_flip(v) for v in got]
    own_late, _ = lax.optimization_barrier(((own[0], own[2]), (parts, weights, packs)))
    other_out, other_down = [core_flip(w) for w in own_late]
    other = (other_out, other_up, other_down)

    def exchange(pieces):
        return [pieces[0], core_flip(pieces[1]), seq_flip(pieces[2], 1), core_x_flip(pieces[3])]

    saved = []
    for layer in range(2):
        ctx, u_all, u_own, kept = attend(layer, ids, parts, weights, packs, prow, pcol)
        if layer == 0:
            ctx, other = lax.optimization_barrier((ctx, other))
        pieces = exchange(ctx)
        if layer == 0:
            res = rows_forward(layer, ids, pieces, u_own, packs, own, other)
            y_low, fwd, slope, *row_kept = res
            row_kept.append(slope)
            across = seq_flip(y_low, 1)
            across, (cot_away, marks_away, fwd_other) = lax.optimization_barrier(
                (across, (cot_away, marks_away, core_flip(fwd)))
            )
            parts = [y_low, core_flip(y_low), across, core_flip(across)]
            saved_low = y_low
            saved.append((u_all, kept, fwd, fwd_other, row_kept))
        else:
            pieces, out0 = lax.optimization_barrier((pieces, to_section(saved_low, 0)))
            cot_rows = jnp.where(same, of_micro(cot, y), cot_away)
            cot_marks = jnp.where(same, of_micro(marks, y), marks_away)
            row_hit = (g * rows + jnp.arange(rows))[:, None] == cot_marks[None, :]
            upstream = nn(row_hit.astype(bf16), cot_rows).astype(bf16)
            y_low, fwd, back = rows_both(ids, pieces, u_own, upstream, packs, own, other)

    flip_x = partial(seq_flip, by=1)
    flip_y = partial(seq_flip, by=2)
    flip_z1 = partial(dp_flip, by=1)
    flip_z2 = partial(dp_flip, by=2)
    low_z, high_z = z % 2, z // 2

    def after(value, others):
        return lax.optimization_barrier((value, others))

    def cut(value, axis, bit):
        return of_axis(value, axis, 1 - bit).astype(bf16), of_axis(value, axis, bit)

    def of_axis(value, axis, index):
        return lax.dynamic_index_in_dim(value, index, axis, keepdims=False)

    def plus(keep, got):
        return keep.astype(f32) + got.astype(f32)

    def bias_rows(small, bias):
        placed = jnp.concatenate([jnp.where(g == i, bias, 0.0) for i in range(4)], axis=1)
        return jnp.concatenate([small[:10], placed], axis=0)

    def inward(partials):
        low = [core_flip(partials[1]), core_flip(partials[3])]
        return plus(partials[0], low[0]), plus(partials[2], low[1]).astype(bf16)

    ua = 1024
    share_w = width // (4 * dp)
    share_f = ff // (4 * dp)
    sub = share_f // 2
    part = width // 2

    d_first, pieces, (small, keep, send) = back[0], exchange(back[1:5]), back[5:]
    gr = grads(1, ids, fwd, core_flip(fwd), keep, core_flip(send))
    pieces, gr = after(pieces, gr)
    ffn1 = lax.psum_scatter(gr[0], SEQ, scatter_dimension=0, tiled=True)
    res = attend_back(1, ids, pieces, kept, prow, pcol, weights)
    d_all, bias, partials = res
    small1 = bias_rows(small, bias)
    summed, send = inward(partials)
    across = flip_x(send)
    d_all, send = after(d_all, send)
    gr = proj_grads(ids, u_all, d_all)
    across, gr = after(across, gr)
    r1a, r1b, r1k = gr
    d_upper = (d_first + summed + across.astype(f32)).astype(bf16)

    got_r1a = flip_y(r1a)
    u_all, kept, fwd, fwd_other, row_kept = saved[0]
    res = rows_back(0, ids, d_upper, row_kept, packs, own, other)
    res, got_r1a = after(res, got_r1a)
    d_first, pieces, (keep, send, small) = res[0], exchange(res[1:5]), res[5:]
    got_r1b = flip_y(r1b)
    gr = grads(0, ids, fwd, fwd_other, keep, core_flip(send))
    pieces, gr = after(pieces, gr)
    u0a, u0b, u0k, d0a, d0b, d0k = gr
    got_u0a, got_d0a, got_u0b, got_d0b = flip_y(u0a), flip_x(d0a), flip_y(u0b), flip_x(d0b)
    res = attend_back(0, ids, pieces, kept, prow, pcol, weights)
    (res, y_low, d_upper), (got_u0a, got_d0a, got_r1b, ffn1) = after(
        (res, y_low, d_upper), (got_u0a, got_d0a, got_r1b, ffn1)
    )
    ffn1 = lax.psum_scatter(ffn1, DP, scatter_dimension=0, tiled=True)[0]
    d_all, bias, partials = res
    small0 = bias_rows(small, bias)

    def step(flights):
        sends = lax.optimization_barrier([send for _, send in flights])
        return [flip(send) for (flip, _), send in zip(flights, sends)]

    def end(got, *more):
        return lax.optimization_barrier((got, more))

    swapped = partial(jnp.where, first)
    small_keep, small_send = swapped(small0, small1), swapped(small1, small0)
    small = small_keep + core_flip(small_send)
    r1 = plus(r1k, jnp.concatenate([got_r1a, got_r1b], axis=1)).astype(bf16)
    r1_send, r1_keep = cut(r1.reshape(2, 2, 2, share_w, -1), 2, low_z)
    summed, d_send = inward(partials)
    got = step([(flip_x, d_send), (flip_z1, r1_send), (flip_x, small)])
    gr = proj_grads(ids, u_all, d_all)
    got, ends = end(got, got_u0b, got_d0b, gr)
    got_u0b, got_d0b, (r0a, r0b, r0k) = ends

    d_lower = (d_first + summed + got[0].astype(f32)).astype(bf16)
    u0 = plus(u0k, jnp.concatenate([got_u0a, got_u0b], axis=1)).astype(bf16)
    u0_send, u0_keep = cut(u0.reshape(2, 2, 2, share_w, -1), 2, low_z)
    r1_send, r1_keep = cut(plus(r1_keep, got[1]).astype(bf16), 1, high_z)
    small = small + got[2]
    got = step([(flip_y, r0a), (flip_z1, u0_send), (flip_y, r0b), (flip_z2, r1_send)])
    d0 = plus(d0k, jnp.concatenate([got_d0a, got_d0b], axis=1)).astype(bf16)
    d0_send, d0_keep = cut(d0.reshape(2, 2, 2, share_f, part), 0, y)
    got, ends = end(got, d0_send)
    d0_send = ends[0]

    u0_send, u0_keep = cut(plus(u0_keep, got[1]).astype(bf16), 1, high_z)
    r0 = plus(r0k, jnp.concatenate([got[0], got[2]], axis=1)).astype(bf16)
    r0_send, r0_keep = cut(r0.reshape(2, 2, 2, share_w, -1), 2, low_z)
    r1_send, r1_keep = cut(plus(r1_keep, got[3]).astype(bf16), 0, x)
    got = step([(flip_z2, u0_send), (flip_y, d0_send), (flip_z1, r0_send), (flip_z1, small)])
    in0 = to_section(d_lower, 0)
    got, ends = end(got, in0, ffn1)
    (near0, far0), ffn1 = ends

    u0_send, u0_keep = cut(plus(u0_keep, got[0]).astype(bf16), 0, x)
    d0_send, d0_keep = cut(plus(d0_keep, got[1]).astype(bf16), 1, low_z)
    r0_send, r0_keep = cut(plus(r0_keep, got[2]).astype(bf16), 1, high_z)
    small = small + got[3]
    got = step([(flip_z2, r0_send), (flip_z1, d0_send), (flip_x, u0_send), (flip_y, small), (flip_x, r1_send)])
    upper = to_section(jnp.stack([y_low, d_upper]), 1)
    got, ends = end(got, upper)
    out1, (near1, far1) = [(ends[0][0][i], ends[0][1][i]) for i in range(2)]
    r1_got = got[4]

    few = 5 * share_w
    one0 = plus(u0_keep, got[2])
    d0_send, d0_keep = cut(plus(d0_keep, got[1]).astype(bf16), 0, high_z)
    r0_send, r0_keep = cut(plus(r0_keep, got[0]).astype(bf16), 0, x)
    small = small + got[3]
    got = step([(flip_z2, d0_send), (flip_x, r0_send), (flip_z2, small)])
    got = end(got)[0]
    two0 = plus(d0_keep, got[0])
    small = small + got[2]

    lower = jnp.concatenate(
        [one0[:, i * part : (i + 1) * part] for i in range(5)] + [two0], axis=0
    )
    upper = ffn1.astype(f32)
    ffn_keep, ffn_send = swapped(lower, upper), swapped(upper, lower)
    att0, att1 = jnp.stack([r0_keep, got[1]]), jnp.stack([r1_keep, r1_got])
    att_keep, att_send = swapped(att0, att1), swapped(att1, att0)
    ffn_got, att_got = core_flip(ffn_send), core_flip(att_send)
    grad_up, grad_out, grad_down, grad_local, grad_glob = assemble(
        ids, ffn_keep, ffn_got, att_keep, att_got, (share_w, share_f, ff, width)
    )

    at = q * dp + z
    piece = partial(lax.dynamic_slice_in_dim, axis=0)
    outs = (
        grad_local,
        jnp.stack([small[10], small[11]]),
        grad_glob,
        jnp.stack([small[12], small[13]]),
        grad_out,
        piece(small[4], at * share_w, share_w),
        jnp.stack([small[2], small[0]]),
        jnp.stack([small[3], small[1]]),
        grad_up,
        piece(small[6:10].reshape(ff), at * (ff // (4 * dp)), ff // (4 * dp)),
        grad_down,
        piece(small[5], at * share_w, share_w),
    )
    layer_outputs = by_micro(first, out0, out1, y)
    in_grads = by_micro(first, (near0, far0), (near1, far1), y)
    return (layer_outputs[None, :, None], in_grads[None, :, None]) + tuple(o[None] for o in outs)


def fits_two_chips(mesh, layer_in):
    sizes = dict(mesh.shape)
    micro, _, length, width = layer_in.shape
    dp = sizes[DP]
    return (
        sizes[SECTION] == 2
        and sizes[SEQ] == 4
        and micro == 2
        and dp == 4
        and length == 4 * HALF
        and width == 12 * HEAD
    )


def solution(mesh):
    in_specs = (
        P(None, DP, SEQ, None),
        P(None, DP, SEQ, None),
        P(None, DP, SEQ),
        P(None, DP, None),
        P(SECTION, None, None),
        P(SECTION, None, None),
        P(SECTION, None, None),
        P(SECTION, None, None),
        P(SECTION, None, None),
        P(SECTION, None),
        P(SECTION, None, None),
        P(SECTION, None, None),
        P(SECTION, None, None),
        P(SECTION, None),
        P(SECTION, None, None),
        P(SECTION, None),
    )
    out_specs = (
        P(SECTION, None, DP, SEQ, None),
        P(SECTION, None, DP, SEQ, None),
        P(SECTION, (SEQ, DP), None),
        P(SECTION, None, None),
        P(SECTION, (SEQ, DP), None),
        P(SECTION, None, None),
        P(SECTION, (SEQ, DP), None),
        P(SECTION, (SEQ, DP)),
        P(SECTION, None, None),
        P(SECTION, None, None),
        P(SECTION, (SEQ, DP), None),
        P(SECTION, (SEQ, DP)),
        P(SECTION, (SEQ, DP), None),
        P(SECTION, (SEQ, DP)),
    )

    def run(layer_in, *rest):
        body = two_chips if fits_two_chips(mesh, layer_in) else on_device
        return jax.shard_map(
            body, mesh=mesh, in_specs=in_specs, out_specs=out_specs, check_vma=False
        )(layer_in, *rest)

    return run
```
